32 devices in a mesh: seq: 4 (over y, x), ctx: 4 (over z), wt: 2 (over core).
Axes of the slice: x: 2, y: 2, z: 4, core: 2. Of those that a mesh axis runs over, the one named last changes fastest.
Arguments:
- layer_input: bfloat16 [4, 1024, 1536], P('seq', 'ctx'), may hold values from -6 to 6
- pairs: int32 [4, 4], P('seq'), may hold values from 0 to 3, each once within a row
- gain_attn: bfloat16 [1536], replicated, may hold values from 0.5 to 1.5
- w_q: bfloat16 [1536, 1536], P(('seq', 'ctx'), 'wt'), may hold values from -0.15625 to 0.15625
- b_q: bfloat16 [1536], P('wt'), may hold values from -3 to 3
- w_k: bfloat16 [1536, 256], P(('seq', 'ctx'), 'wt'), may hold values from -0.15625 to 0.15625
- b_k: bfloat16 [256], P('wt'), may hold values from -3 to 3
- w_v: bfloat16 [1536, 256], P(('seq', 'ctx'), 'wt'), may hold values from -0.15625 to 0.15625
- b_v: bfloat16 [256], P('wt'), may hold values from -3 to 3
- w_o: bfloat16 [1536, 1536], P(('seq', 'ctx'), 'wt'), may hold values from -0.875 to 0.875
- gain_mlp: bfloat16 [1536], replicated, may hold values from 0.5 to 1.5
- w_gate: bfloat16 [1536, 8960], P(('seq', 'ctx'), 'wt'), may hold values from -0.15625 to 0.15625
- w_up: bfloat16 [1536, 8960], P(('seq', 'ctx'), 'wt'), may hold values from -0.15625 to 0.15625
- w_down: bfloat16 [1536, 8960], P(('seq', 'ctx'), 'wt'), may hold values from -0.0625 to 0.0625
- out_grad: bfloat16 [4, 1024, 1536], P('seq', 'ctx'), may hold values from -6 to 6
Outputs:
- layer_output: bfloat16 [4, 1024, 1536], P('seq', 'ctx')
- grad_input: bfloat16 [4, 1024, 1536], P('seq', 'ctx')
- grad_gain_attn: float32 [1536], replicated
- grad_w_q: float32 [1536, 1536], P(('seq', 'ctx'), 'wt')
- grad_b_q: float32 [1536], P('wt')
- grad_w_k: float32 [1536, 256], P(('seq', 'ctx'), 'wt')
- grad_b_k: float32 [256], P('wt')
- grad_w_v: float32 [1536, 256], P(('seq', 'ctx'), 'wt')
- grad_b_v: float32 [256], P('wt')
- grad_w_o: float32 [1536, 1536], P(('seq', 'ctx'), 'wt')
- grad_gain_mlp: float32 [1536], replicated
- grad_w_gate: float32 [1536, 8960], P(('seq', 'ctx'), 'wt')
- grad_w_up: float32 [1536, 8960], P(('seq', 'ctx'), 'wt')
- grad_w_down: float32 [1536, 8960], P(('seq', 'ctx'), 'wt')
The draws below stay inside these ranges and needn't reach their ends.
Inputs may be any that keep to these rules, and one draw needn't show every extreme that they name: Each row of pairs holds every number below 4 once.
All inputs are finite; a program needn't handle non-finite values.
Results may differ from the reference program's by a relative error of at most 0.017.
Values may be sent and summed in bfloat16 or wider, within the bound.
No kernel may reach another device: no remote copies, remote signals or barrier semaphores. Data moves between devices by JAX's collectives and lax.ppermute only.
A program may use at most 192 MiB of HBM per device.

```python
import jax
import jax.numpy as jnp
from jax import lax

D = 1536
H = 12
KVH = 2
HD = 128
FF = 8960
CH = 128
LEN = 1024
SEQS = 4
N_CTX = 4


def steps_of(own_key, shape, pieces, smallest, high):
    factor_of, own = 1.0, jax.random.fold_in(own_key, 6)
    for position, blocks in pieces:
        heights = jnp.exp(jax.random.uniform(jax.random.fold_in(own, position), (blocks,), jnp.float32, smallest / len(pieces), high / len(pieces)))
        factor_of = factor_of * jnp.repeat(heights, shape[position] // blocks).reshape([-1 if axis == position else 1 for axis in range(len(shape))])
    return factor_of


def centred(rng, shape, scale, most, cuts=(), held_as=jnp.bfloat16):
    factor_of = steps_of(rng, shape, cuts, -0.22, 0.18) if cuts else 1.0
    result = jax.random.normal(rng, shape, jnp.float32) * scale * factor_of
    return jnp.minimum(jnp.maximum(result, -most), most).astype(held_as)


def setup_inputs(seed: int = 0) -> dict:
    key_of = jax.random.split(jax.random.key(seed), 16)
    layer_input = centred(key_of[0], (SEQS, LEN, D), 1.0, 6.0, ((0, 4), (1, 4)))
    pairs = jax.vmap(lambda own: jax.random.permutation(own, N_CTX))(jax.random.split(key_of[1], SEQS)).reshape((SEQS, N_CTX)).astype(jnp.int32)
    gain_attn = jnp.clip(1.0 + 0.1 * jax.random.normal(key_of[2], (D,), jnp.float32), 0.5, 1.5).astype(jnp.bfloat16)
    w_q = centred(key_of[3], (D, H * HD), D ** -0.5, 0.15625, ((0, 16), (1, 2)))
    b_q = centred(key_of[4], (H * HD,), 0.5, 3.0, ((0, 2),))
    w_k = centred(key_of[5], (D, KVH * HD), D ** -0.5, 0.15625, ((0, 16), (1, 2)))
    b_k = centred(key_of[6], (KVH * HD,), 0.5, 3.0, ((0, 2),))
    w_v = centred(key_of[7], (D, KVH * HD), D ** -0.5, 0.15625, ((0, 16), (1, 2)))
    b_v = centred(key_of[8], (KVH * HD,), 0.5, 3.0, ((0, 2),))
    w_o = centred(key_of[9], (D, H * HD), (H * HD // 32) ** -0.5, 0.875, ((0, 16), (1, 2)))
    gain_mlp = jnp.clip(1.0 + 0.1 * jax.random.normal(key_of[10], (D,), jnp.float32), 0.5, 1.5).astype(jnp.bfloat16)
    w_gate = centred(key_of[11], (D, FF), D ** -0.5, 0.15625, ((0, 16), (1, 2)))
    w_up = centred(key_of[12], (D, FF), D ** -0.5, 0.15625, ((0, 16), (1, 2)))
    w_down = centred(key_of[13], (D, FF), FF ** -0.5, 0.0625, ((0, 16), (1, 2)))
    out_grad = centred(key_of[14], (SEQS, LEN, D), 1.0, 6.0, ((0, 4), (1, 4)))
    return {"layer_input": layer_input, "pairs": pairs, "gain_attn": gain_attn, "w_q": w_q, "b_q": b_q, "w_k": w_k, "b_k": b_k, "w_v": w_v, "b_v": b_v, "w_o": w_o, "gain_mlp": gain_mlp, "w_gate": w_gate, "w_up": w_up, "w_down": w_down, "out_grad": out_grad}


EPSILON = 1e-06
THETA_BASE = 1000000.0
NEGATIVE = -1e+30

@jax.custom_vjp
def low(v):
    return lax.optimization_barrier(v.astype(jnp.bfloat16)).astype(jnp.float32)

@jax.custom_vjp
def low_back(v):
    return v

def low_keep(v):
    return (low(v), None)

def low_pass(kept, grad):
    return (grad,)

def back_keep(v):
    return (v, None)

def back_low(kept, grad):
    return (low(grad),)
low.defvjp(low_keep, low_pass)
low_back.defvjp(back_keep, back_low)

def matmul(left, right):
    return jnp.dot(left, right, precision=lax.Precision.HIGHEST, preferred_element_type=jnp.float32)

def rotate(values):
    middle = values.shape[-1] // 2
    return jnp.concatenate([-values[..., middle:], values[..., :middle]], -1)

def positions_of(pair_row):
    index = jnp.arange(LEN, dtype=jnp.int32)
    device = index // (2 * CH)
    within = index % (2 * CH)
    chosen = pair_row[device]
    return jnp.where(within < CH, chosen * CH + within, (2 * N_CTX - 1 - chosen) * CH + within - CH)

def rope_tables(positions):
    freqs = THETA_BASE ** (-(jnp.arange(HD // 2, dtype=jnp.float32) * 2.0) / HD)
    angles = positions.astype(jnp.float32)[:, None] * freqs[None, :]
    cosines = jnp.cos(angles)
    sines = jnp.sin(angles)
    return (jnp.concatenate([cosines, cosines], -1), jnp.concatenate([sines, sines], -1))

def apply_rope(values, cosines, sines):
    return values * cosines[:, None, :] + rotate(values) * sines[:, None, :]

def head_attend(query, keys, values, visible):
    scores = low_back(matmul(query, keys.T) * HD ** (-0.5))
    scores = jnp.where(visible, scores, NEGATIVE)
    highest = lax.optimization_barrier(jnp.max(scores, -1, keepdims=True))
    weights = jnp.exp(scores - highest)
    weights = weights / lax.optimization_barrier(jnp.sum(weights, -1, keepdims=True))
    return matmul(low(weights), values)

def layer(hidden_in, gain_attn, w_q, b_q, w_k, b_k, w_v, b_v, w_o, gain_mlp, w_gate, w_up, w_down, cosines, sines, visible):
    rms_attn = lax.rsqrt(lax.optimization_barrier(jnp.mean(hidden_in * hidden_in, -1, keepdims=True)) + EPSILON)
    normed_attn = low(hidden_in * rms_attn * gain_attn)
    query_lin = low_back(matmul(normed_attn, w_q) + b_q).reshape(LEN, H, HD)
    key_lin = low_back(matmul(normed_attn, w_k) + b_k).reshape(LEN, KVH, HD)
    value = low(low_back(matmul(normed_attn, w_v) + b_v)).reshape(LEN, KVH, HD)
    query = low(apply_rope(query_lin, cosines, sines))
    key = low(apply_rope(key_lin, cosines, sines))
    group = H // KVH
    key_heads = jnp.repeat(key, group, axis=1).transpose(1, 0, 2)
    value_heads = jnp.repeat(value, group, axis=1).transpose(1, 0, 2)

    def one_head(inputs):
        return head_attend(inputs[0], inputs[1], inputs[2], visible)
    heads = lax.map(jax.checkpoint(one_head), (query.transpose(1, 0, 2), key_heads, value_heads))
    attn_heads = low(low_back(heads.transpose(1, 0, 2).reshape(LEN, H * HD)))
    hidden = hidden_in + low_back(matmul(attn_heads, w_o.T))
    rms_mlp = lax.rsqrt(lax.optimization_barrier(jnp.mean(hidden * hidden, -1, keepdims=True)) + EPSILON)
    normed_mlp = low(hidden * rms_mlp * gain_mlp)
    gate = low_back(matmul(normed_mlp, w_gate))
    up = low_back(matmul(normed_mlp, w_up))
    act = low(gate / (1.0 + jnp.exp(-gate)) * up)
    return hidden + low_back(matmul(act, w_down.T))

def reference(layer_input, pairs, gain_attn, w_q, b_q, w_k, b_k, w_v, b_v, w_o, gain_mlp, w_gate, w_up, w_down, out_grad):
    params = tuple((weight.astype(jnp.float32) for weight in (gain_attn, w_q, b_q, w_k, b_k, w_v, b_v, w_o, gain_mlp, w_gate, w_up, w_down)))

    def one_sequence(totals, inputs):
        tokens_in, cotangent, pair_row = inputs
        positions = positions_of(pair_row)
        cosines, sines = rope_tables(positions)
        visible = positions[None, :] <= positions[:, None]

        def forward(hidden_in, *weights):
            return layer(hidden_in, *weights, cosines, sines, visible)
        output, pullback = jax.vjp(forward, tokens_in.astype(jnp.float32), *params)
        grads = pullback(cotangent.astype(jnp.float32))
        summed = tuple((running + fresh for running, fresh in zip(totals, grads[1:])))
        return (summed, (output.astype(jnp.bfloat16), grads[0].astype(jnp.bfloat16)))
    start_sums = tuple((jnp.zeros_like(weight) for weight in params))
    sums, (outputs, input_grads) = lax.scan(one_sequence, start_sums, (layer_input, out_grad, pairs))
    return (outputs, input_grads, sums[0], sums[1], sums[2], sums[3], sums[4], sums[5], sums[6], sums[7], sums[8], sums[9], sums[10], sums[11])
```

```python
import jax
import jax.numpy as jnp
from jax import lax
from jax.sharding import PartitionSpec as P

HD = 128
LANES = 128


EPSILON = 1e-06
THETA_BASE = 1000000.0
NEGATIVE = -1e30


def rotate(values):
    middle = values.shape[-1] // 2
    return jnp.concatenate([-values[..., middle:], values[..., :middle]], -1)


def rope_tables(positions):
    freqs = THETA_BASE ** (-(jnp.arange(HD // 2, dtype=jnp.float32) * 2.0) / HD)
    angles = positions.astype(jnp.float32)[:, None] * freqs[None, :]
    cosines = jnp.cos(angles)
    sines = jnp.sin(angles)
    return (jnp.concatenate([cosines, cosines], -1), jnp.concatenate([sines, sines], -1))


def matmul(left, right):
    return jnp.dot(left, right, preferred_element_type=jnp.float32)


def times_transposed(left, right):
    return lax.dot_general(
        left, right, (((1,), (1,)), ((), ())), preferred_element_type=jnp.float32
    )


def inner_rows(left, right):
    return lax.dot_general(
        left, right, (((0,), (0,)), ((), ())), preferred_element_type=jnp.float32
    )


def swap(values, axis, offset):
    size = lax.axis_size(axis)
    return lax.ppermute(values, axis, [(i, i ^ offset) for i in range(size)])


def rows_at(values, index, count):
    return lax.dynamic_slice_in_dim(values, index * count, count, 0)


def place_rows(parts, indices, rows):
    whole = jnp.zeros((rows,) + parts[0].shape[1:], parts[0].dtype)
    for part, index in zip(parts, indices):
        whole = lax.dynamic_update_slice_in_dim(whole, part, index * part.shape[0], 0)
    return whole


def gather_ctx(block):
    size = lax.axis_size("ctx")
    return [block] + [swap(block, "ctx", k) for k in range(1, size)]


def exchange_ctx(pieces):
    return [pieces[0]] + [swap(pieces[k], "ctx", k) for k in range(1, len(pieces))]


def gather_seq(shard):
    size = lax.axis_size("seq")
    if size != 4:
        return lax.all_gather(shard, "seq", axis=0, tiled=True)
    me = lax.axis_index("seq")
    half = shard.shape[0] // 2
    from_x = swap(shard, "seq", 1)
    from_y = swap(shard, "seq", 2)
    far_top = swap(from_y[:half], "seq", 1)
    far_bottom = swap(from_x[half:], "seq", 2)
    far = jnp.concatenate([far_top, far_bottom], 0)
    return place_rows(
        [shard, from_x, from_y, far], [me, me ^ 1, me ^ 2, me ^ 3], size * shard.shape[0]
    )


def scatter_seq(partial_sum):
    size = lax.axis_size("seq")
    if size != 4:
        return lax.psum_scatter(
            partial_sum.astype(jnp.float32), "seq", scatter_dimension=0, tiled=True
        )
    me = lax.axis_index("seq")
    rows = partial_sum.shape[0] // size
    half = rows // 2
    own = rows_at(partial_sum, me, rows)
    for_x = rows_at(partial_sum, me ^ 1, rows)
    for_y = rows_at(partial_sum, me ^ 2, rows)
    for_far = rows_at(partial_sum, me ^ 3, rows)
    got_x = swap(jnp.concatenate([for_far[half:], for_x[half:]], 0), "seq", 1)
    got_y = swap(jnp.concatenate([for_far[:half], for_y[:half]], 0), "seq", 2)
    on_x = (for_x[:half].astype(jnp.float32) + got_y[:half].astype(jnp.float32)).astype(
        jnp.bfloat16
    )
    on_y = (for_y[half:].astype(jnp.float32) + got_x[:half].astype(jnp.float32)).astype(
        jnp.bfloat16
    )
    last_x = swap(on_x, "seq", 1)
    last_y = swap(on_y, "seq", 2)
    top = (
        own[:half].astype(jnp.float32)
        + got_y[half:].astype(jnp.float32)
        + last_x.astype(jnp.float32)
    )
    bottom = (
        own[half:].astype(jnp.float32)
        + got_x[half:].astype(jnp.float32)
        + last_y.astype(jnp.float32)
    )
    return jnp.concatenate([top, bottom], 0)


def add_up(parts):
    total = parts[0].astype(jnp.float32)
    for part in parts[1:]:
        total = total + part.astype(jnp.float32)
    return total


def gather_weight(shard):
    ctx = lax.axis_index("ctx")
    parts = gather_ctx(shard)
    rows = len(parts) * shard.shape[0]
    own = place_rows(parts, [ctx ^ k for k in range(len(parts))], rows)
    return gather_seq(own)


def units_per(units):
    size = lax.axis_size("ctx")
    return -(-units // (size * LANES)) * LANES


def spread_units(shard):
    size = lax.axis_size("ctx")
    ctx = lax.axis_index("ctx")
    width = units_per(shard.shape[1])
    padded = jnp.pad(shard, ((0, 0), (0, size * width - shard.shape[1])))
    pieces = [lax.dynamic_slice_in_dim(padded, (ctx ^ k) * width, width, 1) for k in range(size)]
    parts = exchange_ctx(pieces)
    own = place_rows(parts, [ctx ^ k for k in range(size)], size * shard.shape[0])
    return gather_seq(own)


def collect_units(partial_sum, units):
    size = lax.axis_size("ctx")
    ctx = lax.axis_index("ctx")
    summed = scatter_seq(partial_sum.astype(jnp.bfloat16)).astype(jnp.bfloat16)
    rows, width = summed.shape[0] // size, summed.shape[1]
    parts = exchange_ctx([rows_at(summed, ctx ^ k, rows) for k in range(size)])
    whole = jnp.zeros((rows, size * width), jnp.float32)
    for k in range(size):
        whole = lax.dynamic_update_slice_in_dim(
            whole, parts[k].astype(jnp.float32), (ctx ^ k) * width, 1
        )
    return whole[:, :units]


def scatter_weight(partial_sum):
    size = lax.axis_size("ctx")
    ctx = lax.axis_index("ctx")
    summed = scatter_seq(partial_sum.astype(jnp.bfloat16))
    rows = summed.shape[0] // size
    pieces = [rows_at(summed, ctx ^ k, rows) for k in range(size)]
    return add_up(exchange_ctx([pieces[0]] + [piece.astype(jnp.bfloat16) for piece in pieces[1:]]))


def gather_tokens(half):
    mine = jnp.concatenate(gather_ctx(half), 0)
    return jnp.concatenate([mine, swap(mine, "wt", 1)], 0)


def scatter_tokens(partial_sum):
    size = lax.axis_size("ctx")
    middle = partial_sum.shape[0] // 2
    other = swap(partial_sum[middle:].astype(jnp.bfloat16), "wt", 1)
    chip = partial_sum[:middle] + other.astype(jnp.float32)
    pieces = jnp.split(chip, size, 0)
    return add_up(exchange_ctx([pieces[0]] + [piece.astype(jnp.bfloat16) for piece in pieces[1:]]))


def add_all(values, axes):
    for axis in axes:
        offset = 1
        while offset < lax.axis_size(axis):
            values = values + swap(values, axis, offset)
            offset *= 2
    return values


def norm_back(grad_normed, inputs, inverse_rms, gain):
    weighted = grad_normed * gain
    back = inverse_rms * weighted - inputs * inverse_rms**3 * jnp.mean(
        weighted * inputs, -1, keepdims=True
    )
    gain_grad = jnp.sum(grad_normed * inputs * inverse_rms, 0)
    return (back, gain_grad)


def on_device(
    layer_input,
    pairs,
    gain_attn,
    w_q,
    b_q,
    w_k,
    b_k,
    w_v,
    b_v,
    w_o,
    gain_mlp,
    w_gate,
    w_up,
    w_down,
    out_grad,
):
    _, span_rows, model_width = layer_input.shape
    half_rows = span_rows // 2
    query_cols = w_q.shape[1]
    key_cols = w_k.shape[1]
    heads_here = query_cols // HD
    units_here = w_gate.shape[1]
    ctx_size = lax.axis_size("ctx")
    ctx = lax.axis_index("ctx")
    core = lax.axis_index("wt")
    scale = HD ** (-0.5)

    def own_half(values):
        return rows_at(values, core, half_rows)

    def join_halves(mine):
        other = swap(mine, "wt", 1)
        return jnp.where(
            core == 0, jnp.concatenate([mine, other], 0), jnp.concatenate([other, mine], 0)
        )

    def sum_half(partial_sum):
        return own_half(partial_sum) + swap(rows_at(partial_sum, 1 - core, half_rows), "wt", 1)

    within = jnp.arange(half_rows, dtype=jnp.int32)

    def positions_at(index):
        early = lax.dynamic_index_in_dim(pairs[0], index, 0, False)
        return jnp.concatenate(
            [early * half_rows + within, (2 * ctx_size - 1 - early) * half_rows + within]
        )

    query_positions = positions_at(ctx)
    key_positions = jnp.concatenate([positions_at(ctx ^ k) for k in range(ctx_size)])
    visible = key_positions[None, :] <= query_positions[:, None]
    cosines, sines = rope_tables(query_positions)

    def rope_rows(values):
        return values * cosines[:, None, :] + rotate(values) * sines[:, None, :]

    def unrope_rows(grads):
        return grads * cosines[:, None, :] - rotate(grads * sines[:, None, :])

    input_rows = layer_input.reshape(span_rows, model_width).astype(jnp.float32)
    grad_out = out_grad.reshape(span_rows, model_width)
    gain_one = gain_attn.astype(jnp.float32)
    gain_two = gain_mlp.astype(jnp.float32)

    w_qkv = gather_weight(jnp.concatenate([w_q, w_k, w_v], 1))
    w_out = gather_weight(w_o)
    gate_here = spread_units(w_gate)
    up_here = spread_units(w_up)
    down_here = spread_units(w_down)
    grad_half = own_half(grad_out)
    grad_seq = gather_tokens(grad_half)

    rms_attn = lax.rsqrt(jnp.mean(input_rows * input_rows, -1, keepdims=True) + EPSILON)
    normed_attn = (input_rows * rms_attn * gain_one).astype(jnp.bfloat16)
    bias = jnp.concatenate([b_q, b_k, b_v]).astype(jnp.float32)
    qkv = matmul(normed_attn, w_qkv) + bias
    query = rope_rows(qkv[:, :query_cols].reshape(span_rows, heads_here, HD)).astype(jnp.bfloat16)
    key = rope_rows(qkv[:, query_cols : query_cols + key_cols].reshape(span_rows, 1, HD))
    key_value = jnp.concatenate(
        [key.reshape(span_rows, HD), qkv[:, query_cols + key_cols :]], 1
    ).astype(jnp.bfloat16)
    keys_values = jnp.concatenate(gather_ctx(key_value), 0)
    keys, values = keys_values[:, :HD], keys_values[:, HD:]

    def masked_scores(query_block):
        return jnp.where(visible, times_transposed(query_block, keys) * scale, NEGATIVE)

    heads_out, log_sums = [], []
    for head in range(heads_here):
        scores = masked_scores(query[:, head])
        highest = jnp.max(scores, -1, keepdims=True)
        weights = jnp.exp(scores - highest)
        totals = jnp.sum(weights, -1, keepdims=True)
        heads_out.append(matmul((weights / totals).astype(jnp.bfloat16), values))
        log_sums.append(highest + jnp.log(totals))
    attn_heads = jnp.concatenate(heads_out, 1).astype(jnp.bfloat16)

    input_half = own_half(input_rows)
    hidden = input_half + sum_half(times_transposed(attn_heads, w_out))
    rms_mlp = lax.rsqrt(jnp.mean(hidden * hidden, -1, keepdims=True) + EPSILON)
    normed_half = (hidden * rms_mlp * gain_two).astype(jnp.bfloat16)
    normed_seq = gather_tokens(normed_half)

    gate = matmul(normed_seq, gate_here)
    up = matmul(normed_seq, up_here)
    g_act = matmul(grad_seq, down_here)
    sigmoid_gate = jax.nn.sigmoid(gate)
    silu_gate = gate * sigmoid_gate
    act = (silu_gate * up).astype(jnp.bfloat16)
    g_gate = (g_act * up * sigmoid_gate * (1.0 + gate * (1.0 - sigmoid_gate))).astype(jnp.bfloat16)
    g_up = (g_act * silu_gate).astype(jnp.bfloat16)

    g_normed_mlp = scatter_tokens(
        times_transposed(g_gate, gate_here) + times_transposed(g_up, up_here)
    )
    mlp_out = scatter_tokens(times_transposed(act, down_here))
    layer_output = join_halves((hidden + mlp_out).astype(jnp.bfloat16))
    grad_w_gate = collect_units(inner_rows(normed_seq, g_gate), units_here)
    grad_w_up = collect_units(inner_rows(normed_seq, g_up), units_here)
    grad_w_down = collect_units(inner_rows(grad_seq, act), units_here)

    back_mlp, grad_gain_mlp = norm_back(g_normed_mlp, hidden, rms_mlp, gain_two)
    g_hidden = grad_half.astype(jnp.float32) + back_mlp
    g_branch = join_halves(g_hidden.astype(jnp.bfloat16))
    g_heads = matmul(g_branch, w_out).astype(jnp.bfloat16)

    g_query_parts = []
    g_keys = jnp.zeros(keys.shape, jnp.float32)
    g_values = jnp.zeros(values.shape, jnp.float32)
    for head in range(heads_here):
        grad_block = g_heads[:, head * HD : (head + 1) * HD]
        probs = jnp.exp(masked_scores(query[:, head]) - log_sums[head])
        g_probs = times_transposed(grad_block, values)
        delta = jnp.sum(probs * g_probs, -1, keepdims=True)
        g_scores = (probs * (g_probs - delta)).astype(jnp.bfloat16)
        g_query_parts.append(matmul(g_scores, keys) * scale)
        g_keys = g_keys + inner_rows(g_scores, query[:, head]) * scale
        g_values = g_values + inner_rows(probs.astype(jnp.bfloat16), grad_block)
    g_query = jnp.stack(g_query_parts, 1)
    g_blocks = jnp.split(jnp.concatenate([g_keys, g_values], 1), ctx_size, 0)
    g_key_value = add_up(
        exchange_ctx([g_blocks[0]] + [block.astype(jnp.bfloat16) for block in g_blocks[1:]])
    )
    g_query_lin = unrope_rows(g_query).reshape(span_rows, query_cols)
    g_key_lin = unrope_rows(g_key_value[:, :HD].reshape(span_rows, 1, HD)).reshape(span_rows, HD)
    projected = jnp.concatenate([g_query_lin, g_key_lin, g_key_value[:, HD:]], 1).astype(
        jnp.bfloat16
    )

    g_normed_attn = sum_half(times_transposed(projected, w_qkv))
    back_attn, grad_gain_attn = norm_back(
        g_normed_attn, input_half, own_half(rms_attn), gain_one
    )
    grad_input = join_halves((g_hidden + back_attn).astype(jnp.bfloat16))

    grad_w_o = scatter_weight(inner_rows(g_branch, attn_heads))
    grad_w_qkv = scatter_weight(inner_rows(normed_attn, projected))

    gains = jnp.concatenate([grad_gain_attn, grad_gain_mlp])
    small = jnp.concatenate([gains, jnp.sum(projected.astype(jnp.float32), 0)])
    small = add_all(small.reshape(-1, LANES), ("seq", "ctx")).reshape(-1)
    gains = add_all(small[: 2 * model_width].reshape(-1, LANES), ("wt",)).reshape(-1)
    grad_bias = small[2 * model_width :]
    return (
        layer_output[None],
        grad_input[None],
        gains[:model_width],
        grad_w_qkv[:, :query_cols],
        grad_bias[:query_cols],
        grad_w_qkv[:, query_cols : query_cols + key_cols],
        grad_bias[query_cols : query_cols + key_cols],
        grad_w_qkv[:, query_cols + key_cols :],
        grad_bias[query_cols + key_cols :],
        grad_w_o,
        gains[model_width:],
        grad_w_gate,
        grad_w_up,
        grad_w_down,
    )


def solution(mesh):
    tokens = P("seq", "ctx", None)
    weight = P(("seq", "ctx"), "wt")
    return jax.shard_map(
        on_device,
        mesh=mesh,
        in_specs=(
            tokens,
            P("seq", None),
            P(),
            weight,
            P("wt"),
            weight,
            P("wt"),
            weight,
            P("wt"),
            weight,
            P(),
            weight,
            weight,
            weight,
            tokens,
        ),
        out_specs=(
            tokens,
            tokens,
            P(),
            weight,
            P("wt"),
            weight,
            P("wt"),
            weight,
            P("wt"),
            weight,
            P(),
            weight,
            weight,
            weight,
        ),
        check_vma=False,
    )
```

```python
import jax
import jax.numpy as jnp
from jax import lax
from jax.sharding import PartitionSpec as P

HD = 128
LANES = 128


EPSILON = 1e-06
THETA_BASE = 1000000.0
NEGATIVE = -1e30


def rotate(values):
    middle = values.shape[-1] // 2
    return jnp.concatenate([-values[..., middle:], values[..., :middle]], -1)


def rope_tables(positions):
    freqs = THETA_BASE ** (-(jnp.arange(HD // 2, dtype=jnp.float32) * 2.0) / HD)
    angles = positions.astype(jnp.float32)[:, None] * freqs[None, :]
    cosines = jnp.cos(angles)
    sines = jnp.sin(angles)
    return (jnp.concatenate([cosines, cosines], -1), jnp.concatenate([sines, sines], -1))


def matmul(left, right):
    return jnp.dot(left, right, preferred_element_type=jnp.float32)


def times_transposed(left, right):
    return lax.dot_general(
        left, right, (((1,), (1,)), ((), ())), preferred_element_type=jnp.float32
    )


def inner_rows(left, right):
    return lax.dot_general(
        left, right, (((0,), (0,)), ((), ())), preferred_element_type=jnp.float32
    )


def swap(values, axis, offset):
    size = lax.axis_size(axis)
    return lax.ppermute(values, axis, [(i, i ^ offset) for i in range(size)])


def rows_at(values, index, count):
    return lax.dynamic_slice_in_dim(values, index * count, count, 0)


def place_rows(parts, indices):
    rows = len(parts) * parts[0].shape[0]
    whole = jnp.zeros((rows,) + parts[0].shape[1:], parts[0].dtype)
    for part, index in zip(parts, indices):
        whole = lax.dynamic_update_slice_in_dim(whole, part, index * part.shape[0], 0)
    return whole


def after(values, *others):
    return lax.optimization_barrier((values, others))[0]


def relative(values):
    me = lax.axis_index("seq")
    width = values.shape[-1] // 4
    blocks = [
        lax.dynamic_slice_in_dim(values, (me ^ j) * width, width, values.ndim - 1)
        for j in range(4)
    ]
    return jnp.concatenate(blocks, -1)


def gather_ctx(block):
    size = lax.axis_size("ctx")
    return [block] + [swap(block, "ctx", k) for k in range(1, size)]


def exchange_ctx(pieces):
    return [pieces[0]] + [swap(pieces[k], "ctx", k) for k in range(1, len(pieces))]


def near_seq(shard):
    return swap(shard, "seq", 1), swap(shard, "seq", 2)


def far_seq(from_x, from_y):
    half = from_x.shape[0] // 2
    return swap(from_y[:half], "seq", 1), swap(from_x[half:], "seq", 2)


def lay_seq(shard, near, far):
    return jnp.concatenate([shard, *near, *far], 0)


def scatter_near(partial_sum):
    own, for_x, for_y, for_far = jnp.split(partial_sum, 4, 0)
    half = own.shape[0] // 2
    got_x = swap(jnp.concatenate([for_far[half:], for_x[half:]], 0), "seq", 1)
    got_y = swap(jnp.concatenate([for_far[:half], for_y[:half]], 0), "seq", 2)
    return got_x, got_y


def scatter_far(partial_sum, got_x, got_y):
    own, for_x, for_y, _ = jnp.split(partial_sum, 4, 0)
    half = own.shape[0] // 2
    on_x = add_up([for_x[:half], got_y[:half]]).astype(jnp.bfloat16)
    on_y = add_up([for_y[half:], got_x[:half]]).astype(jnp.bfloat16)
    on_x, on_y = lax.optimization_barrier((on_x, on_y))
    last_x = swap(on_x, "seq", 1)
    last_y = swap(on_y, "seq", 2)
    top = add_up([own[:half], got_y[half:], last_x])
    bottom = add_up([own[half:], got_x[half:], last_y])
    return jnp.concatenate([top, bottom], 0)


def add_up(parts):
    total = parts[0].astype(jnp.float32)
    for part in parts[1:]:
        total = total + part.astype(jnp.float32)
    return total


def units_per(units):
    size = lax.axis_size("ctx")
    return -(-units // (size * LANES)) * LANES


def unit_pieces(shards):
    size = lax.axis_size("ctx")
    ctx = lax.axis_index("ctx")
    width = units_per(shards[0].shape[1])
    padded = [jnp.pad(w, ((0, 0), (0, size * width - w.shape[1]))) for w in shards]
    return [
        jnp.concatenate(
            [lax.dynamic_slice_in_dim(w, (ctx ^ k) * width, width, 1) for w in padded], 1
        )
        for k in range(size)
    ]


def row_pieces(summed):
    size = lax.axis_size("ctx")
    ctx = lax.axis_index("ctx")
    rows = summed.shape[0] // size
    return [rows_at(summed, ctx ^ k, rows) for k in range(size)]


def place_ctx(parts):
    ctx = lax.axis_index("ctx")
    return place_rows(parts, [ctx ^ k for k in range(len(parts))])


def place_units(parts, units):
    size = lax.axis_size("ctx")
    ctx = lax.axis_index("ctx")
    width = units_per(units)
    wholes = []
    for start in range(0, parts[0].shape[1], width):
        whole = jnp.zeros((parts[0].shape[0], size * width), jnp.float32)
        for k in range(size):
            part = parts[k][:, start : start + width].astype(jnp.float32)
            whole = lax.dynamic_update_slice_in_dim(whole, part, (ctx ^ k) * width, 1)
        wholes.append(whole[:, :units])
    return wholes


def narrow_others(pieces):
    return [pieces[0]] + [piece.astype(jnp.bfloat16) for piece in pieces[1:]]


def both_cores(mine):
    return jnp.concatenate([mine, swap(mine, "wt", 1)], 0)


def chip_sum(partial_sum):
    middle = partial_sum.shape[0] // 2
    other = swap(partial_sum[middle:].astype(jnp.bfloat16), "wt", 1)
    chip = partial_sum[:middle] + other.astype(jnp.float32)
    return jnp.split(chip, lax.axis_size("ctx"), 0)


def add_all(values, axes):
    for axis in axes:
        offset = 1
        while offset < lax.axis_size(axis):
            values = values + swap(values, axis, offset)
            offset *= 2
    return values


def norm_back(grad_normed, inputs, inverse_rms, gain):
    weighted = grad_normed * gain
    back = inverse_rms * weighted - inputs * inverse_rms**3 * jnp.mean(
        weighted * inputs, -1, keepdims=True
    )
    gain_grad = jnp.sum(grad_normed * inputs * inverse_rms, 0)
    return (back, gain_grad)


def on_device(
    layer_input,
    pairs,
    gain_attn,
    w_q,
    b_q,
    w_k,
    b_k,
    w_v,
    b_v,
    w_o,
    gain_mlp,
    w_gate,
    w_up,
    w_down,
    out_grad,
):
    _, span_rows, model_width = layer_input.shape
    half_rows = span_rows // 2
    query_cols = w_q.shape[1]
    key_cols = w_k.shape[1]
    heads_here = query_cols // HD
    units_here = w_gate.shape[1]
    ctx_size = lax.axis_size("ctx")
    ctx = lax.axis_index("ctx")
    core = lax.axis_index("wt")
    scale = HD ** (-0.5)

    def own_half(values):
        return rows_at(values, core, half_rows)

    def join_halves(mine):
        other = swap(mine, "wt", 1)
        return jnp.where(
            core == 0, jnp.concatenate([mine, other], 0), jnp.concatenate([other, mine], 0)
        )

    def sum_half(partial_sum):
        return own_half(partial_sum) + swap(rows_at(partial_sum, 1 - core, half_rows), "wt", 1)

    within = jnp.arange(half_rows, dtype=jnp.int32)

    def positions_at(index):
        early = lax.dynamic_index_in_dim(pairs[0], index, 0, False)
        return jnp.concatenate(
            [early * half_rows + within, (2 * ctx_size - 1 - early) * half_rows + within]
        )

    query_positions = positions_at(ctx)
    key_positions = jnp.concatenate([positions_at(ctx ^ k) for k in range(ctx_size)])
    visible = key_positions[None, :] <= query_positions[:, None]
    cosines, sines = rope_tables(query_positions)

    def rope_rows(values):
        return values * cosines[:, None, :] + rotate(values) * sines[:, None, :]

    def unrope_rows(grads):
        return grads * cosines[:, None, :] - rotate(grads * sines[:, None, :])

    input_rows = relative(layer_input.reshape(span_rows, model_width)).astype(jnp.float32)
    grad_out = relative(out_grad.reshape(span_rows, model_width))
    gain_one = relative(gain_attn.astype(jnp.float32))
    gain_two = relative(gain_mlp.astype(jnp.float32))

    attn_shard = place_ctx(gather_ctx(jnp.concatenate([w_q, w_k, w_v, w_o], 1)))
    gate_up_pieces = unit_pieces([w_gate, w_up])
    down_pieces = unit_pieces([w_down])
    grad_half = own_half(grad_out)

    attn_near = near_seq(attn_shard)
    gate_up_parts = exchange_ctx(after(gate_up_pieces, attn_shard))
    attn_near, gate_up_parts = lax.optimization_barrier((attn_near, gate_up_parts))
    attn_far = far_seq(*attn_near)
    down_parts = exchange_ctx(after(down_pieces, gate_up_parts))
    attn_far, down_parts = lax.optimization_barrier((attn_far, down_parts))
    w_attn = lay_seq(attn_shard, attn_near, attn_far)
    w_qkv, w_out = w_attn[:, : query_cols + 2 * key_cols], w_attn[:, query_cols + 2 * key_cols :]
    gate_up_shard = place_ctx(gate_up_parts)
    down_shard = place_ctx(down_parts)
    gate_up_near = near_seq(after(gate_up_shard, attn_far))

    rms_attn = lax.rsqrt(jnp.mean(input_rows * input_rows, -1, keepdims=True) + EPSILON)
    normed_attn = (input_rows * rms_attn * gain_one).astype(jnp.bfloat16)
    bias = jnp.concatenate([b_q, b_k, b_v]).astype(jnp.float32)
    qkv = matmul(normed_attn, w_qkv) + bias
    query = rope_rows(qkv[:, :query_cols].reshape(span_rows, heads_here, HD)).astype(jnp.bfloat16)
    key = rope_rows(qkv[:, query_cols : query_cols + key_cols].reshape(span_rows, 1, HD))
    key_value = jnp.concatenate(
        [key.reshape(span_rows, HD), qkv[:, query_cols + key_cols :]], 1
    ).astype(jnp.bfloat16)
    keys_values = jnp.concatenate(gather_ctx(key_value), 0)
    grad_mine = jnp.concatenate(gather_ctx(after(grad_half, keys_values)), 0)
    keys, values = keys_values[:, :HD], keys_values[:, HD:]

    def masked_scores(query_block):
        return jnp.where(visible, times_transposed(query_block, keys) * scale, NEGATIVE)

    heads_out, log_sums = [], []
    for head in range(heads_here):
        scores = masked_scores(query[:, head])
        highest = jnp.max(scores, -1, keepdims=True)
        weights = jnp.exp(scores - highest)
        totals = jnp.sum(weights, -1, keepdims=True)
        heads_out.append(matmul((weights / totals).astype(jnp.bfloat16), values))
        log_sums.append(highest + jnp.log(totals))
    attn_heads = jnp.concatenate(heads_out, 1).astype(jnp.bfloat16)

    input_half = own_half(input_rows)
    hidden = input_half + sum_half(times_transposed(attn_heads, w_out))
    rms_mlp = lax.rsqrt(jnp.mean(hidden * hidden, -1, keepdims=True) + EPSILON)
    normed_half = (hidden * rms_mlp * gain_two).astype(jnp.bfloat16)
    normed_half, gate_up_near = lax.optimization_barrier((normed_half, gate_up_near))
    normed_mine = jnp.concatenate(gather_ctx(normed_half), 0)
    gate_up_far = far_seq(*gate_up_near)
    down_near = near_seq(after(down_shard, gate_up_far))
    normed_mine, down_near, grad_mine = lax.optimization_barrier(
        (normed_mine, down_near, grad_mine)
    )
    down_far = far_seq(*down_near)
    normed_seq = both_cores(normed_mine)
    grad_seq = both_cores(grad_mine)
    gate_up_here = lay_seq(gate_up_shard, gate_up_near, gate_up_far)
    width = units_per(units_here)
    gate_here, up_here = gate_up_here[:, :width], gate_up_here[:, width:]

    gate = matmul(normed_seq, gate_here)
    up = matmul(normed_seq, up_here)
    down_here = lay_seq(down_shard, down_near, down_far)
    g_act = matmul(grad_seq, down_here)
    sigmoid_gate = jax.nn.sigmoid(gate)
    silu_gate = gate * sigmoid_gate
    act = (silu_gate * up).astype(jnp.bfloat16)
    g_gate = (g_act * up * sigmoid_gate * (1.0 + gate * (1.0 - sigmoid_gate))).astype(jnp.bfloat16)
    g_up = (g_act * silu_gate).astype(jnp.bfloat16)

    g_normed_partial = times_transposed(g_gate, gate_here) + times_transposed(g_up, up_here)
    act, g_gate, g_up, g_normed_partial = lax.optimization_barrier(
        (act, g_gate, g_up, g_normed_partial)
    )
    g_normed_pieces = chip_sum(g_normed_partial)
    g_down = inner_rows(grad_seq, act).astype(jnp.bfloat16)
    act, g_gate, g_up, g_normed_pieces, g_down = lax.optimization_barrier(
        (act, g_gate, g_up, g_normed_pieces, g_down)
    )

    g_normed_parts = exchange_ctx(narrow_others(g_normed_pieces))
    down_got = scatter_near(g_down)
    g_gate_up = inner_rows(normed_seq, jnp.concatenate([g_gate, g_up], 1)).astype(jnp.bfloat16)
    mlp_pieces = chip_sum(after(times_transposed(act, down_here), down_got))
    down_sum = scatter_far(g_down, *down_got).astype(jnp.bfloat16)
    g_normed_parts, mlp_pieces, down_sum, g_gate_up = lax.optimization_barrier(
        (g_normed_parts, mlp_pieces, down_sum, g_gate_up)
    )

    mlp_parts = exchange_ctx(narrow_others(mlp_pieces))
    gate_up_got = scatter_near(g_gate_up)
    g_normed_mlp = add_up(g_normed_parts)

    back_mlp, grad_gain_mlp = norm_back(g_normed_mlp, hidden, rms_mlp, gain_two)
    g_hidden = grad_half.astype(jnp.float32) + back_mlp
    g_branch = join_halves(g_hidden.astype(jnp.bfloat16))
    g_heads = matmul(g_branch, w_out).astype(jnp.bfloat16)

    g_query_parts = []
    g_keys = jnp.zeros(keys.shape, jnp.float32)
    g_values = jnp.zeros(values.shape, jnp.float32)
    for head in range(heads_here):
        grad_block = g_heads[:, head * HD : (head + 1) * HD]
        probs = jnp.exp(masked_scores(query[:, head]) - log_sums[head])
        g_probs = times_transposed(grad_block, values)
        delta = jnp.sum(probs * g_probs, -1, keepdims=True)
        g_scores = (probs * (g_probs - delta)).astype(jnp.bfloat16)
        g_query_parts.append(matmul(g_scores, keys) * scale)
        g_keys = g_keys + inner_rows(g_scores, query[:, head]) * scale
        g_values = g_values + inner_rows(probs.astype(jnp.bfloat16), grad_block)
    g_query = jnp.stack(g_query_parts, 1)
    g_blocks = jnp.split(jnp.concatenate([g_keys, g_values], 1), ctx_size, 0)
    g_out = inner_rows(g_branch, attn_heads).astype(jnp.bfloat16)
    g_blocks, mlp_parts, gate_up_got, g_out = lax.optimization_barrier(
        (g_blocks, mlp_parts, gate_up_got, g_out)
    )

    g_key_value_parts = exchange_ctx(narrow_others(g_blocks))
    gate_up_sum = scatter_far(g_gate_up, *gate_up_got).astype(jnp.bfloat16)
    layer_output = join_halves(relative((hidden + add_up(mlp_parts)).astype(jnp.bfloat16)))
    g_key_value_parts, gate_up_sum = lax.optimization_barrier((g_key_value_parts, gate_up_sum))
    g_key_value = add_up(g_key_value_parts)
    g_query_lin = unrope_rows(g_query).reshape(span_rows, query_cols)
    g_key_lin = unrope_rows(g_key_value[:, :HD].reshape(span_rows, 1, HD)).reshape(span_rows, HD)
    projected = jnp.concatenate([g_query_lin, g_key_lin, g_key_value[:, HD:]], 1).astype(
        jnp.bfloat16
    )
    g_qkv = inner_rows(normed_attn, projected).astype(jnp.bfloat16)
    down_back = exchange_ctx(row_pieces(after(down_sum, g_key_value_parts)))
    out_got = scatter_near(after(g_out, gate_up_sum))
    down_back, out_got, g_qkv = lax.optimization_barrier((down_back, out_got, g_qkv))

    gate_up_back = exchange_ctx(row_pieces(after(gate_up_sum, down_back)))
    qkv_got = scatter_near(g_qkv)
    g_normed_attn = sum_half(times_transposed(after(projected, g_qkv), w_qkv))
    back_attn, grad_gain_attn = norm_back(
        g_normed_attn, input_half, own_half(rms_attn), gain_one
    )
    grad_input = join_halves(relative((g_hidden + back_attn).astype(jnp.bfloat16)))
    out_sum = scatter_far(g_out, *after(out_got, qkv_got))
    qkv_sum = scatter_far(g_qkv, *qkv_got)
    attn_sum = jnp.concatenate([qkv_sum, out_sum], 1)
    attn_back = exchange_ctx(narrow_others(row_pieces(after(attn_sum, gate_up_back))))
    grad_w_gate, grad_w_up = place_units(gate_up_back, units_here)
    (grad_w_down,) = place_units(down_back, units_here)
    grad_w_attn = add_up(attn_back)
    grad_w_qkv = grad_w_attn[:, : query_cols + 2 * key_cols]
    grad_w_o = grad_w_attn[:, query_cols + 2 * key_cols :]

    gains = jnp.concatenate([relative(grad_gain_attn), relative(grad_gain_mlp)])
    small = jnp.concatenate([gains, jnp.sum(projected.astype(jnp.float32), 0)])
    small = add_all(after(small, attn_sum).reshape(-1, LANES), ("seq", "ctx")).reshape(-1)
    gains = add_all(small[: 2 * model_width].reshape(-1, LANES), ("wt",)).reshape(-1)
    grad_bias = small[2 * model_width :]
    return (
        layer_output[None],
        grad_input[None],
        gains[:model_width],
        grad_w_qkv[:, :query_cols],
        grad_bias[:query_cols],
        grad_w_qkv[:, query_cols : query_cols + key_cols],
        grad_bias[query_cols : query_cols + key_cols],
        grad_w_qkv[:, query_cols + key_cols :],
        grad_bias[query_cols + key_cols :],
        grad_w_o,
        gains[model_width:],
        grad_w_gate,
        grad_w_up,
        grad_w_down,
    )


def solution(mesh):
    tokens = P("seq", "ctx", None)
    weight = P(("seq", "ctx"), "wt")
    return jax.shard_map(
        on_device,
        mesh=mesh,
        in_specs=(
            tokens,
            P("seq", None),
            P(),
            weight,
            P("wt"),
            weight,
            P("wt"),
            weight,
            P("wt"),
            weight,
            P(),
            weight,
            weight,
            weight,
            tokens,
        ),
        out_specs=(
            tokens,
            tokens,
            P(),
            weight,
            P("wt"),
            weight,
            P("wt"),
            weight,
            P("wt"),
            weight,
            P(),
            weight,
            weight,
            weight,
        ),
        check_vma=False,
    )
```

```python
import functools

import jax
import jax.numpy as jnp
from jax import lax
from jax.experimental import pallas as pl
from jax.experimental.pallas import tpu as pltpu
from jax.sharding import PartitionSpec as P

HD = 128
LANES = 128


EPSILON = 1e-06
THETA_BASE = 1000000.0
NEGATIVE = -1e30


def rope_tables(positions):
    freqs = THETA_BASE ** (-(jnp.arange(HD // 2, dtype=jnp.float32) * 2.0) / HD)
    angles = positions.astype(jnp.float32)[:, None] * freqs[None, :]
    cosines = jnp.cos(angles)
    sines = jnp.sin(angles)
    return (jnp.concatenate([cosines, cosines], -1), jnp.concatenate([sines, sines], -1))


def matmul(left, right):
    return jnp.dot(left, right, preferred_element_type=jnp.float32)


def times_transposed(left, right):
    return lax.dot_general(
        left, right, (((1,), (1,)), ((), ())), preferred_element_type=jnp.float32
    )


def inner_rows(left, right):
    return lax.dot_general(
        left, right, (((0,), (0,)), ((), ())), preferred_element_type=jnp.float32
    )


def swap(values, axis, offset):
    size = lax.axis_size(axis)
    return lax.ppermute(values, axis, [(i, i ^ offset) for i in range(size)])


def rows_at(values, index, count):
    return lax.dynamic_slice_in_dim(values, index * count, count, 0)


def place_rows(parts, indices):
    rows = len(parts) * parts[0].shape[0]
    whole = jnp.zeros((rows,) + parts[0].shape[1:], parts[0].dtype)
    for part, index in zip(parts, indices):
        whole = lax.dynamic_update_slice_in_dim(whole, part, index * part.shape[0], 0)
    return whole


def together(*values):
    return lax.optimization_barrier(values)


def relative(values):
    me = lax.axis_index("seq")
    width = values.shape[-1] // 4
    blocks = [
        lax.dynamic_slice_in_dim(values, (me ^ j) * width, width, values.ndim - 1)
        for j in range(4)
    ]
    return jnp.concatenate(blocks, -1)


def gather_ctx(block):
    size = lax.axis_size("ctx")
    return [block] + [swap(block, "ctx", k) for k in range(1, size)]


def exchange_ctx(pieces):
    return [pieces[0]] + [swap(pieces[k], "ctx", k) for k in range(1, len(pieces))]


def near_seq(shard):
    return swap(shard, "seq", 1), swap(shard, "seq", 2)


def far_seq(from_x, from_y):
    half = from_x.shape[0] // 2
    return swap(from_y[:half], "seq", 1), swap(from_x[half:], "seq", 2)


def scatter_near(partial_sum):
    own, for_x, for_y, for_far = jnp.split(partial_sum, 4, 0)
    half = own.shape[0] // 2
    got_x = swap(jnp.concatenate([for_far[half:], for_x[half:]], 0), "seq", 1)
    got_y = swap(jnp.concatenate([for_far[:half], for_y[:half]], 0), "seq", 2)
    return got_x, got_y


def relay(partial_sum, got_x, got_y):
    _, for_x, for_y, _ = jnp.split(partial_sum, 4, 0)
    half = for_x.shape[0] // 2
    on_x = add_up([for_x[:half], got_y[:half]]).astype(jnp.bfloat16)
    on_y = add_up([for_y[half:], got_x[:half]]).astype(jnp.bfloat16)
    return together(on_x, on_y)


def scatter_end(partial_sum, got_x, got_y, last_x, last_y):
    own = partial_sum[: partial_sum.shape[0] // 4]
    half = own.shape[0] // 2
    top = add_up([own[:half], got_y[half:], last_x])
    bottom = add_up([own[half:], got_x[half:], last_y])
    return jnp.concatenate([top, bottom], 0)


def scatter_far(partial_sum, got_x, got_y):
    on_x, on_y = relay(partial_sum, got_x, got_y)
    return scatter_end(
        partial_sum, got_x, got_y, swap(on_x, "seq", 1), swap(on_y, "seq", 2)
    )


def add_up(parts):
    total = parts[0].astype(jnp.float32)
    for part in parts[1:]:
        total = total + part.astype(jnp.float32)
    return total


def units_per(units):
    size = lax.axis_size("ctx")
    return -(-units // (size * LANES)) * LANES


def unit_pieces(shards):
    size = lax.axis_size("ctx")
    ctx = lax.axis_index("ctx")
    width = units_per(shards[0].shape[1])
    padded = [jnp.pad(w, ((0, 0), (0, size * width - w.shape[1]))) for w in shards]
    return [
        jnp.concatenate(
            [lax.dynamic_slice_in_dim(w, (ctx ^ k) * width, width, 1) for w in padded], 1
        )
        for k in range(size)
    ]


def row_pieces(summed):
    size = lax.axis_size("ctx")
    ctx = lax.axis_index("ctx")
    rows = summed.shape[0] // size
    return [rows_at(summed, ctx ^ k, rows) for k in range(size)]


def place_units(parts, units):
    size = lax.axis_size("ctx")
    ctx = lax.axis_index("ctx")
    width = units_per(units)
    wholes = []
    for start in range(0, parts[0].shape[1], width):
        whole = jnp.zeros((parts[0].shape[0], size * width), jnp.float32)
        for k in range(size):
            part = parts[k][:, start : start + width].astype(jnp.float32)
            whole = lax.dynamic_update_slice_in_dim(whole, part, (ctx ^ k) * width, 1)
        wholes.append(whole[:, :units])
    return wholes


def narrow_others(pieces):
    return [pieces[0]] + [piece.astype(jnp.bfloat16) for piece in pieces[1:]]


VMEM_BYTES = 56 * 1024 * 1024
LITTLE = pl.CostEstimate(flops=1, bytes_accessed=1, transcendentals=0)


def mlp_tile(tiles_each, x_mine, x_other, o_mine, o_other, *refs):
    up_parts, gate_down_parts, far = refs[:3], refs[3:6], refs[6:8]
    outs, scratch = refs[8:14], refs[14:]
    both_ref, act_ref, back_mine, back_send, out_mine, out_send = outs
    gu, down, sems = scratch
    step = pl.program_id(0)
    width = down.shape[1]

    @pl.when(step == 0)
    def _():
        copies = []
        for to, parts, start, far_start in (
            (gu.at[:, pl.ds(0, width)], gate_down_parts, 0, width),
            (gu.at[:, pl.ds(width, width)], up_parts, 0, 0),
            (down, gate_down_parts, width, 2 * width),
        ):
            row = 0
            starts = [start] * len(parts) + [far_start] * len(far)
            for part, column in zip((*parts, *far), starts):
                copies.append(
                    pltpu.make_async_copy(
                        part.at[:, pl.ds(column, width)],
                        to.at[pl.ds(row, part.shape[0])],
                        sems.at[len(copies)],
                    )
                )
                row += part.shape[0]
        for copy in copies:
            copy.start()
        for copy in copies:
            copy.wait()

    own = step < tiles_each
    rows = jnp.where(own, x_mine[...], x_other[...])
    grads = jnp.where(own, o_mine[...], o_other[...])
    gate_up = matmul(rows, gu[...])
    g_act = matmul(grads, down[...])
    gate, up = gate_up[:, :width], gate_up[:, width:]
    sigmoid_gate = 1.0 / (1.0 + jnp.exp(-gate))
    silu_gate = gate * sigmoid_gate
    act = (silu_gate * up).astype(jnp.bfloat16)
    g_gate = (g_act * up * sigmoid_gate * (1.0 + gate * (1.0 - sigmoid_gate))).astype(jnp.bfloat16)
    g_up = (g_act * silu_gate).astype(jnp.bfloat16)
    act_ref[...] = act
    both_ref[:, :width] = g_gate
    both_ref[:, width:] = g_up
    back = times_transposed(g_gate, gu[:, :width]) + times_transposed(g_up, gu[:, width:])
    out = times_transposed(act, down[...])

    @pl.when(own)
    def _():
        back_mine[...] = back
        out_mine[...] = out

    @pl.when(jnp.logical_not(own))
    def _():
        back_send[...] = back.astype(jnp.bfloat16)
        out_send[...] = out.astype(jnp.bfloat16)


def mlp(x_mine, x_other, o_mine, o_other, up_parts, gate_down_parts, far):
    count, model_width = x_mine.shape
    width = up_parts[0].shape[1]
    tile = min(256, count)
    tiles_each = count // tile
    mine = pl.BlockSpec((tile, model_width), lambda i: (jnp.minimum(i, tiles_each - 1), 0))
    other = pl.BlockSpec((tile, model_width), lambda i: (jnp.maximum(i - tiles_each, 0), 0))
    left = pl.BlockSpec(memory_space=pl.ANY)
    return pl.pallas_call(
        functools.partial(mlp_tile, tiles_each),
        grid=(2 * tiles_each,),
        in_specs=[mine, other, mine, other] + [left] * 8,
        out_specs=[
            pl.BlockSpec((tile, 2 * width), lambda i: (i, 0)),
            pl.BlockSpec((tile, width), lambda i: (i, 0)),
            mine,
            other,
            mine,
            other,
        ],
        out_shape=[
            jax.ShapeDtypeStruct((2 * count, 2 * width), jnp.bfloat16),
            jax.ShapeDtypeStruct((2 * count, width), jnp.bfloat16),
            jax.ShapeDtypeStruct((count, model_width), jnp.float32),
            jax.ShapeDtypeStruct((count, model_width), jnp.bfloat16),
            jax.ShapeDtypeStruct((count, model_width), jnp.float32),
            jax.ShapeDtypeStruct((count, model_width), jnp.bfloat16),
        ],
        scratch_shapes=[
            pltpu.VMEM((model_width, 2 * width), jnp.bfloat16),
            pltpu.VMEM((model_width, width), jnp.bfloat16),
            pltpu.SemaphoreType.DMA((15,)),
        ],
        compiler_params=pltpu.CompilerParams(vmem_limit_bytes=VMEM_BYTES),
        cost_estimate=LITTLE,
        name="mlp",
    )(x_mine, x_other, o_mine, o_other, *up_parts, *gate_down_parts, *far)


def weight_tile(x_mine, x_other, grads, out):
    count = x_mine.shape[0]
    out[...] = (
        inner_rows(x_mine[...], grads[:count]) + inner_rows(x_other[...], grads[count:])
    ).astype(jnp.bfloat16)


def weight_grad(x_mine, x_other, grads):
    count, model_width = x_mine.shape
    tile = model_width // 4
    columns = pl.BlockSpec((count, tile), lambda i: (0, i))
    return pl.pallas_call(
        weight_tile,
        grid=(4,),
        in_specs=[columns, columns, pl.BlockSpec(grads.shape, lambda i: (0, 0))],
        out_specs=pl.BlockSpec((tile, grads.shape[1]), lambda i: (i, 0)),
        out_shape=jax.ShapeDtypeStruct((model_width, grads.shape[1]), jnp.bfloat16),
        compiler_params=pltpu.CompilerParams(vmem_limit_bytes=VMEM_BYTES),
        cost_estimate=LITTLE,
        name="weight_grad",
    )(x_mine, x_other, grads)


def call(body, outs, args, scratch=(), name=None, in_specs=None):
    whole = pl.BlockSpec(memory_space=pltpu.VMEM)
    return pl.pallas_call(
        body,
        in_specs=in_specs or [whole] * len(args),
        out_specs=[whole] * len(outs),
        out_shape=[jax.ShapeDtypeStruct(shape, dtype) for shape, dtype in outs],
        scratch_shapes=list(scratch),
        compiler_params=pltpu.CompilerParams(vmem_limit_bytes=VMEM_BYTES),
        cost_estimate=LITTLE,
        name=name,
    )(*args)


def beside_body(*refs):
    *parts, out = refs
    start = 0
    for part in parts:
        out[:, start : start + part.shape[1]] = part[...]
        start += part.shape[1]


def side_by_side(parts):
    cols = sum(part.shape[1] for part in parts)
    return call(
        beside_body, [((parts[0].shape[0], cols), parts[0].dtype)], parts, name="side_by_side"
    )[0]


def place_body(groups, ctx_ref, *refs):
    *parts, out = refs
    count = len(parts) // groups
    rows = parts[0].shape[0]
    start = 0
    for group in range(groups):
        cols = parts[group * count].shape[1]
        for k in range(count):
            here = pl.ds(pl.multiple_of((ctx_ref[0] ^ k) * rows, rows), rows)
            out[here, start : start + cols] = parts[group * count + k][...]
        start += cols


def place_ctx(*groups):
    ctx = lax.axis_index("ctx")
    count, rows = len(groups[0]), groups[0][0].shape[0]
    if rows % 16:
        order = [ctx ^ k for k in range(count)]
        return jnp.concatenate([place_rows(parts, order) for parts in groups], 1)
    cols = sum(parts[0].shape[1] for parts in groups)
    parts = [part for group in groups for part in group]
    return call(
        functools.partial(place_body, len(groups)),
        [((count * rows, cols), parts[0].dtype)],
        [ctx.astype(jnp.int32).reshape(1), *parts],
        name="place",
        in_specs=[pl.BlockSpec(memory_space=pltpu.SMEM)]
        + [pl.BlockSpec(memory_space=pltpu.VMEM)] * len(parts),
    )[0]


def turn(values, cosines, signed_sines):
    return values * cosines + pltpu.roll(values, HD // 2, 1) * signed_sines


def turn_back(grads, cosines, signed_sines):
    return grads * cosines + pltpu.roll(grads, HD // 2, 1) * (-signed_sines)


def project_body(query_cols, key_cols, x, bias, cosines, signed_sines, *refs):
    shard, from_x, from_y, far_top, far_bottom = refs[:5]
    query, key_value, w_qkv, w_out, sems = refs[5:]
    near = shard.shape[0]
    half = near // 2
    split = w_qkv.shape[1]
    copies = []
    for part, start in (
        (shard, 0),
        (from_x, near),
        (from_y, 2 * near),
        (far_top, 3 * near),
        (far_bottom, 3 * near + half),
    ):
        rows = pl.ds(start, part.shape[0])
        left, right = part.at[:, pl.ds(0, split)], part.at[:, pl.ds(split, w_out.shape[1])]
        for source, target in ((left, w_qkv.at[rows]), (right, w_out.at[rows])):
            copies.append(pltpu.make_async_copy(source, target, sems.at[len(copies)]))
    for copy in copies:
        copy.start()
    for copy in copies[::2]:
        copy.wait()
    lin = matmul(x[...], w_qkv[...]) + bias[...]
    for start in range(0, query_cols, HD):
        query[:, start : start + HD] = turn(
            lin[:, start : start + HD], cosines[...], signed_sines[...]
        ).astype(jnp.bfloat16)
    for start in range(0, key_cols, HD):
        key_value[:, start : start + HD] = turn(
            lin[:, query_cols + start : query_cols + start + HD], cosines[...], signed_sines[...]
        ).astype(jnp.bfloat16)
    key_value[:, key_cols:] = lin[:, query_cols + key_cols :].astype(jnp.bfloat16)
    for copy in copies[1::2]:
        copy.wait()


def attend_body(count, core_ref, query, query_pos, key_pos, w_out, *refs):
    parts, (heads, log_sums, mine, send, total) = refs[:count], refs[count:]
    keys = jnp.concatenate([part[:, :HD] for part in parts], 0)
    values = jnp.concatenate([part[:, HD:] for part in parts], 0)
    visible = key_pos[...] <= query_pos[...]
    for start in range(0, query.shape[1], HD):
        scores = jnp.where(
            visible, times_transposed(query[:, start : start + HD], keys) * HD**-0.5, NEGATIVE
        )
        highest = jnp.max(scores, -1, keepdims=True)
        weights = jnp.exp(scores - highest)
        totals = jnp.sum(weights, -1, keepdims=True)
        heads[:, start : start + HD] = matmul(
            (weights * (1.0 / totals)).astype(jnp.bfloat16), values
        ).astype(jnp.bfloat16)
        log_sums[:, start : start + HD] = jnp.broadcast_to(
            highest + jnp.log(totals), (query.shape[0], HD)
        )
    split_rows(core_ref, times_transposed(heads[...], w_out[...]), total, mine, send)


def split_rows(core_ref, values, total, mine, send):
    half = mine.shape[0]
    core = core_ref[0]
    total[...] = values
    mine[...] = total[pl.ds(pl.multiple_of(core * half, half), half)]
    send[...] = total[pl.ds(pl.multiple_of((1 - core) * half, half), half)]


def norm_body(mine, got, inputs, gain, hidden, inverse_rms, normed):
    values = inputs[...] + mine[...] + got[...]
    hidden[...] = values
    inverse = lax.rsqrt(jnp.mean(values * values, -1, keepdims=True) + EPSILON)
    inverse_rms[...] = inverse
    normed[...] = (values * inverse * gain[...]).astype(jnp.bfloat16)


def norm_back_body(count, base, inputs, inverse_rms, gain, *refs):
    parts, outs = refs[:count], refs[count:]
    grads = parts[0][...].astype(jnp.float32)
    for part in parts[1:]:
        grads = grads + part[...].astype(jnp.float32)
    inverse = inverse_rms[...]
    values = inputs[...]
    weighted = grads * gain[...]
    back = inverse * weighted - values * (inverse * inverse * inverse) * jnp.mean(
        weighted * values, -1, keepdims=True
    )
    result = base[...].astype(jnp.float32) + back
    outs[0][...] = jnp.sum(grads * values * inverse, 0, keepdims=True)
    outs[1][...] = result.astype(jnp.bfloat16)
    if len(outs) > 2:
        outs[2][...] = result


def attend_back_body(
    count,
    core_ref,
    branch_mine,
    branch_other,
    query,
    query_pos,
    key_pos,
    w_out,
    heads,
    log_sums,
    cosines,
    signed_sines,
    *refs,
):
    parts, (query_lin, g_out), g_parts = refs[:count], refs[count : count + 2], refs[count + 2 : -1]
    branch = refs[-1]
    half = branch_mine.shape[0]
    core = core_ref[0]
    branch[pl.ds(pl.multiple_of(core * half, half), half)] = branch_mine[...]
    branch[pl.ds(pl.multiple_of((1 - core) * half, half), half)] = branch_other[...]
    keys = jnp.concatenate([part[:, :HD] for part in parts], 0)
    values = jnp.concatenate([part[:, HD:] for part in parts], 0)
    visible = key_pos[...] <= query_pos[...]
    g_heads = matmul(branch[...], w_out[...]).astype(jnp.bfloat16)
    scale = HD**-0.5
    g_keys = jnp.zeros(keys.shape, jnp.float32)
    g_values = jnp.zeros(values.shape, jnp.float32)
    for start in range(0, query.shape[1], HD):
        head = query[:, start : start + HD]
        g_head = g_heads[:, start : start + HD]
        scores = jnp.where(visible, times_transposed(head, keys) * scale, NEGATIVE)
        probs = jnp.exp(scores - log_sums[:, start : start + 1])
        g_probs = times_transposed(g_head, values)
        delta = jnp.sum(probs * g_probs, -1, keepdims=True)
        g_scores = (probs * (g_probs - delta)).astype(jnp.bfloat16)
        query_lin[:, start : start + HD] = turn_back(
            matmul(g_scores, keys) * scale, cosines[...], signed_sines[...]
        ).astype(jnp.bfloat16)
        g_keys = g_keys + inner_rows(g_scores, head)
        g_values = g_values + inner_rows(probs.astype(jnp.bfloat16), g_head)
    g_keys = g_keys * scale
    g_out[...] = inner_rows(branch[...], heads[...]).astype(jnp.bfloat16)
    rows = parts[0].shape[0]
    for k, out in enumerate(g_parts):
        out[:, :HD] = g_keys[k * rows : (k + 1) * rows].astype(out.dtype)
        out[:, HD:] = g_values[k * rows : (k + 1) * rows].astype(out.dtype)


def project_back_body(
    count, core_ref, query_lin, normed, w_qkv, cosines, signed_sines, *refs
):
    parts, (g_qkv, g_bias, mine, send, lin, total) = refs[:count], refs[count:]
    g_parts = parts[0][...].astype(jnp.float32)
    for part in parts[1:]:
        g_parts = g_parts + part[...].astype(jnp.float32)
    cols = query_lin.shape[1]
    lin[:, :cols] = query_lin[...]
    lin[:, cols : cols + HD] = turn_back(
        g_parts[:, :HD], cosines[...], signed_sines[...]
    ).astype(jnp.bfloat16)
    lin[:, cols + HD :] = g_parts[:, HD:].astype(jnp.bfloat16)
    split_rows(core_ref, times_transposed(lin[...], w_qkv[...]), total, mine, send)
    g_qkv[...] = inner_rows(normed[...], lin[...]).astype(jnp.bfloat16)
    g_bias[...] = jnp.sum(lin[...].astype(jnp.float32), 0, keepdims=True)


def chip_sum(own, got):
    return jnp.split(own + got.astype(jnp.float32), lax.axis_size("ctx"), 0)


def add_tree(parts):
    while len(parts) > 1:
        parts = [parts[i] + parts[i + 1] for i in range(0, len(parts), 2)]
    return parts[0]


def with_rows(block, rows):
    return jnp.concatenate([block, jnp.pad(rows, ((0, 0), (0, block.shape[1] - rows.shape[1])))], 0)


def on_device(
    layer_input,
    pairs,
    gain_attn,
    w_q,
    b_q,
    w_k,
    b_k,
    w_v,
    b_v,
    w_o,
    gain_mlp,
    w_gate,
    w_up,
    w_down,
    out_grad,
):
    _, span_rows, model_width = layer_input.shape
    half_rows = span_rows // 2
    query_cols = w_q.shape[1]
    key_cols = w_k.shape[1]
    units_here = w_gate.shape[1]
    ctx_size = lax.axis_size("ctx")
    ctx = lax.axis_index("ctx")
    core = lax.axis_index("wt")

    def own_half(values):
        return rows_at(values, core, half_rows)

    def join_halves(mine):
        other = swap(mine, "wt", 1)
        return jnp.where(
            core == 0, jnp.concatenate([mine, other], 0), jnp.concatenate([other, mine], 0)
        )

    within = jnp.arange(half_rows, dtype=jnp.int32)

    def positions_at(index):
        early = lax.dynamic_index_in_dim(pairs[0], index, 0, False)
        return jnp.concatenate(
            [early * half_rows + within, (2 * ctx_size - 1 - early) * half_rows + within]
        )

    query_positions = positions_at(ctx)
    key_positions = jnp.concatenate([positions_at(ctx ^ k) for k in range(ctx_size)])[None]
    cosines, sines = rope_tables(query_positions)
    signed_sines = jnp.concatenate([-sines[:, : HD // 2], sines[:, HD // 2 :]], 1)
    query_positions = query_positions[:, None]
    core_index = core.astype(jnp.int32).reshape(1)
    scalar = pl.BlockSpec(memory_space=pltpu.SMEM)
    whole = pl.BlockSpec(memory_space=pltpu.VMEM)
    left = pl.BlockSpec(memory_space=pl.ANY)

    input_rows = relative(layer_input.reshape(span_rows, model_width)).astype(jnp.float32)
    grad_out = relative(out_grad.reshape(span_rows, model_width))
    gain_one = relative(gain_attn.astype(jnp.float32))[None]
    gain_two = relative(gain_mlp.astype(jnp.float32))[None]

    attn_parts = gather_ctx(side_by_side([w_q, w_k, w_v, w_o]))
    gate_up_pieces = unit_pieces([w_gate, w_up])
    down_pieces = unit_pieces([w_down])
    grad_half = own_half(grad_out)
    attn_shard = place_ctx(attn_parts)
    attn_shard, gate_up_pieces, down_pieces = together(attn_shard, gate_up_pieces, down_pieces)

    attn_near = near_seq(attn_shard)
    gate_up_parts = exchange_ctx(gate_up_pieces)
    attn_near, gate_up_parts, down_pieces = together(attn_near, gate_up_parts, down_pieces)
    attn_far = far_seq(*attn_near)
    down_parts = exchange_ctx(down_pieces)
    width = units_per(units_here)
    up_shard = place_ctx([part[:, width:] for part in gate_up_parts])
    attn_far, up_shard = together(attn_far, up_shard)
    up_near = near_seq(up_shard)

    rms_attn = lax.rsqrt(jnp.mean(input_rows * input_rows, -1, keepdims=True) + EPSILON)
    normed_attn = (input_rows * rms_attn * gain_one).astype(jnp.bfloat16)
    qkv_cols = query_cols + 2 * key_cols
    bias = jnp.concatenate([b_q, b_k, b_v]).astype(jnp.float32)[None]
    query, key_value, w_qkv, w_out = call(
        functools.partial(project_body, query_cols, key_cols),
        [
            ((span_rows, query_cols), jnp.bfloat16),
            ((span_rows, 2 * key_cols), jnp.bfloat16),
            ((model_width, qkv_cols), jnp.bfloat16),
            ((model_width, query_cols), jnp.bfloat16),
        ],
        [normed_attn, bias, cosines, signed_sines, attn_shard, *attn_near, *attn_far],
        [pltpu.SemaphoreType.DMA((10,))],
        "project",
        [whole] * 4 + [left] * 5,
    )
    key_value, down_parts = together(key_value, down_parts)

    keys_values = gather_ctx(key_value)
    half_f32 = ((half_rows, model_width), jnp.float32)
    half_bf16 = ((half_rows, model_width), jnp.bfloat16)
    row_f32 = ((1, model_width), jnp.float32)
    attn_heads, log_sums, attn_mine, attn_send = call(
        functools.partial(attend_body, ctx_size),
        [
            ((span_rows, query_cols), jnp.bfloat16),
            ((span_rows, query_cols), jnp.float32),
            half_f32,
            half_f32,
        ],
        [core_index, query, query_positions, key_positions, w_out, *keys_values],
        [pltpu.VMEM((span_rows, model_width), jnp.float32)],
        "attend",
        [scalar] + [whole] * (4 + ctx_size),
    )
    input_half = own_half(input_rows)
    hidden, rms_mlp, normed_half = call(
        norm_body,
        [half_f32, ((half_rows, 1), jnp.float32), half_bf16],
        [attn_mine, swap(attn_send, "wt", 1), input_half, gain_two],
        name="norm",
    )
    gate_down_shard = place_ctx([part[:, :width] for part in gate_up_parts], down_parts)
    normed_half, gate_down_shard, up_near = together(normed_half, gate_down_shard, up_near)

    gate_down_near = near_seq(gate_down_shard)
    normed_parts, gate_down_near, grad_half = together(
        gather_ctx(normed_half), gate_down_near, grad_half
    )

    mlp_far = far_seq(*(jnp.concatenate(pair, 1) for pair in zip(up_near, gate_down_near)))
    normed_mine = jnp.concatenate(normed_parts, 0)
    normed_other = swap(normed_mine, "wt", 1)
    grad_parts, mlp_far = together(gather_ctx(grad_half), mlp_far)
    grad_mine = jnp.concatenate(grad_parts, 0)
    grad_other = swap(grad_mine, "wt", 1)
    g_both, act, back_mine, back_send, out_mine, out_send = mlp(
        normed_mine,
        normed_other,
        grad_mine,
        grad_other,
        [up_shard, *up_near],
        [gate_down_shard, *gate_down_near],
        mlp_far,
    )
    back_got = swap(back_send, "wt", 1)
    out_got = swap(out_send, "wt", 1)
    g_down = weight_grad(grad_mine, grad_other, act)
    g_normed_pieces = narrow_others(chip_sum(back_mine, back_got))
    g_normed_pieces, g_down, out_got = together(g_normed_pieces, g_down, out_got)

    g_normed_parts = exchange_ctx(g_normed_pieces)
    down_got = scatter_near(g_down)
    down_got, g_both = together(down_got, g_both)
    g_gate_up = weight_grad(normed_mine, normed_other, g_both)
    mlp_pieces = chip_sum(out_mine, out_got)
    down_sum = scatter_far(g_down, *down_got).astype(jnp.bfloat16)
    g_normed_parts, down_sum, g_gate_up, mlp_pieces = together(
        g_normed_parts, down_sum, g_gate_up, mlp_pieces
    )

    mlp_parts = exchange_ctx(narrow_others(mlp_pieces))
    gate_up_got = scatter_near(g_gate_up)
    down_pieces = row_pieces(down_sum)
    grad_gain_mlp, branch_mine, g_hidden = call(
        functools.partial(norm_back_body, ctx_size),
        [row_f32, half_bf16, half_f32],
        [grad_half, hidden, rms_mlp, gain_two, *g_normed_parts],
        name="mlp_norm_back",
    )
    block = (span_rows, 2 * key_cols)
    query_lin, g_out, *g_blocks = call(
        functools.partial(attend_back_body, ctx_size),
        [
            ((span_rows, query_cols), jnp.bfloat16),
            ((model_width, query_cols), jnp.bfloat16),
            (block, jnp.float32),
        ]
        + [(block, jnp.bfloat16)] * (ctx_size - 1),
        [
            core_index,
            branch_mine,
            swap(branch_mine, "wt", 1),
            query,
            query_positions,
            key_positions,
            w_out,
            attn_heads,
            log_sums,
            cosines,
            signed_sines,
            *keys_values,
        ],
        [pltpu.VMEM((span_rows, model_width), jnp.bfloat16)],
        "attend_back",
        [scalar] + [whole] * (10 + ctx_size),
    )
    g_blocks, mlp_parts, gate_up_got, g_out, down_pieces = together(
        g_blocks, mlp_parts, gate_up_got, g_out, down_pieces
    )

    g_key_value_parts = exchange_ctx(g_blocks)
    on_x, on_y = relay(g_gate_up, *gate_up_got)
    g_key_value_parts, down_pieces, last_x, last_y = together(
        g_key_value_parts, down_pieces, swap(on_x, "seq", 1), swap(on_y, "seq", 2)
    )
    down_back = exchange_ctx(down_pieces)
    gate_up_sum = scatter_end(g_gate_up, *gate_up_got, last_x, last_y).astype(jnp.bfloat16)
    gate_up_pieces = row_pieces(gate_up_sum)
    g_qkv, g_bias, normed_mine_grad, normed_send_grad = call(
        functools.partial(project_back_body, ctx_size),
        [
            ((model_width, qkv_cols), jnp.bfloat16),
            ((1, qkv_cols), jnp.float32),
            half_f32,
            half_f32,
        ],
        [
            core_index,
            query_lin,
            normed_attn,
            w_qkv,
            cosines,
            signed_sines,
            *g_key_value_parts,
        ],
        [
            pltpu.VMEM((span_rows, qkv_cols), jnp.bfloat16),
            pltpu.VMEM((span_rows, model_width), jnp.float32),
        ],
        "project_back",
        [scalar] + [whole] * (5 + ctx_size),
    )
    normed_got_grad, g_out = together(swap(normed_send_grad, "wt", 1), g_out)
    out_got = scatter_near(g_out)
    grad_gain_attn, grad_input_half = call(
        functools.partial(norm_back_body, 2),
        [row_f32, half_bf16],
        [
            g_hidden,
            input_half,
            own_half(rms_attn),
            gain_one,
            normed_mine_grad,
            normed_got_grad,
        ],
        name="attn_norm_back",
    )
    grad_input_half = relative(grad_input_half)

    small = jnp.concatenate(
        [
            relative(grad_gain_attn)[0],
            relative(grad_gain_mlp)[0],
            g_bias[0],
        ]
    ).astype(jnp.bfloat16)
    small_size = small.shape[0]
    small_rows = -(-small_size // (qkv_cols * 16)) * 16
    small = jnp.pad(small, (0, small_rows * qkv_cols - small_size)).reshape(small_rows, qkv_cols)

    down_back, gate_up_pieces, out_got, g_qkv, small = together(
        down_back, gate_up_pieces, out_got, g_qkv, small
    )

    gate_up_back = exchange_ctx(gate_up_pieces)
    _, for_x, for_y, for_far = jnp.split(g_qkv, 4, 0)
    rows = for_x.shape[0]
    half = rows // 2
    got_x = swap(jnp.concatenate([for_far[half:], for_x[half:], small], 0), "seq", 1)
    got_y = swap(jnp.concatenate([for_far[:half], for_y[:half]], 0), "seq", 2)
    attn_got = tuple(jnp.concatenate(pair, 1) for pair in zip((got_x[:rows], got_y), out_got))
    small = add_up([small, got_x[rows:]]).astype(jnp.bfloat16)
    g_attn = jnp.concatenate([g_qkv, g_out], 1)
    on_x, on_y = relay(g_attn, *attn_got)
    last_x = swap(on_x, "seq", 1)
    last_y = swap(with_rows(on_y, small), "seq", 2)
    small = add_up([small, last_y[half:, :qkv_cols]]).astype(jnp.bfloat16)
    attn_sum = scatter_end(g_attn, *attn_got, last_x, last_y[:half])
    attn_pieces = row_pieces(attn_sum)
    attn_send = [with_rows(piece.astype(jnp.bfloat16), small) for piece in attn_pieces]
    attn_send, gate_up_back, grad_input_half, mlp_parts = together(
        attn_send, gate_up_back, grad_input_half, mlp_parts
    )
    attn_back = exchange_ctx(attn_send)
    grad_input = join_halves(grad_input_half)
    layer_output = join_halves(relative((hidden + add_up(mlp_parts)).astype(jnp.bfloat16)))
    attn_back = attn_pieces[:1] + attn_back[1:]
    rows = attn_pieces[0].shape[0]
    grad_w_gate, grad_w_up = place_units(gate_up_back, units_here)
    (grad_w_down,) = place_units(down_back, units_here)
    grad_w_attn = add_up([part[:rows] for part in attn_back])
    grad_w_qkv = grad_w_attn[:, :qkv_cols]
    grad_w_o = grad_w_attn[:, qkv_cols:]
    small = add_tree(
        [small.astype(jnp.float32)]
        + [part[rows:, :qkv_cols].astype(jnp.float32) for part in attn_back[1:]]
    ).reshape(-1)
    gains = small[: 2 * model_width].reshape(-1, LANES)
    gains = (gains + swap(gains, "wt", 1)).reshape(-1)
    grad_bias = small[2 * model_width : small_size]
    return (
        layer_output[None],
        grad_input[None],
        gains[:model_width],
        grad_w_qkv[:, :query_cols],
        grad_bias[:query_cols],
        grad_w_qkv[:, query_cols : query_cols + key_cols],
        grad_bias[query_cols : query_cols + key_cols],
        grad_w_qkv[:, query_cols + key_cols :],
        grad_bias[query_cols + key_cols :],
        grad_w_o,
        gains[model_width:],
        grad_w_gate,
        grad_w_up,
        grad_w_down,
    )


def solution(mesh):
    tokens = P("seq", "ctx", None)
    weight = P(("seq", "ctx"), "wt")
    return jax.shard_map(
        on_device,
        mesh=mesh,
        in_specs=(
            tokens,
            P("seq", None),
            P(),
            weight,
            P("wt"),
            weight,
            P("wt"),
            weight,
            P("wt"),
            weight,
            P(),
            weight,
            weight,
            weight,
            tokens,
        ),
        out_specs=(
            tokens,
            tokens,
            P(),
            weight,
            P("wt"),
            weight,
            P("wt"),
            weight,
            P("wt"),
            weight,
            P(),
            weight,
            weight,
            weight,
        ),
        check_vma=False,
    )
```

```python
import functools

import jax
import jax.numpy as jnp
from jax import lax
from jax.experimental import pallas as pl
from jax.experimental.pallas import tpu as pltpu
from jax.sharding import PartitionSpec as P

HD = 128
LANES = 128


EPSILON = 1e-06
THETA_BASE = 1000000.0
NEGATIVE = -1e30


def rope_tables(positions):
    freqs = THETA_BASE ** (-(jnp.arange(HD // 2, dtype=jnp.float32) * 2.0) / HD)
    angles = positions.astype(jnp.float32)[:, None] * freqs[None, :]
    cosines = jnp.cos(angles)
    sines = jnp.sin(angles)
    return (jnp.concatenate([cosines, cosines], -1), jnp.concatenate([sines, sines], -1))


def matmul(left, right):
    return jnp.dot(left, right, preferred_element_type=jnp.float32)


def times_transposed(left, right):
    return lax.dot_general(
        left, right, (((1,), (1,)), ((), ())), preferred_element_type=jnp.float32
    )


def inner_rows(left, right):
    return lax.dot_general(
        left, right, (((0,), (0,)), ((), ())), preferred_element_type=jnp.float32
    )


def swap(values, axis, offset):
    size = lax.axis_size(axis)
    return lax.ppermute(values, axis, [(i, i ^ offset) for i in range(size)])


def rows_at(values, index, count):
    return lax.dynamic_slice_in_dim(values, index * count, count, 0)


def place_rows(parts, indices):
    rows = len(parts) * parts[0].shape[0]
    whole = jnp.zeros((rows,) + parts[0].shape[1:], parts[0].dtype)
    for part, index in zip(parts, indices):
        whole = lax.dynamic_update_slice_in_dim(whole, part, index * part.shape[0], 0)
    return whole


def together(*values):
    return lax.optimization_barrier(values)


def relative(values):
    me = lax.axis_index("seq")
    width = values.shape[-1] // 4
    blocks = [
        lax.dynamic_slice_in_dim(values, (me ^ j) * width, width, values.ndim - 1)
        for j in range(4)
    ]
    return jnp.concatenate(blocks, -1)


def gather_ctx(block):
    size = lax.axis_size("ctx")
    return [block] + [swap(block, "ctx", k) for k in range(1, size)]


def exchange_ctx(pieces):
    return [pieces[0]] + [swap(pieces[k], "ctx", k) for k in range(1, len(pieces))]


def near_seq(shard):
    return swap(shard, "seq", 1), swap(shard, "seq", 2)


def far_seq(from_x, from_y):
    half = from_x.shape[0] // 2
    return swap(from_y[:half], "seq", 1), swap(from_x[half:], "seq", 2)


def scatter_near(partial_sum):
    own, for_x, for_y, for_far = jnp.split(partial_sum, 4, 0)
    half = own.shape[0] // 2
    got_x = swap(jnp.concatenate([for_far[half:], for_x[half:]], 0), "seq", 1)
    got_y = swap(jnp.concatenate([for_far[:half], for_y[:half]], 0), "seq", 2)
    return got_x, got_y


def relay(partial_sum, got_x, got_y):
    _, for_x, for_y, _ = jnp.split(partial_sum, 4, 0)
    half = for_x.shape[0] // 2
    on_x = add_up([for_x[:half], got_y[:half]]).astype(jnp.bfloat16)
    on_y = add_up([for_y[half:], got_x[:half]]).astype(jnp.bfloat16)
    return together(on_x, on_y)


def scatter_end(partial_sum, got_x, got_y, last_x, last_y):
    own = partial_sum[: partial_sum.shape[0] // 4]
    half = own.shape[0] // 2
    top = add_up([own[:half], got_y[half:], last_x])
    bottom = add_up([own[half:], got_x[half:], last_y])
    return jnp.concatenate([top, bottom], 0)


def scatter_far(partial_sum, got_x, got_y):
    on_x, on_y = relay(partial_sum, got_x, got_y)
    return scatter_end(
        partial_sum, got_x, got_y, swap(on_x, "seq", 1), swap(on_y, "seq", 2)
    )


def add_up(parts):
    total = parts[0].astype(jnp.float32)
    for part in parts[1:]:
        total = total + part.astype(jnp.float32)
    return total


def units_per(units):
    size = lax.axis_size("ctx")
    return -(-units // (size * LANES)) * LANES


def unit_pieces(shards):
    size = lax.axis_size("ctx")
    ctx = lax.axis_index("ctx")
    width = units_per(shards[0].shape[1])
    padded = [jnp.pad(w, ((0, 0), (0, size * width - w.shape[1]))) for w in shards]
    return [
        jnp.concatenate(
            [lax.dynamic_slice_in_dim(w, (ctx ^ k) * width, width, 1) for w in padded], 1
        )
        for k in range(size)
    ]


def row_pieces(summed):
    size = lax.axis_size("ctx")
    ctx = lax.axis_index("ctx")
    rows = summed.shape[0] // size
    return [rows_at(summed, ctx ^ k, rows) for k in range(size)]


def place_units(parts, units):
    size = lax.axis_size("ctx")
    ctx = lax.axis_index("ctx")
    width = units_per(units)
    wholes = []
    for start in range(0, parts[0].shape[1], width):
        whole = jnp.zeros((parts[0].shape[0], size * width), jnp.float32)
        for k in range(size):
            part = parts[k][:, start : start + width].astype(jnp.float32)
            whole = lax.dynamic_update_slice_in_dim(whole, part, (ctx ^ k) * width, 1)
        wholes.append(whole[:, :units])
    return wholes


def narrow_others(pieces):
    return [pieces[0]] + [piece.astype(jnp.bfloat16) for piece in pieces[1:]]


VMEM_BYTES = 56 * 1024 * 1024
LITTLE = pl.CostEstimate(flops=1, bytes_accessed=1, transcendentals=0)


def stack_copies(targets, sems, used=0):
    copies = []
    for target, parts in targets:
        row, cols = 0, target.shape[1]
        group = []
        for part, column in parts:
            group.append(
                pltpu.make_async_copy(
                    part.at[:, pl.ds(column, cols)],
                    target.at[pl.ds(row, part.shape[0])],
                    sems.at[used + sum(map(len, copies)) + len(group)],
                )
            )
            row += part.shape[0]
        copies.append(group)
    return copies


def start_all(groups):
    for group in groups:
        for copy in group:
            copy.start()


def wait_all(groups):
    for group in groups:
        for copy in group:
            copy.wait()


def gate_up_copies(refs, gu, sems):
    up, gate_down, far = refs[:3], refs[3:6], refs[6:8]
    width = gu.shape[1] // 2
    return [
        (gu.at[:, pl.ds(0, width)], [(p, 0) for p in gate_down] + [(p, width) for p in far]),
        (gu.at[:, pl.ds(width, width)], [(p, 0) for p in up] + [(p, 0) for p in far]),
    ]


def forward_tile(tiles_each, x_mine, x_other, *refs):
    parts, (gate_up, gu, sems) = refs[:8], refs[8:]
    step = pl.program_id(0)

    @pl.when(step == 0)
    def _():
        copies = stack_copies(gate_up_copies(parts, gu, sems), sems)
        start_all(copies)
        wait_all(copies)

    rows = jnp.where(step < tiles_each, x_mine[...], x_other[...])
    gate_up[...] = matmul(rows, gu[...])


def backward_tile(tiles_each, gate_up, o_mine, o_other, *refs):
    parts, refs = refs[:8], refs[8:]
    both_ref, act_ref, back_mine, back_send, out_mine, out_send, gu, down, sems = refs
    step = pl.program_id(0)
    own = step < tiles_each
    width = down.shape[1]

    down_target = [(down, [(p, width) for p in parts[3:6]] + [(p, 2 * width) for p in parts[6:]])]

    @pl.when(step == 0)
    def _():
        first = stack_copies(down_target, sems)
        start_all(first)
        start_all(stack_copies(gate_up_copies(parts, gu, sems), sems, 5))
        wait_all(first)

    grads = jnp.where(own, o_mine[...], o_other[...])
    g_act = matmul(grads, down[...])
    gate, up = gate_up[:, :width], gate_up[:, width:]
    sigmoid_gate = 1.0 / (1.0 + jnp.exp(-gate))
    silu_gate = gate * sigmoid_gate
    act_ref[...] = (silu_gate * up).astype(jnp.bfloat16)
    both_ref[:, :width] = (
        g_act * up * sigmoid_gate * (1.0 + gate * (1.0 - sigmoid_gate))
    ).astype(jnp.bfloat16)
    both_ref[:, width:] = (g_act * silu_gate).astype(jnp.bfloat16)

    @pl.when(step == 0)
    def _():
        wait_all(stack_copies(gate_up_copies(parts, gu, sems), sems, 5))

    back = times_transposed(both_ref[...], gu[...])
    out = times_transposed(act_ref[...], down[...])

    @pl.when(own)
    def _():
        back_mine[...] = back
        out_mine[...] = out

    @pl.when(jnp.logical_not(own))
    def _():
        back_send[...] = back.astype(jnp.bfloat16)
        out_send[...] = out.astype(jnp.bfloat16)


def by_tiles(body, count, ins, halves, parts, outs, half_outs, scratch, name):
    tile = min(256, count)
    tiles_each = count // tile

    def rows(cols):
        return pl.BlockSpec((tile, cols), lambda i: (i, 0))

    def mine(cols):
        return pl.BlockSpec((tile, cols), lambda i: (jnp.minimum(i, tiles_each - 1), 0))

    def other(cols):
        return pl.BlockSpec((tile, cols), lambda i: (jnp.maximum(i - tiles_each, 0), 0))

    return pl.pallas_call(
        functools.partial(body, tiles_each),
        grid=(2 * tiles_each,),
        in_specs=[rows(x.shape[1]) for x in ins]
        + [spec(x.shape[1]) for pair in halves for spec, x in zip((mine, other), pair)]
        + [pl.BlockSpec(memory_space=pl.ANY)] * len(parts),
        out_specs=[rows(cols) for cols, _ in outs]
        + [spec(cols) for cols in half_outs for spec in (mine, other)],
        out_shape=[jax.ShapeDtypeStruct((2 * count, cols), dtype) for cols, dtype in outs]
        + [
            jax.ShapeDtypeStruct((count, cols), dtype)
            for cols in half_outs
            for dtype in (jnp.float32, jnp.bfloat16)
        ],
        scratch_shapes=[pltpu.VMEM(shape, jnp.bfloat16) for shape in scratch]
        + [pltpu.SemaphoreType.DMA((15,))],
        compiler_params=pltpu.CompilerParams(vmem_limit_bytes=VMEM_BYTES),
        cost_estimate=LITTLE,
        name=name,
    )(*ins, *(x for pair in halves for x in pair), *parts)


def weight_tile(x_mine, x_other, grads, out):
    count = x_mine.shape[0]
    out[...] = (
        inner_rows(x_mine[...], grads[:count]) + inner_rows(x_other[...], grads[count:])
    ).astype(jnp.bfloat16)


def weight_grad(x_mine, x_other, grads):
    count, model_width = x_mine.shape
    tile = model_width // 4
    columns = pl.BlockSpec((count, tile), lambda i: (0, i))
    return pl.pallas_call(
        weight_tile,
        grid=(4,),
        in_specs=[columns, columns, pl.BlockSpec(grads.shape, lambda i: (0, 0))],
        out_specs=pl.BlockSpec((tile, grads.shape[1]), lambda i: (i, 0)),
        out_shape=jax.ShapeDtypeStruct((model_width, grads.shape[1]), jnp.bfloat16),
        compiler_params=pltpu.CompilerParams(vmem_limit_bytes=VMEM_BYTES),
        cost_estimate=LITTLE,
        name="weight_grad",
    )(x_mine, x_other, grads)


def call(body, outs, args, scratch=(), name=None, in_specs=None):
    whole = pl.BlockSpec(memory_space=pltpu.VMEM)
    return pl.pallas_call(
        body,
        in_specs=in_specs or [whole] * len(args),
        out_specs=[whole] * len(outs),
        out_shape=[jax.ShapeDtypeStruct(shape, dtype) for shape, dtype in outs],
        scratch_shapes=list(scratch),
        compiler_params=pltpu.CompilerParams(vmem_limit_bytes=VMEM_BYTES),
        cost_estimate=LITTLE,
        name=name,
    )(*args)


def beside_body(*refs):
    *parts, out = refs
    start = 0
    for part in parts:
        out[:, start : start + part.shape[1]] = part[...]
        start += part.shape[1]


def side_by_side(parts):
    cols = sum(part.shape[1] for part in parts)
    return call(
        beside_body, [((parts[0].shape[0], cols), parts[0].dtype)], parts, name="side_by_side"
    )[0]


def place_body(groups, ctx_ref, *refs):
    *parts, out = refs
    count = len(parts) // groups
    rows = parts[0].shape[0]
    start = 0
    for group in range(groups):
        cols = parts[group * count].shape[1]
        for k in range(count):
            here = pl.ds(pl.multiple_of((ctx_ref[0] ^ k) * rows, rows), rows)
            out[here, start : start + cols] = parts[group * count + k][...]
        start += cols


def place_ctx(*groups):
    ctx = lax.axis_index("ctx")
    count, rows = len(groups[0]), groups[0][0].shape[0]
    if rows % 16:
        order = [ctx ^ k for k in range(count)]
        return jnp.concatenate([place_rows(parts, order) for parts in groups], 1)
    cols = sum(parts[0].shape[1] for parts in groups)
    parts = [part for group in groups for part in group]
    return call(
        functools.partial(place_body, len(groups)),
        [((count * rows, cols), parts[0].dtype)],
        [ctx.astype(jnp.int32).reshape(1), *parts],
        name="place",
        in_specs=[pl.BlockSpec(memory_space=pltpu.SMEM)]
        + [pl.BlockSpec(memory_space=pltpu.VMEM)] * len(parts),
    )[0]


def turn(values, cosines, signed_sines):
    return values * cosines + pltpu.roll(values, HD // 2, 1) * signed_sines


def turn_back(grads, cosines, signed_sines):
    return grads * cosines + pltpu.roll(grads, HD // 2, 1) * (-signed_sines)


def project_body(query_cols, key_cols, x, bias, cosines, signed_sines, *refs):
    shard, from_x, from_y, far_top, far_bottom = refs[:5]
    query, key_value, w_qkv, w_out, sems = refs[5:]
    near = shard.shape[0]
    half = near // 2
    split = w_qkv.shape[1]
    copies = []
    for part, start in (
        (shard, 0),
        (from_x, near),
        (from_y, 2 * near),
        (far_top, 3 * near),
        (far_bottom, 3 * near + half),
    ):
        rows = pl.ds(start, part.shape[0])
        left, right = part.at[:, pl.ds(0, split)], part.at[:, pl.ds(split, w_out.shape[1])]
        for source, target in ((left, w_qkv.at[rows]), (right, w_out.at[rows])):
            copies.append(pltpu.make_async_copy(source, target, sems.at[len(copies)]))
    for copy in copies:
        copy.start()
    for copy in copies[::2]:
        copy.wait()
    lin = matmul(x[...], w_qkv[...]) + bias[...]
    for start in range(0, query_cols, HD):
        query[:, start : start + HD] = turn(
            lin[:, start : start + HD], cosines[...], signed_sines[...]
        ).astype(jnp.bfloat16)
    for start in range(0, key_cols, HD):
        key_value[:, start : start + HD] = turn(
            lin[:, query_cols + start : query_cols + start + HD], cosines[...], signed_sines[...]
        ).astype(jnp.bfloat16)
    key_value[:, key_cols:] = lin[:, query_cols + key_cols :].astype(jnp.bfloat16)
    for copy in copies[1::2]:
        copy.wait()


def attend_body(count, core_ref, query, query_pos, key_pos, w_out, *refs):
    parts, (heads, log_sums, mine, send, total) = refs[:count], refs[count:]
    keys = jnp.concatenate([part[:, :HD] for part in parts], 0)
    values = jnp.concatenate([part[:, HD:] for part in parts], 0)
    visible = key_pos[...] <= query_pos[...]
    for start in range(0, query.shape[1], HD):
        scores = jnp.where(
            visible, times_transposed(query[:, start : start + HD], keys) * HD**-0.5, NEGATIVE
        )
        highest = jnp.max(scores, -1, keepdims=True)
        weights = jnp.exp(scores - highest)
        totals = jnp.sum(weights, -1, keepdims=True)
        heads[:, start : start + HD] = matmul(
            (weights * (1.0 / totals)).astype(jnp.bfloat16), values
        ).astype(jnp.bfloat16)
        log_sums[:, start : start + HD] = jnp.broadcast_to(
            highest + jnp.log(totals), (query.shape[0], HD)
        )
    split_rows(core_ref, times_transposed(heads[...], w_out[...]), total, mine, send)


def split_rows(core_ref, values, total, mine, send):
    half = mine.shape[0]
    core = core_ref[0]
    total[...] = values
    mine[...] = total[pl.ds(pl.multiple_of(core * half, half), half)]
    send[...] = total[pl.ds(pl.multiple_of((1 - core) * half, half), half)]


def norm_body(mine, got, inputs, gain, hidden, inverse_rms, normed):
    values = inputs[...] + mine[...] + got[...]
    hidden[...] = values
    inverse = lax.rsqrt(jnp.mean(values * values, -1, keepdims=True) + EPSILON)
    inverse_rms[...] = inverse
    normed[...] = (values * inverse * gain[...]).astype(jnp.bfloat16)


def norm_back_body(count, base, inputs, inverse_rms, gain, *refs):
    parts, outs = refs[:count], refs[count:]
    grads = parts[0][...].astype(jnp.float32)
    for part in parts[1:]:
        grads = grads + part[...].astype(jnp.float32)
    inverse = inverse_rms[...]
    values = inputs[...]
    weighted = grads * gain[...]
    back = inverse * weighted - values * (inverse * inverse * inverse) * jnp.mean(
        weighted * values, -1, keepdims=True
    )
    result = base[...].astype(jnp.float32) + back
    outs[0][...] = jnp.sum(grads * values * inverse, 0, keepdims=True)
    outs[1][...] = result.astype(jnp.bfloat16)
    if len(outs) > 2:
        outs[2][...] = result


def attend_back_body(
    count,
    core_ref,
    branch_mine,
    branch_other,
    query,
    query_pos,
    key_pos,
    w_out,
    heads,
    log_sums,
    cosines,
    signed_sines,
    *refs,
):
    parts, (query_lin, g_out), g_parts = refs[:count], refs[count : count + 2], refs[count + 2 : -1]
    branch = refs[-1]
    half = branch_mine.shape[0]
    core = core_ref[0]
    branch[pl.ds(pl.multiple_of(core * half, half), half)] = branch_mine[...]
    branch[pl.ds(pl.multiple_of((1 - core) * half, half), half)] = branch_other[...]
    keys = jnp.concatenate([part[:, :HD] for part in parts], 0)
    values = jnp.concatenate([part[:, HD:] for part in parts], 0)
    visible = key_pos[...] <= query_pos[...]
    g_heads = matmul(branch[...], w_out[...]).astype(jnp.bfloat16)
    scale = HD**-0.5
    g_keys = jnp.zeros(keys.shape, jnp.float32)
    g_values = jnp.zeros(values.shape, jnp.float32)
    for start in range(0, query.shape[1], HD):
        head = query[:, start : start + HD]
        g_head = g_heads[:, start : start + HD]
        scores = jnp.where(visible, times_transposed(head, keys) * scale, NEGATIVE)
        probs = jnp.exp(scores - log_sums[:, start : start + 1])
        g_probs = times_transposed(g_head, values)
        delta = jnp.sum(probs * g_probs, -1, keepdims=True)
        g_scores = (probs * (g_probs - delta)).astype(jnp.bfloat16)
        query_lin[:, start : start + HD] = turn_back(
            matmul(g_scores, keys) * scale, cosines[...], signed_sines[...]
        ).astype(jnp.bfloat16)
        g_keys = g_keys + inner_rows(g_scores, head)
        g_values = g_values + inner_rows(probs.astype(jnp.bfloat16), g_head)
    g_keys = g_keys * scale
    g_out[...] = inner_rows(branch[...], heads[...]).astype(jnp.bfloat16)
    rows = parts[0].shape[0]
    for k, out in enumerate(g_parts):
        out[:, :HD] = g_keys[k * rows : (k + 1) * rows].astype(out.dtype)
        out[:, HD:] = g_values[k * rows : (k + 1) * rows].astype(out.dtype)


def product_body(left, right, out):
    out[...] = inner_rows(left[...], right[...]).astype(jnp.bfloat16)


def project_back_body(
    count, core_ref, query_lin, w_qkv, cosines, signed_sines, inputs, inverse_rms, *refs
):
    parts, (lin, g_bias, g_gain, mine, send, total) = refs[:count], refs[count:]
    g_parts = parts[0][...].astype(jnp.float32)
    for part in parts[1:]:
        g_parts = g_parts + part[...].astype(jnp.float32)
    cols = query_lin.shape[1]
    lin[:, :cols] = query_lin[...]
    lin[:, cols : cols + HD] = turn_back(
        g_parts[:, :HD], cosines[...], signed_sines[...]
    ).astype(jnp.bfloat16)
    lin[:, cols + HD :] = g_parts[:, HD:].astype(jnp.bfloat16)
    split_rows(core_ref, times_transposed(lin[...], w_qkv[...]), total, mine, send)
    g_gain[...] = jnp.sum(total[...] * inputs[...] * inverse_rms[...], 0, keepdims=True)
    g_bias[...] = jnp.sum(lin[...].astype(jnp.float32), 0, keepdims=True)


def chip_sum(own, got):
    return jnp.split(own + got.astype(jnp.float32), lax.axis_size("ctx"), 0)


def add_tree(parts):
    while len(parts) > 1:
        parts = [parts[i] + parts[i + 1] for i in range(0, len(parts), 2)]
    return parts[0]


def with_rows(block, rows):
    return jnp.concatenate([block, jnp.pad(rows, ((0, 0), (0, block.shape[1] - rows.shape[1])))], 0)


def on_device(
    layer_input,
    pairs,
    gain_attn,
    w_q,
    b_q,
    w_k,
    b_k,
    w_v,
    b_v,
    w_o,
    gain_mlp,
    w_gate,
    w_up,
    w_down,
    out_grad,
):
    _, span_rows, model_width = layer_input.shape
    half_rows = span_rows // 2
    query_cols = w_q.shape[1]
    key_cols = w_k.shape[1]
    units_here = w_gate.shape[1]
    ctx_size = lax.axis_size("ctx")
    ctx = lax.axis_index("ctx")
    core = lax.axis_index("wt")

    def own_half(values):
        return rows_at(values, core, half_rows)

    def join_halves(mine):
        other = swap(mine, "wt", 1)
        return jnp.where(
            core == 0, jnp.concatenate([mine, other], 0), jnp.concatenate([other, mine], 0)
        )

    within = jnp.arange(half_rows, dtype=jnp.int32)

    def positions_at(index):
        early = lax.dynamic_index_in_dim(pairs[0], index, 0, False)
        return jnp.concatenate(
            [early * half_rows + within, (2 * ctx_size - 1 - early) * half_rows + within]
        )

    query_positions = positions_at(ctx)
    key_positions = jnp.concatenate([positions_at(ctx ^ k) for k in range(ctx_size)])[None]
    cosines, sines = rope_tables(query_positions)
    signed_sines = jnp.concatenate([-sines[:, : HD // 2], sines[:, HD // 2 :]], 1)
    query_positions = query_positions[:, None]
    core_index = core.astype(jnp.int32).reshape(1)
    scalar = pl.BlockSpec(memory_space=pltpu.SMEM)
    whole = pl.BlockSpec(memory_space=pltpu.VMEM)
    left = pl.BlockSpec(memory_space=pl.ANY)

    input_rows = relative(layer_input.reshape(span_rows, model_width)).astype(jnp.float32)
    grad_out = relative(out_grad.reshape(span_rows, model_width))
    gain_one = relative(gain_attn.astype(jnp.float32))[None]
    gain_two = relative(gain_mlp.astype(jnp.float32))[None]

    attn_parts = gather_ctx(side_by_side([w_q, w_k, w_v, w_o]))
    gate_up_pieces = unit_pieces([w_gate, w_up])
    down_pieces = unit_pieces([w_down])
    grad_half = own_half(grad_out)
    attn_shard = place_ctx(attn_parts)
    attn_shard, gate_up_pieces, down_pieces = together(attn_shard, gate_up_pieces, down_pieces)

    attn_near = near_seq(attn_shard)
    gate_up_parts = exchange_ctx(gate_up_pieces)
    attn_near, gate_up_parts, down_pieces = together(attn_near, gate_up_parts, down_pieces)
    attn_far = far_seq(*attn_near)
    down_parts = exchange_ctx(down_pieces)
    width = units_per(units_here)
    up_shard = place_ctx([part[:, width:] for part in gate_up_parts])
    attn_far, up_shard = together(attn_far, up_shard)
    up_near = near_seq(up_shard)

    rms_attn = lax.rsqrt(jnp.mean(input_rows * input_rows, -1, keepdims=True) + EPSILON)
    normed_attn = (input_rows * rms_attn * gain_one).astype(jnp.bfloat16)
    qkv_cols = query_cols + 2 * key_cols
    bias = jnp.concatenate([b_q, b_k, b_v]).astype(jnp.float32)[None]
    query, key_value, w_qkv, w_out = call(
        functools.partial(project_body, query_cols, key_cols),
        [
            ((span_rows, query_cols), jnp.bfloat16),
            ((span_rows, 2 * key_cols), jnp.bfloat16),
            ((model_width, qkv_cols), jnp.bfloat16),
            ((model_width, query_cols), jnp.bfloat16),
        ],
        [normed_attn, bias, cosines, signed_sines, attn_shard, *attn_near, *attn_far],
        [pltpu.SemaphoreType.DMA((10,))],
        "project",
        [whole] * 4 + [left] * 5,
    )
    key_value, down_parts = together(key_value, down_parts)

    gate_down_shard = place_ctx([part[:, :width] for part in gate_up_parts], down_parts)
    keys_values, gate_down_shard = together(gather_ctx(key_value), gate_down_shard)
    half_f32 = ((half_rows, model_width), jnp.float32)
    half_bf16 = ((half_rows, model_width), jnp.bfloat16)
    row_f32 = ((1, model_width), jnp.float32)
    attn_heads, log_sums, attn_mine, attn_send = call(
        functools.partial(attend_body, ctx_size),
        [
            ((span_rows, query_cols), jnp.bfloat16),
            ((span_rows, query_cols), jnp.float32),
            half_f32,
            half_f32,
        ],
        [core_index, query, query_positions, key_positions, w_out, *keys_values],
        [pltpu.VMEM((span_rows, model_width), jnp.float32)],
        "attend",
        [scalar] + [whole] * (4 + ctx_size),
    )
    input_half = own_half(input_rows)
    hidden, rms_mlp, normed_half = call(
        norm_body,
        [half_f32, ((half_rows, 1), jnp.float32), half_bf16],
        [attn_mine, swap(attn_send, "wt", 1), input_half, gain_two],
        name="norm",
    )
    normed_half, gate_down_shard, up_near = together(normed_half, gate_down_shard, up_near)

    gate_down_near = near_seq(gate_down_shard)
    normed_parts, gate_down_near, grad_half = together(
        gather_ctx(normed_half), gate_down_near, grad_half
    )

    mlp_far = far_seq(*(jnp.concatenate(pair, 1) for pair in zip(up_near, gate_down_near)))
    normed_mine = jnp.concatenate(normed_parts, 0)
    normed_other, grad_half = together(swap(normed_mine, "wt", 1), grad_half)
    count = normed_mine.shape[0]
    mlp_parts = [up_shard, *up_near, gate_down_shard, *gate_down_near, *mlp_far]
    (gate_up,) = by_tiles(
        forward_tile,
        count,
        [],
        [(normed_mine, normed_other)],
        mlp_parts,
        [(2 * width, jnp.float32)],
        [],
        [(model_width, 2 * width)],
        "gate_up",
    )
    grad_parts, gate_up = together(gather_ctx(grad_half), gate_up)
    grad_mine = jnp.concatenate(grad_parts, 0)
    grad_other = swap(grad_mine, "wt", 1)
    g_both, act, back_mine, back_send, out_mine, out_send = by_tiles(
        backward_tile,
        count,
        [gate_up],
        [(grad_mine, grad_other)],
        mlp_parts,
        [(2 * width, jnp.bfloat16), (width, jnp.bfloat16)],
        [model_width, model_width],
        [(model_width, 2 * width), (model_width, width)],
        "mlp_back",
    )
    back_got = swap(back_send, "wt", 1)
    out_got = swap(out_send, "wt", 1)
    g_down = weight_grad(grad_mine, grad_other, act)
    g_normed_pieces = narrow_others(chip_sum(back_mine, back_got))
    g_normed_pieces, g_down, out_got = together(g_normed_pieces, g_down, out_got)

    g_normed_parts = exchange_ctx(g_normed_pieces)
    down_got = scatter_near(g_down)
    down_got, g_both = together(down_got, g_both)
    g_gate_up = weight_grad(normed_mine, normed_other, g_both)
    mlp_pieces = chip_sum(out_mine, out_got)
    down_sum = scatter_far(g_down, *down_got).astype(jnp.bfloat16)
    g_normed_parts, down_sum, g_gate_up, mlp_pieces = together(
        g_normed_parts, down_sum, g_gate_up, mlp_pieces
    )

    down_back = lax.all_to_all(
        down_sum.reshape(ctx_size, -1, down_sum.shape[1]), "ctx", 0, 0, tiled=True
    )
    gate_up_got = scatter_near(g_gate_up)
    grad_gain_mlp, branch_mine, g_hidden = call(
        functools.partial(norm_back_body, ctx_size),
        [row_f32, half_bf16, half_f32],
        [grad_half, hidden, rms_mlp, gain_two, *g_normed_parts],
        name="mlp_norm_back",
    )
    block = (span_rows, 2 * key_cols)
    query_lin, g_out, *g_blocks = call(
        functools.partial(attend_back_body, ctx_size),
        [
            ((span_rows, query_cols), jnp.bfloat16),
            ((model_width, query_cols), jnp.bfloat16),
            (block, jnp.float32),
        ]
        + [(block, jnp.bfloat16)] * (ctx_size - 1),
        [
            core_index,
            branch_mine,
            swap(branch_mine, "wt", 1),
            query,
            query_positions,
            key_positions,
            w_out,
            attn_heads,
            log_sums,
            cosines,
            signed_sines,
            *keys_values,
        ],
        [pltpu.VMEM((span_rows, model_width), jnp.bfloat16)],
        "attend_back",
        [scalar] + [whole] * (10 + ctx_size),
    )
    g_blocks, down_back = together(g_blocks, down_back)
    g_key_value_parts, gate_up_got, mlp_pieces = together(
        exchange_ctx(g_blocks), gate_up_got, mlp_pieces
    )

    mlp_parts = exchange_ctx(narrow_others(mlp_pieces))
    on_x, on_y = relay(g_gate_up, *gate_up_got)
    last_x, last_y, g_out = together(swap(on_x, "seq", 1), swap(on_y, "seq", 2), g_out)
    out_got = scatter_near(g_out)
    gate_up_sum = scatter_end(g_gate_up, *gate_up_got, last_x, last_y).astype(jnp.bfloat16)
    gate_up_blocks = gate_up_sum.reshape(ctx_size, -1, 2 * width)
    g_lin, g_bias, grad_gain_attn, normed_mine_grad, normed_send_grad = call(
        functools.partial(project_back_body, ctx_size),
        [
            ((span_rows, qkv_cols), jnp.bfloat16),
            ((1, qkv_cols), jnp.float32),
            row_f32,
            half_f32,
            half_f32,
        ],
        [
            core_index,
            query_lin,
            w_qkv,
            cosines,
            signed_sines,
            input_rows,
            rms_attn,
            *g_key_value_parts,
        ],
        [pltpu.VMEM((span_rows, model_width), jnp.float32)],
        "project_back",
        [scalar] + [whole] * (6 + ctx_size),
    )
    (g_qkv,) = call(
        product_body,
        [((model_width, qkv_cols), jnp.bfloat16)],
        [normed_attn, g_lin],
        name="qkv_grads",
    )
    small = jnp.concatenate(
        [
            relative(grad_gain_attn)[0],
            relative(grad_gain_mlp)[0],
            g_bias[0],
        ]
    ).astype(jnp.bfloat16)
    small_size = small.shape[0]
    small_rows = -(-small_size // (qkv_cols * 16)) * 16
    small = jnp.pad(small, (0, small_rows * qkv_cols - small_size)).reshape(small_rows, qkv_cols)

    mlp_parts, gate_up_blocks, out_got, g_qkv, small = together(
        mlp_parts, gate_up_blocks, out_got, g_qkv, small
    )

    gate_up_back = lax.all_to_all(gate_up_blocks, "ctx", 0, 0, tiled=True)
    _, for_x, for_y, for_far = jnp.split(g_qkv, 4, 0)
    rows = for_x.shape[0]
    half = rows // 2
    got_x = swap(jnp.concatenate([for_far[half:], for_x[half:], small], 0), "seq", 1)
    got_y = swap(jnp.concatenate([for_far[:half], for_y[:half]], 0), "seq", 2)
    attn_got = tuple(jnp.concatenate(pair, 1) for pair in zip((got_x[:rows], got_y), out_got))
    small = add_up([small, got_x[rows:]]).astype(jnp.bfloat16)
    g_attn = jnp.concatenate([g_qkv, g_out], 1)
    on_x, on_y = relay(g_attn, *attn_got)
    last_x = swap(on_x, "seq", 1)
    last_y = swap(with_rows(on_y, small), "seq", 2)
    small = add_up([small, last_y[half:, :qkv_cols]]).astype(jnp.bfloat16)
    attn_sum = scatter_end(g_attn, *attn_got, last_x, last_y[:half])
    attn_pieces = row_pieces(attn_sum)
    rows, attn_cols = attn_pieces[0].shape
    small_cols = -(-small_size // (rows * LANES)) * LANES
    small = jnp.pad(small.reshape(-1)[:small_size], (0, rows * small_cols - small_size))
    small = small.reshape(rows, small_cols)
    attn_send = [
        jnp.concatenate([piece.astype(jnp.bfloat16), small], 1) for piece in attn_pieces
    ]
    attn_send, gate_up_back, down_back, normed_send_grad, mlp_parts = together(
        attn_send, gate_up_back, down_back, normed_send_grad, mlp_parts
    )

    attn_back = exchange_ctx(attn_send)
    _, grad_input_half = call(
        functools.partial(norm_back_body, 2),
        [row_f32, half_bf16],
        [
            g_hidden,
            input_half,
            own_half(rms_attn),
            gain_one,
            normed_mine_grad,
            swap(normed_send_grad, "wt", 1),
        ],
        name="attn_norm_back",
    )
    grad_input_half = relative(grad_input_half)

    grad_input = join_halves(grad_input_half)
    layer_output = join_halves(relative((hidden + add_up(mlp_parts)).astype(jnp.bfloat16)))
    attn_back, grad_input, layer_output = together(attn_back, grad_input, layer_output)
    attn_back = attn_pieces[:1] + attn_back[1:]
    grad_w_gate, grad_w_up = (
        jnp.concatenate([block[:, start : start + width] for block in gate_up_back], 1)[
            :, :units_here
        ].astype(jnp.float32)
        for start in (0, width)
    )
    grad_w_down = jnp.concatenate(list(down_back), 1)[:, :units_here].astype(jnp.float32)
    grad_w_attn = add_up([part[:, :attn_cols] for part in attn_back])
    grad_w_qkv = grad_w_attn[:, :qkv_cols]
    grad_w_o = grad_w_attn[:, qkv_cols:]
    small = add_tree(
        [small.astype(jnp.float32)]
        + [part[:, attn_cols:].astype(jnp.float32) for part in attn_back[1:]]
    ).reshape(-1)
    gains = small[: 2 * model_width].reshape(-1, LANES)
    gains = (gains + swap(gains, "wt", 1)).reshape(-1)
    grad_bias = small[2 * model_width : small_size]
    return (
        layer_output[None],
        grad_input[None],
        gains[:model_width],
        grad_w_qkv[:, :query_cols],
        grad_bias[:query_cols],
        grad_w_qkv[:, query_cols : query_cols + key_cols],
        grad_bias[query_cols : query_cols + key_cols],
        grad_w_qkv[:, query_cols + key_cols :],
        grad_bias[query_cols + key_cols :],
        grad_w_o,
        gains[model_width:],
        grad_w_gate,
        grad_w_up,
        grad_w_down,
    )


def solution(mesh):
    tokens = P("seq", "ctx", None)
    weight = P(("seq", "ctx"), "wt")
    return jax.shard_map(
        on_device,
        mesh=mesh,
        in_specs=(
            tokens,
            P("seq", None),
            P(),
            weight,
            P("wt"),
            weight,
            P("wt"),
            weight,
            P("wt"),
            weight,
            P(),
            weight,
            weight,
            weight,
            tokens,
        ),
        out_specs=(
            tokens,
            tokens,
            P(),
            weight,
            P("wt"),
            weight,
            P("wt"),
            weight,
            P("wt"),
            weight,
            P(),
            weight,
            weight,
            weight,
        ),
        check_vma=False,
    )
```

```python
import functools
import math

import jax
import jax.numpy as jnp
from jax import lax
from jax.experimental import pallas as pl
from jax.experimental.pallas import tpu as pltpu
from jax.sharding import PartitionSpec as P

HD = 128
LANES = 128


EPSILON = 1e-06
THETA_BASE = 1000000.0
NEGATIVE = -1e30


def rope_tables(positions):
    freqs = THETA_BASE ** (-(jnp.arange(HD // 2, dtype=jnp.float32) * 2.0) / HD)
    angles = positions.astype(jnp.float32)[:, None] * freqs[None, :]
    cosines = jnp.cos(angles)
    sines = jnp.sin(angles)
    return (jnp.concatenate([cosines, cosines], -1), jnp.concatenate([sines, sines], -1))


def matmul(left, right):
    return jnp.dot(left, right, preferred_element_type=jnp.float32)


def times_transposed(left, right):
    return lax.dot_general(
        left, right, (((1,), (1,)), ((), ())), preferred_element_type=jnp.float32
    )


def inner_rows(left, right):
    return lax.dot_general(
        left, right, (((0,), (0,)), ((), ())), preferred_element_type=jnp.float32
    )


def swap(values, axis, offset):
    size = lax.axis_size(axis)
    return lax.ppermute(values, axis, [(i, i ^ offset) for i in range(size)])


def rows_at(values, index, count):
    return lax.dynamic_slice_in_dim(values, index * count, count, 0)


def place_rows(parts, indices):
    rows = len(parts) * parts[0].shape[0]
    whole = jnp.zeros((rows,) + parts[0].shape[1:], parts[0].dtype)
    for part, index in zip(parts, indices):
        whole = lax.dynamic_update_slice_in_dim(whole, part, index * part.shape[0], 0)
    return whole


def together(*values):
    return lax.optimization_barrier(values)


def relative(values):
    me = lax.axis_index("seq")
    width = values.shape[-1] // 4
    blocks = [
        lax.dynamic_slice_in_dim(values, (me ^ j) * width, width, values.ndim - 1)
        for j in range(4)
    ]
    return jnp.concatenate(blocks, -1)


def gather_ctx(block):
    size = lax.axis_size("ctx")
    return [block] + [swap(block, "ctx", k) for k in range(1, size)]


def exchange_ctx(pieces):
    return [pieces[0]] + [swap(pieces[k], "ctx", k) for k in range(1, len(pieces))]


def near_seq(shard):
    return swap(shard, "seq", 1), swap(shard, "seq", 2)


def far_seq(from_x, from_y):
    half = from_x.shape[0] // 2
    return swap(from_y[:half], "seq", 1), swap(from_x[half:], "seq", 2)


def near_payload(partial_sum):
    _, for_x, for_y, for_far = jnp.split(partial_sum, 4, 0)
    half = for_x.shape[0] // 2
    return (
        jnp.concatenate([for_far[half:], for_x[half:]], 0),
        jnp.concatenate([for_far[:half], for_y[:half]], 0),
    )


def near_swap(payload):
    return swap(payload[0], "seq", 1), swap(payload[1], "seq", 2)


def scatter_near(partial_sum):
    return near_swap(near_payload(partial_sum))


def relay(partial_sum, got_x, got_y):
    _, for_x, for_y, _ = jnp.split(partial_sum, 4, 0)
    half = for_x.shape[0] // 2
    on_x = add_up([for_x[:half], got_y[:half]]).astype(jnp.bfloat16)
    on_y = add_up([for_y[half:], got_x[:half]]).astype(jnp.bfloat16)
    return together(on_x, on_y)


def scatter_end(partial_sum, got_x, got_y, last_x, last_y):
    own = partial_sum[: partial_sum.shape[0] // 4]
    half = own.shape[0] // 2
    top = add_up([own[:half], got_y[half:], last_x])
    bottom = add_up([own[half:], got_x[half:], last_y])
    return jnp.concatenate([top, bottom], 0)


def scatter_far(partial_sum, got_x, got_y):
    on_x, on_y = relay(partial_sum, got_x, got_y)
    return scatter_end(
        partial_sum, got_x, got_y, swap(on_x, "seq", 1), swap(on_y, "seq", 2)
    )


def add_up(parts):
    total = parts[0].astype(jnp.float32)
    for part in parts[1:]:
        total = total + part.astype(jnp.float32)
    return total


def units_per(units):
    size = lax.axis_size("ctx")
    return -(-units // (size * LANES)) * LANES


def unit_pieces(shards):
    size = lax.axis_size("ctx")
    ctx = lax.axis_index("ctx")
    width = units_per(shards[0].shape[1])
    padded = [jnp.pad(w, ((0, 0), (0, size * width - w.shape[1]))) for w in shards]
    return [
        jnp.concatenate(
            [lax.dynamic_slice_in_dim(w, (ctx ^ k) * width, width, 1) for w in padded], 1
        )
        for k in range(size)
    ]


def row_pieces(summed):
    size = lax.axis_size("ctx")
    ctx = lax.axis_index("ctx")
    rows = summed.shape[0] // size
    return [rows_at(summed, ctx ^ k, rows) for k in range(size)]


def place_units(parts, units):
    size = lax.axis_size("ctx")
    ctx = lax.axis_index("ctx")
    width = units_per(units)
    wholes = []
    for start in range(0, parts[0].shape[1], width):
        whole = jnp.zeros((parts[0].shape[0], size * width), jnp.float32)
        for k in range(size):
            part = parts[k][:, start : start + width].astype(jnp.float32)
            whole = lax.dynamic_update_slice_in_dim(whole, part, (ctx ^ k) * width, 1)
        wholes.append(whole[:, :units])
    return wholes


def narrow_others(pieces):
    return [pieces[0]] + [piece.astype(jnp.bfloat16) for piece in pieces[1:]]


VMEM_BYTES = 56 * 1024 * 1024
ALONE = ("mlp_norm_back", "attend_back", "project_back",)
LITTLE = pl.CostEstimate(flops=1, bytes_accessed=1, transcendentals=0)


def stack_copies(targets, sems, used=0):
    copies = []
    for target, parts in targets:
        row, cols = 0, target.shape[1]
        group = []
        for part, column in parts:
            group.append(
                pltpu.make_async_copy(
                    part.at[:, pl.ds(column, cols)],
                    target.at[pl.ds(row, part.shape[0])],
                    sems.at[used + sum(map(len, copies)) + len(group)],
                )
            )
            row += part.shape[0]
        copies.append(group)
    return copies


def start_all(groups):
    for group in groups:
        for copy in group:
            copy.start()


def wait_all(groups):
    for group in groups:
        for copy in group:
            copy.wait()


def gate_up_copies(refs, gu, sems):
    up, gate_down, far = refs[:3], refs[3:6], refs[6:8]
    width = gu.shape[1] // 2
    return [
        (gu.at[:, pl.ds(0, width)], [(p, 0) for p in gate_down] + [(p, width) for p in far]),
        (gu.at[:, pl.ds(width, width)], [(p, 0) for p in up] + [(p, 0) for p in far]),
    ]


def forward_tile(tiles_each, x_mine, x_other, *refs):
    parts, (gate_up, gu, sems) = refs[:8], refs[8:]
    step = pl.program_id(0)

    @pl.when(step == 0)
    def _():
        copies = stack_copies(gate_up_copies(parts, gu, sems), sems)
        start_all(copies)
        wait_all(copies)

    rows = jnp.where(step < tiles_each, x_mine[...], x_other[...])
    gate_up[...] = matmul(rows, gu[...])


def backward_tile(tiles_each, gate_up, o_mine, o_other, *refs):
    parts, refs = refs[:8], refs[8:]
    both_ref, act_ref, back_mine, back_send, out_mine, out_send, gu, down, sems = refs
    step = pl.program_id(0)
    own = step < tiles_each
    width = down.shape[1]

    down_target = [(down, [(p, width) for p in parts[3:6]] + [(p, 2 * width) for p in parts[6:]])]

    @pl.when(step == 0)
    def _():
        first = stack_copies(down_target, sems)
        start_all(first)
        start_all(stack_copies(gate_up_copies(parts, gu, sems), sems, 5))
        wait_all(first)

    grads = jnp.where(own, o_mine[...], o_other[...])
    g_act = matmul(grads, down[...])
    gate, up = gate_up[:, :width], gate_up[:, width:]
    sigmoid_gate = 1.0 / (1.0 + jnp.exp(-gate))
    silu_gate = gate * sigmoid_gate
    act_ref[...] = (silu_gate * up).astype(jnp.bfloat16)
    both_ref[:, :width] = (
        g_act * up * sigmoid_gate * (1.0 + gate * (1.0 - sigmoid_gate))
    ).astype(jnp.bfloat16)
    both_ref[:, width:] = (g_act * silu_gate).astype(jnp.bfloat16)

    @pl.when(step == 0)
    def _():
        wait_all(stack_copies(gate_up_copies(parts, gu, sems), sems, 5))

    back = times_transposed(both_ref[...], gu[...])
    out = times_transposed(act_ref[...], down[...])

    @pl.when(own)
    def _():
        back_mine[...] = back
        out_mine[...] = out

    @pl.when(jnp.logical_not(own))
    def _():
        back_send[...] = back.astype(jnp.bfloat16)
        out_send[...] = out.astype(jnp.bfloat16)


def by_tiles(body, count, ins, halves, parts, outs, half_outs, scratch, name, grant):
    tile = min(256, count)
    tiles_each = count // tile

    def rows(cols):
        return pl.BlockSpec((tile, cols), lambda i: (i, 0))

    def mine(cols):
        return pl.BlockSpec((tile, cols), lambda i: (jnp.minimum(i, tiles_each - 1), 0))

    def other(cols):
        return pl.BlockSpec((tile, cols), lambda i: (jnp.maximum(i - tiles_each, 0), 0))

    return pl.pallas_call(
        functools.partial(body, tiles_each),
        grid=(2 * tiles_each,),
        in_specs=[rows(x.shape[1]) for x in ins]
        + [spec(x.shape[1]) for pair in halves for spec, x in zip((mine, other), pair)]
        + [pl.BlockSpec(memory_space=pl.ANY)] * len(parts),
        out_specs=[rows(cols) for cols, _ in outs]
        + [spec(cols) for cols in half_outs for spec in (mine, other)],
        out_shape=[jax.ShapeDtypeStruct((2 * count, cols), dtype) for cols, dtype in outs]
        + [
            jax.ShapeDtypeStruct((count, cols), dtype)
            for cols in half_outs
            for dtype in (jnp.float32, jnp.bfloat16)
        ],
        scratch_shapes=[pltpu.VMEM(shape, jnp.bfloat16) for shape in scratch]
        + [pltpu.SemaphoreType.DMA((15,))],
        compiler_params=pltpu.CompilerParams(vmem_limit_bytes=grant * 1024 * 1024),
        cost_estimate=LITTLE,
        name=name,
    )(*ins, *(x for pair in halves for x in pair), *parts)


def weight_tile(x_mine, x_other, grads, out):
    count = x_mine.shape[0]
    out[...] = (
        inner_rows(x_mine[...], grads[:count]) + inner_rows(x_other[...], grads[count:])
    ).astype(jnp.bfloat16)


def weight_grad(x_mine, x_other, grads):
    count, model_width = x_mine.shape
    tile = model_width // 4
    columns = pl.BlockSpec((count, tile), lambda i: (0, i))
    return pl.pallas_call(
        weight_tile,
        grid=(4,),
        in_specs=[columns, columns, pl.BlockSpec(grads.shape, lambda i: (0, 0))],
        out_specs=pl.BlockSpec((tile, grads.shape[1]), lambda i: (i, 0)),
        out_shape=jax.ShapeDtypeStruct((model_width, grads.shape[1]), jnp.bfloat16),
        compiler_params=pltpu.CompilerParams(vmem_limit_bytes=24 * 1024 * 1024),
        cost_estimate=LITTLE,
        name="weight_grad",
    )(x_mine, x_other, grads)


def call(body, outs, args, scratch=(), name=None, in_specs=None, rows_keys=0):
    whole = pl.BlockSpec(memory_space=pltpu.VMEM)
    held = sum(x.size * x.dtype.itemsize for x in args)
    held += sum(math.prod(shape) * jnp.dtype(dtype).itemsize for shape, dtype in outs)
    grant = min(VMEM_BYTES, 2 * held + 48 * rows_keys + 8 * 1024 * 1024)
    if name in ALONE:
        grant = VMEM_BYTES
    return pl.pallas_call(
        body,
        in_specs=in_specs or [whole] * len(args),
        out_specs=[whole] * len(outs),
        out_shape=[jax.ShapeDtypeStruct(shape, dtype) for shape, dtype in outs],
        scratch_shapes=list(scratch),
        compiler_params=pltpu.CompilerParams(vmem_limit_bytes=grant),
        cost_estimate=LITTLE,
        name=name,
    )(*args)


def beside_body(*refs):
    *parts, out = refs
    start = 0
    for part in parts:
        out[:, start : start + part.shape[1]] = part[...]
        start += part.shape[1]


def side_by_side(parts):
    cols = sum(part.shape[1] for part in parts)
    return call(
        beside_body, [((parts[0].shape[0], cols), parts[0].dtype)], parts, name="side_by_side"
    )[0]


def place_body(groups, ctx_ref, *refs):
    *parts, out, sems = refs
    count = len(parts) // groups
    rows = parts[0].shape[0]
    start = 0
    copies = []
    for group in range(groups):
        cols = parts[group * count].shape[1]
        for k in range(count):
            here = pl.ds(pl.multiple_of((ctx_ref[0] ^ k) * rows, rows), rows)
            copies.append(
                pltpu.make_async_copy(
                    parts[group * count + k],
                    out.at[here, pl.ds(start, cols)],
                    sems.at[len(copies)],
                )
            )
        start += cols
    for copy in copies:
        copy.start()
    for copy in copies:
        copy.wait()


def place_ctx(*groups):
    ctx = lax.axis_index("ctx")
    count, rows = len(groups[0]), groups[0][0].shape[0]
    if rows % 16:
        order = [ctx ^ k for k in range(count)]
        return jnp.concatenate([place_rows(parts, order) for parts in groups], 1)
    cols = sum(parts[0].shape[1] for parts in groups)
    parts = [part for group in groups for part in group]
    return call(
        functools.partial(place_body, len(groups)),
        [((count * rows, cols), parts[0].dtype)],
        [ctx.astype(jnp.int32).reshape(1), *parts],
        [pltpu.SemaphoreType.DMA((len(parts),))],
        "place",
        [pl.BlockSpec(memory_space=pltpu.SMEM)]
        + [pl.BlockSpec(memory_space=pl.ANY)] * len(parts),
    )[0]


def turn(values, cosines, signed_sines):
    return values * cosines + pltpu.roll(values, HD // 2, 1) * signed_sines


def turn_back(grads, cosines, signed_sines):
    return grads * cosines + pltpu.roll(grads, HD // 2, 1) * (-signed_sines)


def project_body(query_cols, key_cols, x, bias, cosines, signed_sines, *refs):
    shard, from_x, from_y, far_top, far_bottom = refs[:5]
    query, key_value, w_qkv, w_out, sems = refs[5:]
    near = shard.shape[0]
    half = near // 2
    split = w_qkv.shape[1]
    copies = []
    for part, start in (
        (shard, 0),
        (from_x, near),
        (from_y, 2 * near),
        (far_top, 3 * near),
        (far_bottom, 3 * near + half),
    ):
        rows = pl.ds(start, part.shape[0])
        left, right = part.at[:, pl.ds(0, split)], part.at[:, pl.ds(split, w_out.shape[1])]
        for source, target in ((left, w_qkv.at[rows]), (right, w_out.at[rows])):
            copies.append(pltpu.make_async_copy(source, target, sems.at[len(copies)]))
    for copy in copies:
        copy.start()
    for copy in copies[::2]:
        copy.wait()
    lin = matmul(x[...], w_qkv[...]) + bias[...]
    for start in range(0, query_cols, HD):
        query[:, start : start + HD] = turn(
            lin[:, start : start + HD], cosines[...], signed_sines[...]
        ).astype(jnp.bfloat16)
    for start in range(0, key_cols, HD):
        key_value[:, start : start + HD] = turn(
            lin[:, query_cols + start : query_cols + start + HD], cosines[...], signed_sines[...]
        ).astype(jnp.bfloat16)
    key_value[:, key_cols:] = lin[:, query_cols + key_cols :].astype(jnp.bfloat16)
    for copy in copies[1::2]:
        copy.wait()


def attend_body(count, core_ref, query, query_pos, key_pos, w_out, *refs):
    parts, (heads, log_sums, mine, send, total) = refs[:count], refs[count:]
    keys = jnp.concatenate([part[:, :HD] for part in parts], 0)
    values = jnp.concatenate([part[:, HD:] for part in parts], 0)
    visible = key_pos[...] <= query_pos[...]
    for start in range(0, query.shape[1], HD):
        scores = jnp.where(
            visible, times_transposed(query[:, start : start + HD], keys) * HD**-0.5, NEGATIVE
        )
        highest = jnp.max(scores, -1, keepdims=True)
        weights = jnp.exp(scores - highest)
        totals = jnp.sum(weights, -1, keepdims=True)
        heads[:, start : start + HD] = matmul(
            (weights * (1.0 / totals)).astype(jnp.bfloat16), values
        ).astype(jnp.bfloat16)
        log_sums[:, start : start + HD] = jnp.broadcast_to(
            highest + jnp.log(totals), (query.shape[0], HD)
        )
    split_rows(core_ref, times_transposed(heads[...], w_out[...]), total, mine, send)


def split_rows(core_ref, values, total, mine, send):
    half = mine.shape[0]
    core = core_ref[0]
    total[...] = values
    mine[...] = total[pl.ds(pl.multiple_of(core * half, half), half)]
    send[...] = total[pl.ds(pl.multiple_of((1 - core) * half, half), half)]


def norm_body(mine, got, inputs, gain, hidden, inverse_rms, normed):
    values = inputs[...] + mine[...] + got[...]
    hidden[...] = values
    inverse = lax.rsqrt(jnp.mean(values * values, -1, keepdims=True) + EPSILON)
    inverse_rms[...] = inverse
    normed[...] = (values * inverse * gain[...]).astype(jnp.bfloat16)


def norm_back_body(count, base, inputs, inverse_rms, gain, *refs):
    parts, outs = refs[:count], refs[count:]
    grads = parts[0][...].astype(jnp.float32)
    for part in parts[1:]:
        grads = grads + part[...].astype(jnp.float32)
    inverse = inverse_rms[...]
    values = inputs[...]
    weighted = grads * gain[...]
    back = inverse * weighted - values * (inverse * inverse * inverse) * jnp.mean(
        weighted * values, -1, keepdims=True
    )
    result = base[...].astype(jnp.float32) + back
    outs[0][...] = jnp.sum(grads * values * inverse, 0, keepdims=True)
    outs[1][...] = result.astype(jnp.bfloat16)
    if len(outs) > 2:
        outs[2][...] = result


def attend_back_body(
    count,
    core_ref,
    branch_mine,
    branch_other,
    query,
    query_pos,
    key_pos,
    w_out,
    heads,
    log_sums,
    cosines,
    signed_sines,
    *refs,
):
    parts, (query_lin, g_out), g_parts = refs[:count], refs[count : count + 2], refs[count + 2 : -1]
    branch = refs[-1]
    half = branch_mine.shape[0]
    core = core_ref[0]
    branch[pl.ds(pl.multiple_of(core * half, half), half)] = branch_mine[...]
    branch[pl.ds(pl.multiple_of((1 - core) * half, half), half)] = branch_other[...]
    keys = jnp.concatenate([part[:, :HD] for part in parts], 0)
    values = jnp.concatenate([part[:, HD:] for part in parts], 0)
    visible = key_pos[...] <= query_pos[...]
    g_heads = matmul(branch[...], w_out[...]).astype(jnp.bfloat16)
    scale = HD**-0.5
    g_keys = jnp.zeros(keys.shape, jnp.float32)
    g_values = jnp.zeros(values.shape, jnp.float32)
    for start in range(0, query.shape[1], HD):
        head = query[:, start : start + HD]
        g_head = g_heads[:, start : start + HD]
        scores = jnp.where(visible, times_transposed(head, keys) * scale, NEGATIVE)
        probs = jnp.exp(scores - log_sums[:, start : start + 1])
        g_probs = times_transposed(g_head, values)
        delta = jnp.sum(probs * g_probs, -1, keepdims=True)
        g_scores = (probs * (g_probs - delta)).astype(jnp.bfloat16)
        query_lin[:, start : start + HD] = turn_back(
            matmul(g_scores, keys) * scale, cosines[...], signed_sines[...]
        ).astype(jnp.bfloat16)
        g_keys = g_keys + inner_rows(g_scores, head)
        g_values = g_values + inner_rows(probs.astype(jnp.bfloat16), g_head)
    g_keys = g_keys * scale
    g_out[...] = inner_rows(branch[...], heads[...]).astype(jnp.bfloat16)
    rows = parts[0].shape[0]
    for k, out in enumerate(g_parts):
        out[:, :HD] = g_keys[k * rows : (k + 1) * rows].astype(out.dtype)
        out[:, HD:] = g_values[k * rows : (k + 1) * rows].astype(out.dtype)


def product_body(left, right, out):
    out[...] = inner_rows(left[...], right[...]).astype(jnp.bfloat16)


def project_back_body(
    count, core_ref, query_lin, w_qkv, cosines, signed_sines, inputs, inverse_rms, *refs
):
    parts, (lin, g_bias, g_gain, mine, send, total) = refs[:count], refs[count:]
    g_parts = parts[0][...].astype(jnp.float32)
    for part in parts[1:]:
        g_parts = g_parts + part[...].astype(jnp.float32)
    cols = query_lin.shape[1]
    lin[:, :cols] = query_lin[...]
    lin[:, cols : cols + HD] = turn_back(
        g_parts[:, :HD], cosines[...], signed_sines[...]
    ).astype(jnp.bfloat16)
    lin[:, cols + HD :] = g_parts[:, HD:].astype(jnp.bfloat16)
    split_rows(core_ref, times_transposed(lin[...], w_qkv[...]), total, mine, send)
    g_gain[...] = jnp.sum(total[...] * inputs[...] * inverse_rms[...], 0, keepdims=True)
    g_bias[...] = jnp.sum(lin[...].astype(jnp.float32), 0, keepdims=True)


def chip_sum(own, got):
    total = (own + got.astype(jnp.float32)).astype(jnp.bfloat16)
    return jnp.split(total, lax.axis_size("ctx"), 0)


def add_tree(parts):
    while len(parts) > 1:
        parts = [parts[i] + parts[i + 1] for i in range(0, len(parts), 2)]
    return parts[0]


def with_rows(block, rows):
    return jnp.concatenate([block, jnp.pad(rows, ((0, 0), (0, block.shape[1] - rows.shape[1])))], 0)


def on_device(
    layer_input,
    pairs,
    gain_attn,
    w_q,
    b_q,
    w_k,
    b_k,
    w_v,
    b_v,
    w_o,
    gain_mlp,
    w_gate,
    w_up,
    w_down,
    out_grad,
):
    _, span_rows, model_width = layer_input.shape
    half_rows = span_rows // 2
    query_cols = w_q.shape[1]
    key_cols = w_k.shape[1]
    units_here = w_gate.shape[1]
    ctx_size = lax.axis_size("ctx")
    ctx = lax.axis_index("ctx")
    core = lax.axis_index("wt")

    def own_half(values):
        return rows_at(values, core, half_rows)

    def join_halves(mine):
        other = swap(mine, "wt", 1)
        return jnp.where(
            core == 0, jnp.concatenate([mine, other], 0), jnp.concatenate([other, mine], 0)
        )

    within = jnp.arange(half_rows, dtype=jnp.int32)

    def positions_at(index):
        early = lax.dynamic_index_in_dim(pairs[0], index, 0, False)
        return jnp.concatenate(
            [early * half_rows + within, (2 * ctx_size - 1 - early) * half_rows + within]
        )

    query_positions = positions_at(ctx)
    key_positions = jnp.concatenate([positions_at(ctx ^ k) for k in range(ctx_size)])[None]
    cosines, sines = rope_tables(query_positions)
    signed_sines = jnp.concatenate([-sines[:, : HD // 2], sines[:, HD // 2 :]], 1)
    query_positions = query_positions[:, None]
    core_index = core.astype(jnp.int32).reshape(1)
    scalar = pl.BlockSpec(memory_space=pltpu.SMEM)
    whole = pl.BlockSpec(memory_space=pltpu.VMEM)
    left = pl.BlockSpec(memory_space=pl.ANY)

    input_rows = relative(layer_input.reshape(span_rows, model_width)).astype(jnp.float32)
    grad_out = relative(out_grad.reshape(span_rows, model_width))
    gain_one = relative(gain_attn.astype(jnp.float32))[None]
    gain_two = relative(gain_mlp.astype(jnp.float32))[None]

    rms_attn = lax.rsqrt(jnp.mean(input_rows * input_rows, -1, keepdims=True) + EPSILON)
    normed_attn = (input_rows * rms_attn * gain_one).astype(jnp.bfloat16)
    qkv_cols = query_cols + 2 * key_cols
    bias = jnp.concatenate([b_q, b_k, b_v]).astype(jnp.float32)[None]
    input_half = own_half(input_rows)
    attn_parts = gather_ctx(side_by_side([w_q, w_k, w_v, w_o]))
    gate_up_pieces = unit_pieces([w_gate, w_up])
    down_pieces = unit_pieces([w_down])
    grad_half = own_half(grad_out)
    attn_shard = place_ctx(attn_parts)
    attn_shard, gate_up_pieces, down_pieces, tables = together(
        attn_shard,
        gate_up_pieces,
        down_pieces,
        (
            normed_attn,
            bias,
            cosines,
            signed_sines,
            query_positions,
            key_positions,
            input_half,
            grad_half,
            gain_two,
        ),
    )
    normed_attn, bias, cosines, signed_sines, query_positions, key_positions = tables[:6]
    input_half, grad_half, gain_two = tables[6:]

    attn_near = near_seq(attn_shard)
    gate_up_parts = exchange_ctx(gate_up_pieces)
    attn_near, gate_up_parts, down_pieces = together(attn_near, gate_up_parts, down_pieces)
    attn_far = far_seq(*attn_near)
    down_parts = exchange_ctx(down_pieces)
    width = units_per(units_here)
    up_shard = place_ctx([part[:, width:] for part in gate_up_parts])
    attn_far, up_shard = together(attn_far, up_shard)
    up_near = near_seq(up_shard)

    query, key_value, w_qkv, w_out = call(
        functools.partial(project_body, query_cols, key_cols),
        [
            ((span_rows, query_cols), jnp.bfloat16),
            ((span_rows, 2 * key_cols), jnp.bfloat16),
            ((model_width, qkv_cols), jnp.bfloat16),
            ((model_width, query_cols), jnp.bfloat16),
        ],
        [normed_attn, bias, cosines, signed_sines, attn_shard, *attn_near, *attn_far],
        [pltpu.SemaphoreType.DMA((10,))],
        "project",
        [whole] * 4 + [left] * 5,
    )
    key_value, down_parts = together(key_value, down_parts)

    gate_down_shard = place_ctx([part[:, :width] for part in gate_up_parts], down_parts)
    keys_values, gate_down_shard = together(gather_ctx(key_value), gate_down_shard)
    half_f32 = ((half_rows, model_width), jnp.float32)
    half_bf16 = ((half_rows, model_width), jnp.bfloat16)
    row_f32 = ((1, model_width), jnp.float32)
    attn_heads, log_sums, attn_mine, attn_send = call(
        functools.partial(attend_body, ctx_size),
        [
            ((span_rows, query_cols), jnp.bfloat16),
            ((span_rows, query_cols), jnp.float32),
            half_f32,
            half_f32,
        ],
        [core_index, query, query_positions, key_positions, w_out, *keys_values],
        [pltpu.VMEM((span_rows, model_width), jnp.float32)],
        "attend",
        [scalar] + [whole] * (4 + ctx_size),
        span_rows * key_positions.size,
    )
    hidden, rms_mlp, normed_half = call(
        norm_body,
        [half_f32, ((half_rows, 1), jnp.float32), half_bf16],
        [attn_mine, swap(attn_send, "wt", 1), input_half, gain_two],
        name="norm",
    )
    normed_half, gate_down_shard, up_near = together(normed_half, gate_down_shard, up_near)

    gate_down_near = near_seq(gate_down_shard)
    normed_parts, gate_down_near, grad_half = together(
        gather_ctx(normed_half), gate_down_near, grad_half
    )

    mlp_far = far_seq(*(jnp.concatenate(pair, 1) for pair in zip(up_near, gate_down_near)))
    normed_mine = jnp.concatenate(normed_parts, 0)
    normed_other, grad_half = together(swap(normed_mine, "wt", 1), grad_half)
    count = normed_mine.shape[0]
    mlp_parts = [up_shard, *up_near, gate_down_shard, *gate_down_near, *mlp_far]
    (gate_up,) = by_tiles(
        forward_tile,
        count,
        [],
        [(normed_mine, normed_other)],
        mlp_parts,
        [(2 * width, jnp.float32)],
        [],
        [(model_width, 2 * width)],
        "gate_up",
        26,
    )
    grad_parts, gate_up = together(gather_ctx(grad_half), gate_up)
    grad_mine = jnp.concatenate(grad_parts, 0)
    grad_other = swap(grad_mine, "wt", 1)
    g_both, act, back_mine, back_send, out_mine, out_send = by_tiles(
        backward_tile,
        count,
        [gate_up],
        [(grad_mine, grad_other)],
        mlp_parts,
        [(2 * width, jnp.bfloat16), (width, jnp.bfloat16)],
        [model_width, model_width],
        [(model_width, 2 * width), (model_width, width)],
        "mlp_back",
        42,
    )
    back_got = swap(back_send, "wt", 1)
    out_got = swap(out_send, "wt", 1)
    g_down = weight_grad(grad_mine, grad_other, act)
    g_normed_pieces = chip_sum(back_mine, back_got)
    g_normed_pieces, g_down, out_got, g_both = together(
        g_normed_pieces, g_down, out_got, g_both
    )

    g_normed_parts = exchange_ctx(g_normed_pieces)
    down_got = scatter_near(g_down)
    g_gate_up = weight_grad(normed_mine, normed_other, g_both)
    down_got, g_gate_up = together(down_got, g_gate_up)
    gate_up_payload = near_payload(g_gate_up)
    mlp_pieces = chip_sum(out_mine, out_got)
    down_sum = scatter_far(g_down, *down_got).astype(jnp.bfloat16)
    g_normed_parts, down_sum, gate_up_payload, mlp_pieces = together(
        g_normed_parts, down_sum, gate_up_payload, mlp_pieces
    )

    down_back = lax.all_to_all(
        down_sum.reshape(ctx_size, -1, down_sum.shape[1]), "ctx", 0, 0, tiled=True
    )
    gate_up_got = near_swap(gate_up_payload)
    grad_gain_mlp, branch_mine, g_hidden = call(
        functools.partial(norm_back_body, ctx_size),
        [row_f32, half_bf16, half_f32],
        [grad_half, hidden, rms_mlp, gain_two, *g_normed_parts],
        name="mlp_norm_back",
    )
    block = (span_rows, 2 * key_cols)
    query_lin, g_out, *g_blocks = call(
        functools.partial(attend_back_body, ctx_size),
        [
            ((span_rows, query_cols), jnp.bfloat16),
            ((model_width, query_cols), jnp.bfloat16),
            (block, jnp.float32),
        ]
        + [(block, jnp.bfloat16)] * (ctx_size - 1),
        [
            core_index,
            branch_mine,
            swap(branch_mine, "wt", 1),
            query,
            query_positions,
            key_positions,
            w_out,
            attn_heads,
            log_sums,
            cosines,
            signed_sines,
            *keys_values,
        ],
        [pltpu.VMEM((span_rows, model_width), jnp.bfloat16)],
        "attend_back",
        [scalar] + [whole] * (10 + ctx_size),
        span_rows * key_positions.size,
    )
    g_blocks, down_back = together(g_blocks, down_back)
    g_key_value_parts, gate_up_got, mlp_pieces = together(
        exchange_ctx(g_blocks), gate_up_got, mlp_pieces
    )

    mlp_parts = exchange_ctx(mlp_pieces)
    on_x, on_y = relay(g_gate_up, *gate_up_got)
    last_x, last_y, g_out = together(swap(on_x, "seq", 1), swap(on_y, "seq", 2), g_out)
    out_got = scatter_near(g_out)
    gate_up_sum = scatter_end(g_gate_up, *gate_up_got, last_x, last_y).astype(jnp.bfloat16)
    gate_up_blocks = gate_up_sum.reshape(ctx_size, -1, 2 * width)
    g_lin, g_bias, grad_gain_attn, normed_mine_grad, normed_send_grad = call(
        functools.partial(project_back_body, ctx_size),
        [
            ((span_rows, qkv_cols), jnp.bfloat16),
            ((1, qkv_cols), jnp.float32),
            row_f32,
            half_f32,
            half_f32,
        ],
        [
            core_index,
            query_lin,
            w_qkv,
            cosines,
            signed_sines,
            input_rows,
            rms_attn,
            *g_key_value_parts,
        ],
        [pltpu.VMEM((span_rows, model_width), jnp.float32)],
        "project_back",
        [scalar] + [whole] * (6 + ctx_size),
    )
    (g_qkv,) = call(
        product_body,
        [((model_width, qkv_cols), jnp.bfloat16)],
        [normed_attn, g_lin],
        name="qkv_grads",
    )
    small = jnp.concatenate(
        [
            relative(grad_gain_attn)[0],
            relative(grad_gain_mlp)[0],
            g_bias[0],
        ]
    ).astype(jnp.bfloat16)
    small_size = small.shape[0]
    small_rows = -(-small_size // (qkv_cols * 16)) * 16
    small = jnp.pad(small, (0, small_rows * qkv_cols - small_size)).reshape(small_rows, qkv_cols)

    mlp_parts, gate_up_blocks, out_got, g_qkv, small = together(
        mlp_parts, gate_up_blocks, out_got, g_qkv, small
    )

    gate_up_back = lax.all_to_all(gate_up_blocks, "ctx", 0, 0, tiled=True)
    _, for_x, for_y, for_far = jnp.split(g_qkv, 4, 0)
    rows = for_x.shape[0]
    half = rows // 2
    got_x = swap(jnp.concatenate([for_far[half:], for_x[half:], small], 0), "seq", 1)
    got_y = swap(jnp.concatenate([for_far[:half], for_y[:half]], 0), "seq", 2)
    attn_got = tuple(jnp.concatenate(pair, 1) for pair in zip((got_x[:rows], got_y), out_got))
    small = add_up([small, got_x[rows:]]).astype(jnp.bfloat16)
    g_attn = jnp.concatenate([g_qkv, g_out], 1)
    on_x, on_y = relay(g_attn, *attn_got)
    last_x = swap(on_x, "seq", 1)
    last_y = swap(with_rows(on_y, small), "seq", 2)
    small = add_up([small, last_y[half:, :qkv_cols]]).astype(jnp.bfloat16)
    attn_sum = scatter_end(g_attn, *attn_got, last_x, last_y[:half])
    attn_pieces = row_pieces(attn_sum)
    rows, attn_cols = attn_pieces[0].shape
    small_cols = -(-small_size // (rows * LANES)) * LANES
    small = jnp.pad(small.reshape(-1)[:small_size], (0, rows * small_cols - small_size))
    small = small.reshape(rows, small_cols)
    attn_send = [
        jnp.concatenate([piece.astype(jnp.bfloat16), small], 1) for piece in attn_pieces
    ]
    attn_send, gate_up_back, down_back, normed_send_grad, mlp_parts = together(
        attn_send, gate_up_back, down_back, normed_send_grad, mlp_parts
    )

    attn_back = exchange_ctx(attn_send)
    _, grad_input_half = call(
        functools.partial(norm_back_body, 2),
        [row_f32, half_bf16],
        [
            g_hidden,
            input_half,
            own_half(rms_attn),
            gain_one,
            normed_mine_grad,
            swap(normed_send_grad, "wt", 1),
        ],
        name="attn_norm_back",
    )
    grad_input_half = relative(grad_input_half)

    grad_input = join_halves(grad_input_half)
    layer_output = join_halves(relative((hidden + add_up(mlp_parts)).astype(jnp.bfloat16)))
    attn_back, grad_input, layer_output = together(attn_back, grad_input, layer_output)
    attn_back = attn_pieces[:1] + attn_back[1:]
    grad_w_gate, grad_w_up = (
        jnp.concatenate([block[:, start : start + width] for block in gate_up_back], 1)[
            :, :units_here
        ].astype(jnp.float32)
        for start in (0, width)
    )
    grad_w_down = jnp.concatenate(list(down_back), 1)[:, :units_here].astype(jnp.float32)
    grad_w_attn = add_up([part[:, :attn_cols] for part in attn_back])
    grad_w_qkv = grad_w_attn[:, :qkv_cols]
    grad_w_o = grad_w_attn[:, qkv_cols:]
    small = add_tree(
        [small.astype(jnp.float32)]
        + [part[:, attn_cols:].astype(jnp.float32) for part in attn_back[1:]]
    ).reshape(-1)
    gains = small[: 2 * model_width].reshape(-1, LANES)
    gains = (gains + swap(gains, "wt", 1)).reshape(-1)
    grad_bias = small[2 * model_width : small_size]
    return (
        layer_output[None],
        grad_input[None],
        gains[:model_width],
        grad_w_qkv[:, :query_cols],
        grad_bias[:query_cols],
        grad_w_qkv[:, query_cols : query_cols + key_cols],
        grad_bias[query_cols : query_cols + key_cols],
        grad_w_qkv[:, query_cols + key_cols :],
        grad_bias[query_cols + key_cols :],
        grad_w_o,
        gains[model_width:],
        grad_w_gate,
        grad_w_up,
        grad_w_down,
    )


def solution(mesh):
    tokens = P("seq", "ctx", None)
    weight = P(("seq", "ctx"), "wt")
    return jax.shard_map(
        on_device,
        mesh=mesh,
        in_specs=(
            tokens,
            P("seq", None),
            P(),
            weight,
            P("wt"),
            weight,
            P("wt"),
            weight,
            P("wt"),
            weight,
            P(),
            weight,
            weight,
            weight,
            tokens,
        ),
        out_specs=(
            tokens,
            tokens,
            P(),
            weight,
            P("wt"),
            weight,
            P("wt"),
            weight,
            P("wt"),
            weight,
            P(),
            weight,
            weight,
            weight,
        ),
        check_vma=False,
    )
```

```python
import functools
import math

import jax
import jax.numpy as jnp
from jax import lax
from jax.experimental import pallas as pl
from jax.experimental.pallas import tpu as pltpu
from jax.sharding import PartitionSpec as P

HD = 128
LANES = 128


EPSILON = 1e-06
THETA_BASE = 1000000.0
NEGATIVE = -1e30


def rope_tables(positions):
    freqs = THETA_BASE ** (-(jnp.arange(HD // 2, dtype=jnp.float32) * 2.0) / HD)
    angles = positions.astype(jnp.float32)[:, None] * freqs[None, :]
    cosines = jnp.cos(angles)
    sines = jnp.sin(angles)
    return (jnp.concatenate([cosines, cosines], -1), jnp.concatenate([sines, sines], -1))


def matmul(left, right):
    return jnp.dot(left, right, preferred_element_type=jnp.float32)


def times_transposed(left, right):
    return lax.dot_general(
        left, right, (((1,), (1,)), ((), ())), preferred_element_type=jnp.float32
    )


def inner_rows(left, right):
    return lax.dot_general(
        left, right, (((0,), (0,)), ((), ())), preferred_element_type=jnp.float32
    )


def swap(values, axis, offset):
    size = lax.axis_size(axis)
    return lax.ppermute(values, axis, [(i, i ^ offset) for i in range(size)])


def rows_at(values, index, count):
    return lax.dynamic_slice_in_dim(values, index * count, count, 0)


def place_rows(parts, indices):
    rows = len(parts) * parts[0].shape[0]
    whole = jnp.zeros((rows,) + parts[0].shape[1:], parts[0].dtype)
    for part, index in zip(parts, indices):
        whole = lax.dynamic_update_slice_in_dim(whole, part, index * part.shape[0], 0)
    return whole


def together(*values):
    return lax.optimization_barrier(values)


def relative(values):
    me = lax.axis_index("seq")
    width = values.shape[-1] // 4
    blocks = [
        lax.dynamic_slice_in_dim(values, (me ^ j) * width, width, values.ndim - 1)
        for j in range(4)
    ]
    return jnp.concatenate(blocks, -1)


def gather_ctx(block):
    size = lax.axis_size("ctx")
    return [block] + [swap(block, "ctx", k) for k in range(1, size)]


def exchange_ctx(pieces):
    return [pieces[0]] + [swap(pieces[k], "ctx", k) for k in range(1, len(pieces))]


def near_seq(shard):
    return swap(shard, "seq", 1), swap(shard, "seq", 2)


def far_seq(from_x, from_y):
    half = from_x.shape[0] // 2
    return swap(from_y[:half], "seq", 1), swap(from_x[half:], "seq", 2)


def near_payload(partial_sum):
    _, for_x, for_y, for_far = jnp.split(partial_sum, 4, 0)
    half = for_x.shape[0] // 2
    return (
        jnp.concatenate([for_far[half:], for_x[half:]], 0),
        jnp.concatenate([for_far[:half], for_y[:half]], 0),
    )


def near_swap(payload):
    return swap(payload[0], "seq", 1), swap(payload[1], "seq", 2)


def scatter_near(partial_sum):
    return near_swap(near_payload(partial_sum))


def relay(partial_sum, got_x, got_y):
    _, for_x, for_y, _ = jnp.split(partial_sum, 4, 0)
    half = for_x.shape[0] // 2
    on_x = add_up([for_x[:half], got_y[:half]]).astype(jnp.bfloat16)
    on_y = add_up([for_y[half:], got_x[:half]]).astype(jnp.bfloat16)
    return together(on_x, on_y)


def scatter_end(partial_sum, got_x, got_y, last_x, last_y):
    own = partial_sum[: partial_sum.shape[0] // 4]
    half = own.shape[0] // 2
    top = add_up([own[:half], got_y[half:], last_x])
    bottom = add_up([own[half:], got_x[half:], last_y])
    return jnp.concatenate([top, bottom], 0)


def scatter_far(partial_sum, got_x, got_y):
    on_x, on_y = relay(partial_sum, got_x, got_y)
    return scatter_end(
        partial_sum, got_x, got_y, swap(on_x, "seq", 1), swap(on_y, "seq", 2)
    )


def add_up(parts):
    total = parts[0].astype(jnp.float32)
    for part in parts[1:]:
        total = total + part.astype(jnp.float32)
    return total


def units_per(units):
    size = lax.axis_size("ctx")
    return -(-units // (size * LANES)) * LANES


def unit_pieces(shards):
    size = lax.axis_size("ctx")
    ctx = lax.axis_index("ctx")
    width = units_per(shards[0].shape[1])
    padded = [jnp.pad(w, ((0, 0), (0, size * width - w.shape[1]))) for w in shards]
    return [
        jnp.concatenate(
            [lax.dynamic_slice_in_dim(w, (ctx ^ k) * width, width, 1) for w in padded], 1
        )
        for k in range(size)
    ]


def row_pieces(summed):
    size = lax.axis_size("ctx")
    ctx = lax.axis_index("ctx")
    rows = summed.shape[0] // size
    return [rows_at(summed, ctx ^ k, rows) for k in range(size)]


def place_units(parts, units):
    size = lax.axis_size("ctx")
    ctx = lax.axis_index("ctx")
    width = units_per(units)
    wholes = []
    for start in range(0, parts[0].shape[1], width):
        whole = jnp.zeros((parts[0].shape[0], size * width), jnp.float32)
        for k in range(size):
            part = parts[k][:, start : start + width].astype(jnp.float32)
            whole = lax.dynamic_update_slice_in_dim(whole, part, (ctx ^ k) * width, 1)
        wholes.append(whole[:, :units])
    return wholes


def narrow_others(pieces):
    return [pieces[0]] + [piece.astype(jnp.bfloat16) for piece in pieces[1:]]


VMEM_BYTES = 56 * 1024 * 1024
ALONE = ("side_by_side", "mlp_norm_back", "attend_back", "project_back")
LITTLE = pl.CostEstimate(flops=1, bytes_accessed=1, transcendentals=0)


def stack_copies(targets, sems, used=0):
    copies = []
    for target, parts in targets:
        row, cols = 0, target.shape[1]
        group = []
        for part, column in parts:
            group.append(
                pltpu.make_async_copy(
                    part.at[:, pl.ds(column, cols)],
                    target.at[pl.ds(row, part.shape[0])],
                    sems.at[used + sum(map(len, copies)) + len(group)],
                )
            )
            row += part.shape[0]
        copies.append(group)
    return copies


def start_all(groups):
    for group in groups:
        for copy in group:
            copy.start()


def wait_all(groups):
    for group in groups:
        for copy in group:
            copy.wait()


def gate_up_copies(refs, gu, sems):
    up, gate_down, far = refs[:3], refs[3:6], refs[6:8]
    width = gu.shape[1] // 2
    return [
        (gu.at[:, pl.ds(0, width)], [(p, 0) for p in gate_down] + [(p, width) for p in far]),
        (gu.at[:, pl.ds(width, width)], [(p, 0) for p in up] + [(p, 0) for p in far]),
    ]


def forward_tile(tiles_each, x_mine, x_other, *refs):
    parts, (gate_up, gu, sems) = refs[:8], refs[8:]
    step = pl.program_id(0)

    @pl.when(step == 0)
    def _():
        copies = stack_copies(gate_up_copies(parts, gu, sems), sems)
        start_all(copies)
        wait_all(copies)

    rows = jnp.where(step < tiles_each, x_mine[...], x_other[...])
    gate_up[...] = matmul(rows, gu[...])


def backward_tile(tiles_each, gate_up, o_mine, o_other, *refs):
    parts, refs = refs[:8], refs[8:]
    both_ref, act_ref, back_mine, back_send, out_mine, out_send, gu, down, sems = refs
    step = pl.program_id(0)
    own = step < tiles_each
    width = down.shape[1]

    down_target = [(down, [(p, width) for p in parts[3:6]] + [(p, 2 * width) for p in parts[6:]])]

    @pl.when(step == 0)
    def _():
        first = stack_copies(down_target, sems)
        start_all(first)
        start_all(stack_copies(gate_up_copies(parts, gu, sems), sems, 5))
        wait_all(first)

    grads = jnp.where(own, o_mine[...], o_other[...])
    g_act = matmul(grads, down[...])
    gate, up = gate_up[:, :width], gate_up[:, width:]
    sigmoid_gate = 1.0 / (1.0 + jnp.exp(-gate))
    silu_gate = gate * sigmoid_gate
    act_ref[...] = (silu_gate * up).astype(jnp.bfloat16)
    both_ref[:, :width] = (
        g_act * up * sigmoid_gate * (1.0 + gate * (1.0 - sigmoid_gate))
    ).astype(jnp.bfloat16)
    both_ref[:, width:] = (g_act * silu_gate).astype(jnp.bfloat16)

    @pl.when(step == 0)
    def _():
        wait_all(stack_copies(gate_up_copies(parts, gu, sems), sems, 5))

    back = times_transposed(both_ref[...], gu[...])
    out = times_transposed(act_ref[...], down[...])

    @pl.when(own)
    def _():
        back_mine[...] = back
        out_mine[...] = out

    @pl.when(jnp.logical_not(own))
    def _():
        back_send[...] = back.astype(jnp.bfloat16)
        out_send[...] = out.astype(jnp.bfloat16)


def by_tiles(body, count, ins, halves, parts, outs, half_outs, scratch, name, grant):
    tile = min(256, count)
    tiles_each = count // tile

    def rows(cols):
        return pl.BlockSpec((tile, cols), lambda i: (i, 0))

    def mine(cols):
        return pl.BlockSpec((tile, cols), lambda i: (jnp.minimum(i, tiles_each - 1), 0))

    def other(cols):
        return pl.BlockSpec((tile, cols), lambda i: (jnp.maximum(i - tiles_each, 0), 0))

    return pl.pallas_call(
        functools.partial(body, tiles_each),
        grid=(2 * tiles_each,),
        in_specs=[rows(x.shape[1]) for x in ins]
        + [spec(x.shape[1]) for pair in halves for spec, x in zip((mine, other), pair)]
        + [pl.BlockSpec(memory_space=pl.ANY)] * len(parts),
        out_specs=[rows(cols) for cols, _ in outs]
        + [spec(cols) for cols in half_outs for spec in (mine, other)],
        out_shape=[jax.ShapeDtypeStruct((2 * count, cols), dtype) for cols, dtype in outs]
        + [
            jax.ShapeDtypeStruct((count, cols), dtype)
            for cols in half_outs
            for dtype in (jnp.float32, jnp.bfloat16)
        ],
        scratch_shapes=[pltpu.VMEM(shape, jnp.bfloat16) for shape in scratch]
        + [pltpu.SemaphoreType.DMA((15,))],
        compiler_params=pltpu.CompilerParams(vmem_limit_bytes=grant * 1024 * 1024),
        cost_estimate=LITTLE,
        name=name,
    )(*ins, *(x for pair in halves for x in pair), *parts)


def weight_tile(x_mine, x_other, grads, out):
    count = x_mine.shape[0]
    out[...] = (
        inner_rows(x_mine[...], grads[:count]) + inner_rows(x_other[...], grads[count:])
    ).astype(jnp.bfloat16)


def weight_grad(x_mine, x_other, grads):
    count, model_width = x_mine.shape
    tile = model_width // 4
    columns = pl.BlockSpec((count, tile), lambda i: (0, i))
    return pl.pallas_call(
        weight_tile,
        grid=(4,),
        in_specs=[columns, columns, pl.BlockSpec(grads.shape, lambda i: (0, 0))],
        out_specs=pl.BlockSpec((tile, grads.shape[1]), lambda i: (i, 0)),
        out_shape=jax.ShapeDtypeStruct((model_width, grads.shape[1]), jnp.bfloat16),
        compiler_params=pltpu.CompilerParams(vmem_limit_bytes=24 * 1024 * 1024),
        cost_estimate=LITTLE,
        name="weight_grad",
    )(x_mine, x_other, grads)


def call(body, outs, args, scratch=(), name=None, in_specs=None, rows_keys=0):
    whole = pl.BlockSpec(memory_space=pltpu.VMEM)
    held = sum(x.size * x.dtype.itemsize for x in args)
    held += sum(math.prod(shape) * jnp.dtype(dtype).itemsize for shape, dtype in outs)
    grant = min(VMEM_BYTES, 2 * held + 48 * rows_keys + 8 * 1024 * 1024)
    if name in ALONE:
        grant = VMEM_BYTES
    return pl.pallas_call(
        body,
        in_specs=in_specs or [whole] * len(args),
        out_specs=[whole] * len(outs),
        out_shape=[jax.ShapeDtypeStruct(shape, dtype) for shape, dtype in outs],
        scratch_shapes=list(scratch),
        compiler_params=pltpu.CompilerParams(vmem_limit_bytes=grant),
        cost_estimate=LITTLE,
        name=name,
    )(*args)


def beside_body(*refs):
    *parts, out = refs
    start = 0
    for part in parts:
        out[:, start : start + part.shape[1]] = part[...]
        start += part.shape[1]


def side_by_side(parts):
    cols = sum(part.shape[1] for part in parts)
    return call(
        beside_body, [((parts[0].shape[0], cols), parts[0].dtype)], parts, name="side_by_side"
    )[0]


def place_body(plan, ctx_ref, *refs):
    count = max(part for part, *_ in plan) + 1
    parts, outs, sems = refs[:count], refs[count:-1], refs[-1]
    copies = []
    for part, k, column, cols, out, start in plan:
        rows = parts[part].shape[0]
        first = 0 if k is None else pl.multiple_of((ctx_ref[0] ^ k) * rows, rows)
        copies.append(
            pltpu.make_async_copy(
                parts[part].at[:, pl.ds(column, cols)],
                outs[out].at[pl.ds(first, rows), pl.ds(start, cols)],
                sems.at[len(copies)],
            )
        )
    for copy in copies:
        copy.start()
    for copy in copies:
        copy.wait()


def place_ctx(parts, spans, beside=None):
    ctx = lax.axis_index("ctx")
    count, rows = len(parts), parts[0].shape[0]
    if rows % 16:
        order = [ctx ^ k for k in range(count)]
        placed = [
            place_rows([part[:, column : column + cols] for part in parts], order)
            for column, cols in spans
        ]
        return placed if beside is None else [jnp.concatenate([beside, placed[0]], 1)]
    start = 0 if beside is None else beside.shape[1]
    plan = [
        (k, k, column, cols, out, start)
        for out, (column, cols) in enumerate(spans)
        for k in range(count)
    ]
    if beside is not None:
        plan.append((count, None, 0, start, 0, 0))
        parts = [*parts, beside]
    return call(
        functools.partial(place_body, plan),
        [((count * rows, start + cols), parts[0].dtype) for _, cols in spans],
        [ctx.astype(jnp.int32).reshape(1), *parts],
        [pltpu.SemaphoreType.DMA((len(plan),))],
        "place",
        [pl.BlockSpec(memory_space=pltpu.SMEM)]
        + [pl.BlockSpec(memory_space=pl.ANY)] * len(parts),
    )


def turn(values, cosines, signed_sines):
    return values * cosines + pltpu.roll(values, HD // 2, 1) * signed_sines


def turn_back(grads, cosines, signed_sines):
    return grads * cosines + pltpu.roll(grads, HD // 2, 1) * (-signed_sines)


def project_body(query_cols, key_cols, x, bias, cosines, signed_sines, *refs):
    shard, from_x, from_y, far_top, far_bottom = refs[:5]
    query, key_value, w_qkv, w_out, sems = refs[5:]
    near = shard.shape[0]
    half = near // 2
    split = w_qkv.shape[1]
    copies = []
    for part, start in (
        (shard, 0),
        (from_x, near),
        (from_y, 2 * near),
        (far_top, 3 * near),
        (far_bottom, 3 * near + half),
    ):
        rows = pl.ds(start, part.shape[0])
        left, right = part.at[:, pl.ds(0, split)], part.at[:, pl.ds(split, w_out.shape[1])]
        for source, target in ((left, w_qkv.at[rows]), (right, w_out.at[rows])):
            copies.append(pltpu.make_async_copy(source, target, sems.at[len(copies)]))
    for copy in copies:
        copy.start()
    for copy in copies[::2]:
        copy.wait()
    lin = matmul(x[...], w_qkv[...]) + bias[...]
    for start in range(0, query_cols, HD):
        query[:, start : start + HD] = turn(
            lin[:, start : start + HD], cosines[...], signed_sines[...]
        ).astype(jnp.bfloat16)
    for start in range(0, key_cols, HD):
        key_value[:, start : start + HD] = turn(
            lin[:, query_cols + start : query_cols + start + HD], cosines[...], signed_sines[...]
        ).astype(jnp.bfloat16)
    key_value[:, key_cols:] = lin[:, query_cols + key_cols :].astype(jnp.bfloat16)
    for copy in copies[1::2]:
        copy.wait()


def attend_body(count, core_ref, query, query_pos, key_pos, w_out, *refs):
    parts, (heads, log_sums, mine, send, total) = refs[:count], refs[count:]
    keys = jnp.concatenate([part[:, :HD] for part in parts], 0)
    values = jnp.concatenate([part[:, HD:] for part in parts], 0)
    visible = key_pos[...] <= query_pos[...]
    for start in range(0, query.shape[1], HD):
        scores = jnp.where(
            visible, times_transposed(query[:, start : start + HD], keys) * HD**-0.5, NEGATIVE
        )
        highest = jnp.max(scores, -1, keepdims=True)
        weights = jnp.exp(scores - highest)
        totals = jnp.sum(weights, -1, keepdims=True)
        heads[:, start : start + HD] = matmul(
            (weights * (1.0 / totals)).astype(jnp.bfloat16), values
        ).astype(jnp.bfloat16)
        log_sums[:, start : start + HD] = jnp.broadcast_to(
            highest + jnp.log(totals), (query.shape[0], HD)
        )
    split_rows(core_ref, times_transposed(heads[...], w_out[...]), total, mine, send)


def split_rows(core_ref, values, total, mine, send):
    half = mine.shape[0]
    core = core_ref[0]
    total[...] = values
    mine[...] = total[pl.ds(pl.multiple_of(core * half, half), half)]
    send[...] = total[pl.ds(pl.multiple_of((1 - core) * half, half), half)]


def norm_body(mine, got, inputs, gain, hidden, inverse_rms, normed):
    values = inputs[...] + mine[...] + got[...]
    hidden[...] = values
    inverse = lax.rsqrt(jnp.mean(values * values, -1, keepdims=True) + EPSILON)
    inverse_rms[...] = inverse
    normed[...] = (values * inverse * gain[...]).astype(jnp.bfloat16)


def norm_back_body(count, base, inputs, inverse_rms, gain, *refs):
    parts, outs = refs[:count], refs[count:]
    grads = parts[0][...].astype(jnp.float32)
    for part in parts[1:]:
        grads = grads + part[...].astype(jnp.float32)
    inverse = inverse_rms[...]
    values = inputs[...]
    weighted = grads * gain[...]
    back = inverse * weighted - values * (inverse * inverse * inverse) * jnp.mean(
        weighted * values, -1, keepdims=True
    )
    result = base[...].astype(jnp.float32) + back
    outs[0][...] = jnp.sum(grads * values * inverse, 0, keepdims=True)
    outs[1][...] = result.astype(jnp.bfloat16)
    if len(outs) > 2:
        outs[2][...] = result


def attend_back_body(
    count,
    core_ref,
    branch_mine,
    branch_other,
    query,
    query_pos,
    key_pos,
    w_out,
    heads,
    log_sums,
    cosines,
    signed_sines,
    *refs,
):
    parts, (query_lin, g_out), g_parts = refs[:count], refs[count : count + 2], refs[count + 2 : -1]
    branch = refs[-1]
    half = branch_mine.shape[0]
    core = core_ref[0]
    branch[pl.ds(pl.multiple_of(core * half, half), half)] = branch_mine[...]
    branch[pl.ds(pl.multiple_of((1 - core) * half, half), half)] = branch_other[...]
    keys = jnp.concatenate([part[:, :HD] for part in parts], 0)
    values = jnp.concatenate([part[:, HD:] for part in parts], 0)
    visible = key_pos[...] <= query_pos[...]
    g_heads = matmul(branch[...], w_out[...]).astype(jnp.bfloat16)
    scale = HD**-0.5
    g_keys = jnp.zeros(keys.shape, jnp.float32)
    g_values = jnp.zeros(values.shape, jnp.float32)
    for start in range(0, query.shape[1], HD):
        head = query[:, start : start + HD]
        g_head = g_heads[:, start : start + HD]
        scores = jnp.where(visible, times_transposed(head, keys) * scale, NEGATIVE)
        probs = jnp.exp(scores - log_sums[:, start : start + 1])
        g_probs = times_transposed(g_head, values)
        delta = jnp.sum(probs * g_probs, -1, keepdims=True)
        g_scores = (probs * (g_probs - delta)).astype(jnp.bfloat16)
        query_lin[:, start : start + HD] = turn_back(
            matmul(g_scores, keys) * scale, cosines[...], signed_sines[...]
        ).astype(jnp.bfloat16)
        g_keys = g_keys + inner_rows(g_scores, head)
        g_values = g_values + inner_rows(probs.astype(jnp.bfloat16), g_head)
    g_keys = g_keys * scale
    g_out[...] = inner_rows(branch[...], heads[...]).astype(jnp.bfloat16)
    rows = parts[0].shape[0]
    for k, out in enumerate(g_parts):
        out[:, :HD] = g_keys[k * rows : (k + 1) * rows].astype(out.dtype)
        out[:, HD:] = g_values[k * rows : (k + 1) * rows].astype(out.dtype)


def product_body(left, right, out):
    out[...] = inner_rows(left[...], right[...]).astype(jnp.bfloat16)


def project_back_body(
    count, core_ref, query_lin, w_qkv, cosines, signed_sines, inputs, inverse_rms, *refs
):
    parts, (lin, g_bias, g_gain, mine, send, total) = refs[:count], refs[count:]
    g_parts = parts[0][...].astype(jnp.float32)
    for part in parts[1:]:
        g_parts = g_parts + part[...].astype(jnp.float32)
    cols = query_lin.shape[1]
    lin[:, :cols] = query_lin[...]
    lin[:, cols : cols + HD] = turn_back(
        g_parts[:, :HD], cosines[...], signed_sines[...]
    ).astype(jnp.bfloat16)
    lin[:, cols + HD :] = g_parts[:, HD:].astype(jnp.bfloat16)
    split_rows(core_ref, times_transposed(lin[...], w_qkv[...]), total, mine, send)
    g_gain[...] = jnp.sum(total[...] * inputs[...] * inverse_rms[...], 0, keepdims=True)
    g_bias[...] = jnp.sum(lin[...].astype(jnp.float32), 0, keepdims=True)


def chip_sum(own, got):
    total = (own + got.astype(jnp.float32)).astype(jnp.bfloat16)
    return jnp.split(total, lax.axis_size("ctx"), 0)


def add_tree(parts):
    while len(parts) > 1:
        parts = [parts[i] + parts[i + 1] for i in range(0, len(parts), 2)]
    return parts[0]


def with_rows(block, rows):
    return jnp.concatenate([block, jnp.pad(rows, ((0, 0), (0, block.shape[1] - rows.shape[1])))], 0)


def on_device(
    layer_input,
    pairs,
    gain_attn,
    w_q,
    b_q,
    w_k,
    b_k,
    w_v,
    b_v,
    w_o,
    gain_mlp,
    w_gate,
    w_up,
    w_down,
    out_grad,
):
    _, span_rows, model_width = layer_input.shape
    half_rows = span_rows // 2
    query_cols = w_q.shape[1]
    key_cols = w_k.shape[1]
    units_here = w_gate.shape[1]
    ctx_size = lax.axis_size("ctx")
    ctx = lax.axis_index("ctx")
    core = lax.axis_index("wt")

    def own_half(values):
        return rows_at(values, core, half_rows)

    def join_halves(mine):
        other = swap(mine, "wt", 1)
        return jnp.where(
            core == 0, jnp.concatenate([mine, other], 0), jnp.concatenate([other, mine], 0)
        )

    within = jnp.arange(half_rows, dtype=jnp.int32)

    def positions_at(index):
        early = lax.dynamic_index_in_dim(pairs[0], index, 0, False)
        return jnp.concatenate(
            [early * half_rows + within, (2 * ctx_size - 1 - early) * half_rows + within]
        )

    query_positions = positions_at(ctx)
    key_positions = jnp.concatenate([positions_at(ctx ^ k) for k in range(ctx_size)])[None]
    cosines, sines = rope_tables(query_positions)
    signed_sines = jnp.concatenate([-sines[:, : HD // 2], sines[:, HD // 2 :]], 1)
    query_positions = query_positions[:, None]
    core_index = core.astype(jnp.int32).reshape(1)
    scalar = pl.BlockSpec(memory_space=pltpu.SMEM)
    whole = pl.BlockSpec(memory_space=pltpu.VMEM)
    left = pl.BlockSpec(memory_space=pl.ANY)

    input_rows = relative(layer_input.reshape(span_rows, model_width)).astype(jnp.float32)
    grad_out = relative(out_grad.reshape(span_rows, model_width))
    gain_one = relative(gain_attn.astype(jnp.float32))[None]
    gain_two = relative(gain_mlp.astype(jnp.float32))[None]

    rms_attn = lax.rsqrt(jnp.mean(input_rows * input_rows, -1, keepdims=True) + EPSILON)
    normed_attn = (input_rows * rms_attn * gain_one).astype(jnp.bfloat16)
    qkv_cols = query_cols + 2 * key_cols
    bias = jnp.concatenate([b_q, b_k, b_v]).astype(jnp.float32)[None]
    input_half = own_half(input_rows)
    attn_parts = gather_ctx(side_by_side([w_q, w_k, w_v, w_o]))
    gate_up_pieces = unit_pieces([w_gate, w_up])
    down_pieces = unit_pieces([w_down])
    grad_half = own_half(grad_out)
    (attn_shard,) = place_ctx(attn_parts, [(0, attn_parts[0].shape[1])])
    attn_shard, gate_up_pieces, down_pieces, tables = together(
        attn_shard,
        gate_up_pieces,
        down_pieces,
        (
            normed_attn,
            bias,
            cosines,
            signed_sines,
            query_positions,
            key_positions,
            input_half,
            grad_half,
            gain_two,
        ),
    )
    normed_attn, bias, cosines, signed_sines, query_positions, key_positions = tables[:6]
    input_half, grad_half, gain_two = tables[6:]

    attn_near = near_seq(attn_shard)
    gate_up_parts = exchange_ctx(gate_up_pieces)
    attn_near, gate_up_parts, down_pieces = together(attn_near, gate_up_parts, down_pieces)
    attn_far = far_seq(*attn_near)
    down_parts = exchange_ctx(down_pieces)
    width = units_per(units_here)
    up_shard, gate_shard = place_ctx(gate_up_parts, [(width, width), (0, width)])
    attn_far, up_shard = together(attn_far, up_shard)
    up_near = near_seq(up_shard)

    query, key_value, w_qkv, w_out = call(
        functools.partial(project_body, query_cols, key_cols),
        [
            ((span_rows, query_cols), jnp.bfloat16),
            ((span_rows, 2 * key_cols), jnp.bfloat16),
            ((model_width, qkv_cols), jnp.bfloat16),
            ((model_width, query_cols), jnp.bfloat16),
        ],
        [normed_attn, bias, cosines, signed_sines, attn_shard, *attn_near, *attn_far],
        [pltpu.SemaphoreType.DMA((10,))],
        "project",
        [whole] * 4 + [left] * 5,
    )
    key_value, down_parts = together(key_value, down_parts)

    (gate_down_shard,) = place_ctx(down_parts, [(0, width)], gate_shard)
    keys_values, gate_down_shard = together(gather_ctx(key_value), gate_down_shard)
    half_f32 = ((half_rows, model_width), jnp.float32)
    half_bf16 = ((half_rows, model_width), jnp.bfloat16)
    row_f32 = ((1, model_width), jnp.float32)
    attn_heads, log_sums, attn_mine, attn_send = call(
        functools.partial(attend_body, ctx_size),
        [
            ((span_rows, query_cols), jnp.bfloat16),
            ((span_rows, query_cols), jnp.float32),
            half_f32,
            half_f32,
        ],
        [core_index, query, query_positions, key_positions, w_out, *keys_values],
        [pltpu.VMEM((span_rows, model_width), jnp.float32)],
        "attend",
        [scalar] + [whole] * (4 + ctx_size),
        span_rows * key_positions.size,
    )
    hidden, rms_mlp, normed_half = call(
        norm_body,
        [half_f32, ((half_rows, 1), jnp.float32), half_bf16],
        [attn_mine, swap(attn_send, "wt", 1), input_half, gain_two],
        name="norm",
    )
    normed_half, gate_down_shard, up_near = together(normed_half, gate_down_shard, up_near)

    gate_down_near = near_seq(gate_down_shard)
    normed_parts, gate_down_near, grad_half = together(
        gather_ctx(normed_half), gate_down_near, grad_half
    )

    mlp_far = far_seq(*(jnp.concatenate(pair, 1) for pair in zip(up_near, gate_down_near)))
    normed_mine = jnp.concatenate(normed_parts, 0)
    normed_other, grad_half = together(swap(normed_mine, "wt", 1), grad_half)
    count = normed_mine.shape[0]
    mlp_parts = [up_shard, *up_near, gate_down_shard, *gate_down_near, *mlp_far]
    (gate_up,) = by_tiles(
        forward_tile,
        count,
        [],
        [(normed_mine, normed_other)],
        mlp_parts,
        [(2 * width, jnp.float32)],
        [],
        [(model_width, 2 * width)],
        "gate_up",
        26,
    )
    grad_parts, gate_up = together(gather_ctx(grad_half), gate_up)
    grad_mine = jnp.concatenate(grad_parts, 0)
    grad_other = swap(grad_mine, "wt", 1)
    g_both, act, back_mine, back_send, out_mine, out_send = by_tiles(
        backward_tile,
        count,
        [gate_up],
        [(grad_mine, grad_other)],
        mlp_parts,
        [(2 * width, jnp.bfloat16), (width, jnp.bfloat16)],
        [model_width, model_width],
        [(model_width, 2 * width), (model_width, width)],
        "mlp_back",
        42,
    )
    back_got = swap(back_send, "wt", 1)
    out_got = swap(out_send, "wt", 1)
    g_down = weight_grad(grad_mine, grad_other, act)
    g_normed_pieces = chip_sum(back_mine, back_got)
    g_normed_pieces, g_down, out_got, g_both = together(
        g_normed_pieces, g_down, out_got, g_both
    )

    g_normed_parts = exchange_ctx(g_normed_pieces)
    down_got = scatter_near(g_down)
    g_gate_up = weight_grad(normed_mine, normed_other, g_both)
    down_got, g_gate_up = together(down_got, g_gate_up)
    gate_up_payload = near_payload(g_gate_up)
    mlp_pieces = chip_sum(out_mine, out_got)
    down_sum = scatter_far(g_down, *down_got).astype(jnp.bfloat16)
    g_normed_parts, down_sum, gate_up_payload, mlp_pieces = together(
        g_normed_parts, down_sum, gate_up_payload, mlp_pieces
    )

    down_back = lax.all_to_all(
        down_sum.reshape(ctx_size, -1, down_sum.shape[1]), "ctx", 0, 0, tiled=True
    )
    gate_up_got = near_swap(gate_up_payload)
    grad_gain_mlp, branch_mine, g_hidden = call(
        functools.partial(norm_back_body, ctx_size),
        [row_f32, half_bf16, half_f32],
        [grad_half, hidden, rms_mlp, gain_two, *g_normed_parts],
        name="mlp_norm_back",
    )
    block = (span_rows, 2 * key_cols)
    query_lin, g_out, *g_blocks = call(
        functools.partial(attend_back_body, ctx_size),
        [
            ((span_rows, query_cols), jnp.bfloat16),
            ((model_width, query_cols), jnp.bfloat16),
            (block, jnp.float32),
        ]
        + [(block, jnp.bfloat16)] * (ctx_size - 1),
        [
            core_index,
            branch_mine,
            swap(branch_mine, "wt", 1),
            query,
            query_positions,
            key_positions,
            w_out,
            attn_heads,
            log_sums,
            cosines,
            signed_sines,
            *keys_values,
        ],
        [pltpu.VMEM((span_rows, model_width), jnp.bfloat16)],
        "attend_back",
        [scalar] + [whole] * (10 + ctx_size),
        span_rows * key_positions.size,
    )
    g_blocks, down_back = together(g_blocks, down_back)
    g_key_value_parts, gate_up_got, mlp_pieces = together(
        exchange_ctx(g_blocks), gate_up_got, mlp_pieces
    )

    mlp_parts = exchange_ctx(mlp_pieces)
    on_x, on_y = relay(g_gate_up, *gate_up_got)
    last_x, last_y, g_out = together(swap(on_x, "seq", 1), swap(on_y, "seq", 2), g_out)
    out_got = scatter_near(g_out)
    gate_up_sum = scatter_end(g_gate_up, *gate_up_got, last_x, last_y).astype(jnp.bfloat16)
    gate_up_blocks = gate_up_sum.reshape(ctx_size, -1, 2 * width)
    g_lin, g_bias, grad_gain_attn, normed_mine_grad, normed_send_grad = call(
        functools.partial(project_back_body, ctx_size),
        [
            ((span_rows, qkv_cols), jnp.bfloat16),
            ((1, qkv_cols), jnp.float32),
            row_f32,
            half_f32,
            half_f32,
        ],
        [
            core_index,
            query_lin,
            w_qkv,
            cosines,
            signed_sines,
            input_rows,
            rms_attn,
            *g_key_value_parts,
        ],
        [pltpu.VMEM((span_rows, model_width), jnp.float32)],
        "project_back",
        [scalar] + [whole] * (6 + ctx_size),
    )
    (g_qkv,) = call(
        product_body,
        [((model_width, qkv_cols), jnp.bfloat16)],
        [normed_attn, g_lin],
        name="qkv_grads",
    )
    small = jnp.concatenate(
        [
            relative(grad_gain_attn)[0],
            relative(grad_gain_mlp)[0],
            g_bias[0],
        ]
    ).astype(jnp.bfloat16)
    small_size = small.shape[0]
    small_rows = -(-small_size // (qkv_cols * 16)) * 16
    small = jnp.pad(small, (0, small_rows * qkv_cols - small_size)).reshape(small_rows, qkv_cols)

    payload_x, payload_y = near_payload(g_qkv)
    rows = payload_x.shape[0]
    half = rows // 2
    mlp_parts, gate_up_blocks, out_got, g_qkv, small, payload_y = together(
        mlp_parts, gate_up_blocks, out_got, g_qkv, small, payload_y
    )
    payload_x = jnp.concatenate([near_payload(g_qkv)[0], small], 0)

    gate_up_back = lax.all_to_all(gate_up_blocks, "ctx", 0, 0, tiled=True)
    got_x, got_y = near_swap((payload_x, payload_y))
    qkv_got = (got_x[:rows], got_y)
    small = add_up([small, got_x[rows:]]).astype(jnp.bfloat16)
    on_x, on_y = together(
        *(jnp.concatenate(pair, 1) for pair in zip(relay(g_qkv, *qkv_got), relay(g_out, *out_got)))
    )
    last_x = swap(on_x, "seq", 1)
    last_y = swap(with_rows(on_y, small), "seq", 2)
    small = add_up([small, last_y[half:, :qkv_cols]]).astype(jnp.bfloat16)
    attn_got = tuple(jnp.concatenate(pair, 1) for pair in zip(qkv_got, out_got))
    g_attn = jnp.concatenate([g_qkv, g_out], 1)
    attn_sum = scatter_end(g_attn, *attn_got, last_x, last_y[:half])
    attn_pieces = row_pieces(attn_sum)
    rows, attn_cols = attn_pieces[0].shape
    small_cols = -(-small_size // (rows * LANES)) * LANES
    small = jnp.pad(small.reshape(-1)[:small_size], (0, rows * small_cols - small_size))
    small = small.reshape(rows, small_cols)
    attn_send = [
        jnp.concatenate([piece.astype(jnp.bfloat16), small], 1) for piece in attn_pieces
    ]
    attn_send, gate_up_back, down_back, normed_send_grad, mlp_parts = together(
        attn_send, gate_up_back, down_back, normed_send_grad, mlp_parts
    )

    attn_back = exchange_ctx(attn_send)
    _, grad_input_half = call(
        functools.partial(norm_back_body, 2),
        [row_f32, half_bf16],
        [
            g_hidden,
            input_half,
            own_half(rms_attn),
            gain_one,
            normed_mine_grad,
            swap(normed_send_grad, "wt", 1),
        ],
        name="attn_norm_back",
    )
    grad_input_half = relative(grad_input_half)

    grad_input = join_halves(grad_input_half)
    layer_output = join_halves(relative((hidden + add_up(mlp_parts)).astype(jnp.bfloat16)))
    attn_back, grad_input, layer_output = together(attn_back, grad_input, layer_output)
    attn_back = attn_pieces[:1] + attn_back[1:]
    grad_w_gate, grad_w_up = (
        jnp.concatenate([block[:, start : start + width] for block in gate_up_back], 1)[
            :, :units_here
        ].astype(jnp.float32)
        for start in (0, width)
    )
    grad_w_down = jnp.concatenate(list(down_back), 1)[:, :units_here].astype(jnp.float32)
    grad_w_attn = add_up([part[:, :attn_cols] for part in attn_back])
    grad_w_qkv = grad_w_attn[:, :qkv_cols]
    grad_w_o = grad_w_attn[:, qkv_cols:]
    small = add_tree(
        [small.astype(jnp.float32)]
        + [part[:, attn_cols:].astype(jnp.float32) for part in attn_back[1:]]
    ).reshape(-1)
    gains = small[: 2 * model_width].reshape(-1, LANES)
    gains = (gains + swap(gains, "wt", 1)).reshape(-1)
    grad_bias = small[2 * model_width : small_size]
    return (
        layer_output[None],
        grad_input[None],
        gains[:model_width],
        grad_w_qkv[:, :query_cols],
        grad_bias[:query_cols],
        grad_w_qkv[:, query_cols : query_cols + key_cols],
        grad_bias[query_cols : query_cols + key_cols],
        grad_w_qkv[:, query_cols + key_cols :],
        grad_bias[query_cols + key_cols :],
        grad_w_o,
        gains[model_width:],
        grad_w_gate,
        grad_w_up,
        grad_w_down,
    )


def solution(mesh):
    tokens = P("seq", "ctx", None)
    weight = P(("seq", "ctx"), "wt")
    return jax.shard_map(
        on_device,
        mesh=mesh,
        in_specs=(
            tokens,
            P("seq", None),
            P(),
            weight,
            P("wt"),
            weight,
            P("wt"),
            weight,
            P("wt"),
            weight,
            P(),
            weight,
            weight,
            weight,
            tokens,
        ),
        out_specs=(
            tokens,
            tokens,
            P(),
            weight,
            P("wt"),
            weight,
            P("wt"),
            weight,
            P("wt"),
            weight,
            P(),
            weight,
            weight,
            weight,
        ),
        check_vma=False,
    )
```

```python
import functools
import math

import jax
import jax.numpy as jnp
from jax import lax
from jax.experimental import pallas as pl
from jax.experimental.pallas import tpu as pltpu
from jax.sharding import PartitionSpec as P

HD = 128
LANES = 128


EPSILON = 1e-06
THETA_BASE = 1000000.0
NEGATIVE = -1e30


def rope_tables(positions):
    freqs = THETA_BASE ** (-(jnp.arange(HD // 2, dtype=jnp.float32) * 2.0) / HD)
    angles = positions.astype(jnp.float32)[:, None] * freqs[None, :]
    cosines = jnp.cos(angles)
    sines = jnp.sin(angles)
    return (jnp.concatenate([cosines, cosines], -1), jnp.concatenate([sines, sines], -1))


def matmul(left, right):
    return jnp.dot(left, right, preferred_element_type=jnp.float32)


def times_transposed(left, right):
    return lax.dot_general(
        left, right, (((1,), (1,)), ((), ())), preferred_element_type=jnp.float32
    )


def inner_rows(left, right):
    return lax.dot_general(
        left, right, (((0,), (0,)), ((), ())), preferred_element_type=jnp.float32
    )


def swap(values, axis, offset):
    size = lax.axis_size(axis)
    return lax.ppermute(values, axis, [(i, i ^ offset) for i in range(size)])


def rows_at(values, index, count):
    return lax.dynamic_slice_in_dim(values, index * count, count, 0)


def place_rows(parts, indices):
    rows = len(parts) * parts[0].shape[0]
    whole = jnp.zeros((rows,) + parts[0].shape[1:], parts[0].dtype)
    for part, index in zip(parts, indices):
        whole = lax.dynamic_update_slice_in_dim(whole, part, index * part.shape[0], 0)
    return whole


def together(*values):
    return lax.optimization_barrier(values)


def relative(values):
    me = lax.axis_index("seq")
    width = values.shape[-1] // 4
    blocks = [
        lax.dynamic_slice_in_dim(values, (me ^ j) * width, width, values.ndim - 1)
        for j in range(4)
    ]
    return jnp.concatenate(blocks, -1)


def gather_ctx(block):
    size = lax.axis_size("ctx")
    return [block] + [swap(block, "ctx", k) for k in range(1, size)]


def exchange_ctx(pieces):
    return [pieces[0]] + [swap(pieces[k], "ctx", k) for k in range(1, len(pieces))]


def near_seq(shard):
    return swap(shard, "seq", 1), swap(shard, "seq", 2)


def far_seq(from_x, from_y):
    half = from_x.shape[0] // 2
    return swap(from_y[:half], "seq", 1), swap(from_x[half:], "seq", 2)


def near_payload(partial_sum):
    _, for_x, for_y, for_far = jnp.split(partial_sum, 4, 0)
    half = for_x.shape[0] // 2
    return (
        jnp.concatenate([for_far[half:], for_x[half:]], 0),
        jnp.concatenate([for_far[:half], for_y[:half]], 0),
    )


def near_swap(payload):
    return swap(payload[0], "seq", 1), swap(payload[1], "seq", 2)


def scatter_near(partial_sum):
    return near_swap(near_payload(partial_sum))


def relay(partial_sum, got_x, got_y):
    _, for_x, for_y, _ = jnp.split(partial_sum, 4, 0)
    half = for_x.shape[0] // 2
    on_x = add_up([for_x[:half], got_y[:half]]).astype(jnp.bfloat16)
    on_y = add_up([for_y[half:], got_x[:half]]).astype(jnp.bfloat16)
    return together(on_x, on_y)


def scatter_end(partial_sum, got_x, got_y, last_x, last_y):
    own = partial_sum[: partial_sum.shape[0] // 4]
    half = own.shape[0] // 2
    top = add_up([own[:half], got_y[half:], last_x])
    bottom = add_up([own[half:], got_x[half:], last_y])
    return jnp.concatenate([top, bottom], 0)


def scatter_far(partial_sum, got_x, got_y):
    on_x, on_y = relay(partial_sum, got_x, got_y)
    return scatter_end(
        partial_sum, got_x, got_y, swap(on_x, "seq", 1), swap(on_y, "seq", 2)
    )


def add_up(parts):
    total = parts[0].astype(jnp.float32)
    for part in parts[1:]:
        total = total + part.astype(jnp.float32)
    return total


def units_per(units):
    size = lax.axis_size("ctx")
    return -(-units // (size * LANES)) * LANES


def unit_pieces(shards):
    size = lax.axis_size("ctx")
    ctx = lax.axis_index("ctx")
    width = units_per(shards[0].shape[1])
    padded = [jnp.pad(w, ((0, 0), (0, size * width - w.shape[1]))) for w in shards]
    return [
        jnp.concatenate(
            [lax.dynamic_slice_in_dim(w, (ctx ^ k) * width, width, 1) for w in padded], 1
        )
        for k in range(size)
    ]


def row_pieces(summed):
    size = lax.axis_size("ctx")
    ctx = lax.axis_index("ctx")
    rows = summed.shape[0] // size
    return [rows_at(summed, ctx ^ k, rows) for k in range(size)]


def place_units(parts, units):
    size = lax.axis_size("ctx")
    ctx = lax.axis_index("ctx")
    width = units_per(units)
    wholes = []
    for start in range(0, parts[0].shape[1], width):
        whole = jnp.zeros((parts[0].shape[0], size * width), jnp.float32)
        for k in range(size):
            part = parts[k][:, start : start + width].astype(jnp.float32)
            whole = lax.dynamic_update_slice_in_dim(whole, part, (ctx ^ k) * width, 1)
        wholes.append(whole[:, :units])
    return wholes


def narrow_others(pieces):
    return [pieces[0]] + [piece.astype(jnp.bfloat16) for piece in pieces[1:]]


VMEM_BYTES = 56 * 1024 * 1024
ALONE = ("side_by_side", "mlp_norm_back", "attend_back", "project_back")
LITTLE = pl.CostEstimate(flops=1, bytes_accessed=1, transcendentals=0)


def stack_copies(targets, sems, used=0):
    copies = []
    for target, parts in targets:
        row, cols = 0, target.shape[1]
        group = []
        for part, column in parts:
            group.append(
                pltpu.make_async_copy(
                    part.at[:, pl.ds(column, cols)],
                    target.at[pl.ds(row, part.shape[0])],
                    sems.at[used + sum(map(len, copies)) + len(group)],
                )
            )
            row += part.shape[0]
        copies.append(group)
    return copies


def start_all(groups):
    for group in groups:
        for copy in group:
            copy.start()


def wait_all(groups):
    for group in groups:
        for copy in group:
            copy.wait()


def gate_up_copies(refs, gu, sems):
    up, gate_down, far = refs[:3], refs[3:6], refs[6:8]
    width = gu.shape[1] // 2
    return [
        (gu.at[:, pl.ds(0, width)], [(p, 0) for p in gate_down] + [(p, width) for p in far]),
        (gu.at[:, pl.ds(width, width)], [(p, 0) for p in up] + [(p, 0) for p in far]),
    ]


def forward_tile(tiles_each, x_mine, x_other, *refs):
    parts, (gate_up, gu, sems) = refs[:8], refs[8:]
    step = pl.program_id(0)

    @pl.when(step == 0)
    def _():
        copies = stack_copies(gate_up_copies(parts, gu, sems), sems)
        start_all(copies)
        wait_all(copies)

    rows = jnp.where(step < tiles_each, x_mine[...], x_other[...])
    gate_up[...] = matmul(rows, gu[...]).astype(gate_up.dtype)


def backward_tile(tiles_each, gate_up, o_mine, o_other, *refs):
    parts, refs = refs[:8], refs[8:]
    both_ref, act_ref, back_mine, back_send, out_mine, out_send, gu, down, sems = refs
    step = pl.program_id(0)
    own = step < tiles_each
    width = down.shape[1]

    down_target = [(down, [(p, width) for p in parts[3:6]] + [(p, 2 * width) for p in parts[6:]])]

    @pl.when(step == 0)
    def _():
        first = stack_copies(down_target, sems)
        start_all(first)
        start_all(stack_copies(gate_up_copies(parts, gu, sems), sems, 5))
        wait_all(first)

    grads = jnp.where(own, o_mine[...], o_other[...])
    g_act = matmul(grads, down[...])
    gate = gate_up[:, :width].astype(jnp.float32)
    up = gate_up[:, width:].astype(jnp.float32)
    sigmoid_gate = 1.0 / (1.0 + jnp.exp(-gate))
    silu_gate = gate * sigmoid_gate
    act_ref[...] = (silu_gate * up).astype(jnp.bfloat16)
    both_ref[:, :width] = (
        g_act * up * sigmoid_gate * (1.0 + gate * (1.0 - sigmoid_gate))
    ).astype(jnp.bfloat16)
    both_ref[:, width:] = (g_act * silu_gate).astype(jnp.bfloat16)

    @pl.when(step == 0)
    def _():
        wait_all(stack_copies(gate_up_copies(parts, gu, sems), sems, 5))

    back = times_transposed(both_ref[...], gu[...])
    out = times_transposed(act_ref[...], down[...])

    @pl.when(own)
    def _():
        back_mine[...] = back
        out_mine[...] = out

    @pl.when(jnp.logical_not(own))
    def _():
        back_send[...] = back.astype(jnp.bfloat16)
        out_send[...] = out.astype(jnp.bfloat16)


def by_tiles(body, count, ins, halves, parts, outs, half_outs, scratch, name, grant):
    tile = min(256, count)
    tiles_each = count // tile

    def rows(cols):
        return pl.BlockSpec((tile, cols), lambda i: (i, 0))

    def mine(cols):
        return pl.BlockSpec((tile, cols), lambda i: (jnp.minimum(i, tiles_each - 1), 0))

    def other(cols):
        return pl.BlockSpec((tile, cols), lambda i: (jnp.maximum(i - tiles_each, 0), 0))

    return pl.pallas_call(
        functools.partial(body, tiles_each),
        grid=(2 * tiles_each,),
        in_specs=[rows(x.shape[1]) for x in ins]
        + [spec(x.shape[1]) for pair in halves for spec, x in zip((mine, other), pair)]
        + [pl.BlockSpec(memory_space=pl.ANY)] * len(parts),
        out_specs=[rows(cols) for cols, _ in outs]
        + [spec(cols) for cols in half_outs for spec in (mine, other)],
        out_shape=[jax.ShapeDtypeStruct((2 * count, cols), dtype) for cols, dtype in outs]
        + [
            jax.ShapeDtypeStruct((count, cols), dtype)
            for cols in half_outs
            for dtype in (jnp.float32, jnp.bfloat16)
        ],
        scratch_shapes=[pltpu.VMEM(shape, jnp.bfloat16) for shape in scratch]
        + [pltpu.SemaphoreType.DMA((15,))],
        compiler_params=pltpu.CompilerParams(vmem_limit_bytes=grant * 1024 * 1024),
        cost_estimate=LITTLE,
        name=name,
    )(*ins, *(x for pair in halves for x in pair), *parts)


def weight_tile(x_mine, x_other, grads, out):
    count = x_mine.shape[0]
    out[...] = (
        inner_rows(x_mine[...], grads[:count]) + inner_rows(x_other[...], grads[count:])
    ).astype(jnp.bfloat16)


def weight_grad(x_mine, x_other, grads):
    count, model_width = x_mine.shape
    tile = model_width // 3
    columns = pl.BlockSpec((count, tile), lambda i: (0, i))
    return pl.pallas_call(
        weight_tile,
        grid=(3,),
        in_specs=[columns, columns, pl.BlockSpec(grads.shape, lambda i: (0, 0))],
        out_specs=pl.BlockSpec((tile, grads.shape[1]), lambda i: (i, 0)),
        out_shape=jax.ShapeDtypeStruct((model_width, grads.shape[1]), jnp.bfloat16),
        compiler_params=pltpu.CompilerParams(vmem_limit_bytes=28 * 1024 * 1024),
        cost_estimate=LITTLE,
        name="weight_grad",
    )(x_mine, x_other, grads)


def call(body, outs, args, scratch=(), name=None, in_specs=None, rows_keys=0):
    whole = pl.BlockSpec(memory_space=pltpu.VMEM)
    held = sum(x.size * x.dtype.itemsize for x in args)
    held += sum(math.prod(shape) * jnp.dtype(dtype).itemsize for shape, dtype in outs)
    grant = min(VMEM_BYTES, 2 * held + 48 * rows_keys + 8 * 1024 * 1024)
    if name in ALONE:
        grant = VMEM_BYTES
    return pl.pallas_call(
        body,
        in_specs=in_specs or [whole] * len(args),
        out_specs=[whole] * len(outs),
        out_shape=[jax.ShapeDtypeStruct(shape, dtype) for shape, dtype in outs],
        scratch_shapes=list(scratch),
        compiler_params=pltpu.CompilerParams(vmem_limit_bytes=grant),
        cost_estimate=LITTLE,
        name=name,
    )(*args)


def beside_body(*refs):
    *parts, out = refs
    start = 0
    for part in parts:
        out[:, start : start + part.shape[1]] = part[...]
        start += part.shape[1]


def side_by_side(parts):
    cols = sum(part.shape[1] for part in parts)
    return call(
        beside_body, [((parts[0].shape[0], cols), parts[0].dtype)], parts, name="side_by_side"
    )[0]


def place_body(plan, ctx_ref, *refs):
    count = max(part for part, *_ in plan) + 1
    parts, outs, sems = refs[:count], refs[count:-1], refs[-1]
    copies = []
    for part, k, column, cols, out, start in plan:
        rows = parts[part].shape[0]
        first = 0 if k is None else pl.multiple_of((ctx_ref[0] ^ k) * rows, rows)
        copies.append(
            pltpu.make_async_copy(
                parts[part].at[:, pl.ds(column, cols)],
                outs[out].at[pl.ds(first, rows), pl.ds(start, cols)],
                sems.at[len(copies)],
            )
        )
    for copy in copies:
        copy.start()
    for copy in copies:
        copy.wait()


def place_ctx(parts, spans, beside=None):
    ctx = lax.axis_index("ctx")
    count, rows = len(parts), parts[0].shape[0]
    if rows % 16:
        order = [ctx ^ k for k in range(count)]
        placed = [
            place_rows([part[:, column : column + cols] for part in parts], order)
            for column, cols in spans
        ]
        return placed if beside is None else [jnp.concatenate([beside, placed[0]], 1)]
    start = 0 if beside is None else beside.shape[1]
    plan = [
        (k, k, column, cols, out, start)
        for out, (column, cols) in enumerate(spans)
        for k in range(count)
    ]
    if beside is not None:
        plan.append((count, None, 0, start, 0, 0))
        parts = [*parts, beside]
    return call(
        functools.partial(place_body, plan),
        [((count * rows, start + cols), parts[0].dtype) for _, cols in spans],
        [ctx.astype(jnp.int32).reshape(1), *parts],
        [pltpu.SemaphoreType.DMA((len(plan),))],
        "place",
        [pl.BlockSpec(memory_space=pltpu.SMEM)]
        + [pl.BlockSpec(memory_space=pl.ANY)] * len(parts),
    )


def turn(values, cosines, signed_sines):
    return values * cosines + pltpu.roll(values, HD // 2, 1) * signed_sines


def turn_back(grads, cosines, signed_sines):
    return grads * cosines + pltpu.roll(grads, HD // 2, 1) * (-signed_sines)


def project_body(query_cols, key_cols, x, bias, cosines, signed_sines, *refs):
    shard, from_x, from_y, far_top, far_bottom = refs[:5]
    query, key_value, w_qkv, w_out, sems = refs[5:]
    near = shard.shape[0]
    half = near // 2
    split = w_qkv.shape[1]
    copies = []
    for part, start in (
        (shard, 0),
        (from_x, near),
        (from_y, 2 * near),
        (far_top, 3 * near),
        (far_bottom, 3 * near + half),
    ):
        rows = pl.ds(start, part.shape[0])
        left, right = part.at[:, pl.ds(0, split)], part.at[:, pl.ds(split, w_out.shape[1])]
        for source, target in ((left, w_qkv.at[rows]), (right, w_out.at[rows])):
            copies.append(pltpu.make_async_copy(source, target, sems.at[len(copies)]))
    for copy in copies:
        copy.start()
    for copy in copies[::2]:
        copy.wait()
    lin = matmul(x[...], w_qkv[...]) + bias[...]
    for start in range(0, query_cols, HD):
        query[:, start : start + HD] = turn(
            lin[:, start : start + HD], cosines[...], signed_sines[...]
        ).astype(jnp.bfloat16)
    for start in range(0, key_cols, HD):
        key_value[:, start : start + HD] = turn(
            lin[:, query_cols + start : query_cols + start + HD], cosines[...], signed_sines[...]
        ).astype(jnp.bfloat16)
    key_value[:, key_cols:] = lin[:, query_cols + key_cols :].astype(jnp.bfloat16)
    for copy in copies[1::2]:
        copy.wait()


def attend_body(count, core_ref, query, query_pos, key_pos, w_out, *refs):
    parts, (heads, log_sums, mine, send, total) = refs[:count], refs[count:]
    keys = jnp.concatenate([part[:, :HD] for part in parts], 0)
    values = jnp.concatenate([part[:, HD:] for part in parts], 0)
    visible = key_pos[...] <= query_pos[...]
    for start in range(0, query.shape[1], HD):
        scores = jnp.where(
            visible, times_transposed(query[:, start : start + HD], keys) * HD**-0.5, NEGATIVE
        )
        highest = jnp.max(scores, -1, keepdims=True)
        weights = jnp.exp(scores - highest)
        totals = jnp.sum(weights, -1, keepdims=True)
        heads[:, start : start + HD] = matmul(
            (weights * (1.0 / totals)).astype(jnp.bfloat16), values
        ).astype(jnp.bfloat16)
        log_sums[:, start : start + HD] = jnp.broadcast_to(
            highest + jnp.log(totals), (query.shape[0], HD)
        )
    split_rows(core_ref, times_transposed(heads[...], w_out[...]), total, mine, send)


def split_rows(core_ref, values, total, mine, send):
    half = mine.shape[0]
    core = core_ref[0]
    total[...] = values
    mine[...] = total[pl.ds(pl.multiple_of(core * half, half), half)]
    send[...] = total[pl.ds(pl.multiple_of((1 - core) * half, half), half)]


def norm_body(mine, got, inputs, gain, hidden, inverse_rms, normed):
    values = inputs[...] + mine[...] + got[...]
    hidden[...] = values
    inverse = lax.rsqrt(jnp.mean(values * values, -1, keepdims=True) + EPSILON)
    inverse_rms[...] = inverse
    normed[...] = (values * inverse * gain[...]).astype(jnp.bfloat16)


def norm_back_body(count, base, inputs, inverse_rms, gain, *refs):
    parts, outs = refs[:count], refs[count:]
    grads = parts[0][...].astype(jnp.float32)
    for part in parts[1:]:
        grads = grads + part[...].astype(jnp.float32)
    inverse = inverse_rms[...]
    values = inputs[...]
    weighted = grads * gain[...]
    back = inverse * weighted - values * (inverse * inverse * inverse) * jnp.mean(
        weighted * values, -1, keepdims=True
    )
    result = base[...].astype(jnp.float32) + back
    outs[0][...] = jnp.sum(grads * values * inverse, 0, keepdims=True)
    outs[1][...] = result.astype(jnp.bfloat16)
    if len(outs) > 2:
        outs[2][...] = result


def attend_back_body(
    count,
    core_ref,
    branch_mine,
    branch_other,
    query,
    query_pos,
    key_pos,
    w_out,
    heads,
    log_sums,
    cosines,
    signed_sines,
    *refs,
):
    parts, (query_lin, g_out), g_parts = refs[:count], refs[count : count + 2], refs[count + 2 : -1]
    branch = refs[-1]
    half = branch_mine.shape[0]
    core = core_ref[0]
    branch[pl.ds(pl.multiple_of(core * half, half), half)] = branch_mine[...]
    branch[pl.ds(pl.multiple_of((1 - core) * half, half), half)] = branch_other[...]
    keys = jnp.concatenate([part[:, :HD] for part in parts], 0)
    values = jnp.concatenate([part[:, HD:] for part in parts], 0)
    visible = key_pos[...] <= query_pos[...]
    g_heads = matmul(branch[...], w_out[...]).astype(jnp.bfloat16)
    scale = HD**-0.5
    g_keys = jnp.zeros(keys.shape, jnp.float32)
    g_values = jnp.zeros(values.shape, jnp.float32)
    for start in range(0, query.shape[1], HD):
        head = query[:, start : start + HD]
        g_head = g_heads[:, start : start + HD]
        scores = jnp.where(visible, times_transposed(head, keys) * scale, NEGATIVE)
        probs = jnp.exp(scores - log_sums[:, start : start + 1])
        g_probs = times_transposed(g_head, values)
        delta = jnp.sum(probs * g_probs, -1, keepdims=True)
        g_scores = (probs * (g_probs - delta)).astype(jnp.bfloat16)
        query_lin[:, start : start + HD] = turn_back(
            matmul(g_scores, keys) * scale, cosines[...], signed_sines[...]
        ).astype(jnp.bfloat16)
        g_keys = g_keys + inner_rows(g_scores, head)
        g_values = g_values + inner_rows(probs.astype(jnp.bfloat16), g_head)
    g_keys = g_keys * scale
    g_out[...] = inner_rows(branch[...], heads[...]).astype(jnp.bfloat16)
    rows = parts[0].shape[0]
    for k, out in enumerate(g_parts):
        out[:, :HD] = g_keys[k * rows : (k + 1) * rows].astype(out.dtype)
        out[:, HD:] = g_values[k * rows : (k + 1) * rows].astype(out.dtype)


def product_body(left, right, out):
    out[...] = inner_rows(left[...], right[...]).astype(jnp.bfloat16)


def project_back_body(
    count, core_ref, query_lin, w_qkv, cosines, signed_sines, inputs, inverse_rms, *refs
):
    parts, (lin, g_bias, g_gain, mine, send, total) = refs[:count], refs[count:]
    g_parts = parts[0][...].astype(jnp.float32)
    for part in parts[1:]:
        g_parts = g_parts + part[...].astype(jnp.float32)
    cols = query_lin.shape[1]
    lin[:, :cols] = query_lin[...]
    lin[:, cols : cols + HD] = turn_back(
        g_parts[:, :HD], cosines[...], signed_sines[...]
    ).astype(jnp.bfloat16)
    lin[:, cols + HD :] = g_parts[:, HD:].astype(jnp.bfloat16)
    split_rows(core_ref, times_transposed(lin[...], w_qkv[...]), total, mine, send)
    g_gain[...] = jnp.sum(total[...] * inputs[...] * inverse_rms[...], 0, keepdims=True)
    g_bias[...] = jnp.sum(lin[...].astype(jnp.float32), 0, keepdims=True)


def chip_sum(own, got):
    total = (own + got.astype(jnp.float32)).astype(jnp.bfloat16)
    return jnp.split(total, lax.axis_size("ctx"), 0)


def add_tree(parts):
    while len(parts) > 1:
        parts = [parts[i] + parts[i + 1] for i in range(0, len(parts), 2)]
    return parts[0]


def with_rows(block, rows):
    return jnp.concatenate([block, jnp.pad(rows, ((0, 0), (0, block.shape[1] - rows.shape[1])))], 0)


def on_device(
    layer_input,
    pairs,
    gain_attn,
    w_q,
    b_q,
    w_k,
    b_k,
    w_v,
    b_v,
    w_o,
    gain_mlp,
    w_gate,
    w_up,
    w_down,
    out_grad,
):
    _, span_rows, model_width = layer_input.shape
    half_rows = span_rows // 2
    query_cols = w_q.shape[1]
    key_cols = w_k.shape[1]
    units_here = w_gate.shape[1]
    ctx_size = lax.axis_size("ctx")
    ctx = lax.axis_index("ctx")
    core = lax.axis_index("wt")

    def own_half(values):
        return rows_at(values, core, half_rows)

    def join_halves(mine):
        other = swap(mine, "wt", 1)
        return jnp.where(
            core == 0, jnp.concatenate([mine, other], 0), jnp.concatenate([other, mine], 0)
        )

    within = jnp.arange(half_rows, dtype=jnp.int32)

    def positions_at(index):
        early = lax.dynamic_index_in_dim(pairs[0], index, 0, False)
        return jnp.concatenate(
            [early * half_rows + within, (2 * ctx_size - 1 - early) * half_rows + within]
        )

    query_positions = positions_at(ctx)
    key_positions = jnp.concatenate([positions_at(ctx ^ k) for k in range(ctx_size)])[None]
    cosines, sines = rope_tables(query_positions)
    signed_sines = jnp.concatenate([-sines[:, : HD // 2], sines[:, HD // 2 :]], 1)
    query_positions = query_positions[:, None]
    core_index = core.astype(jnp.int32).reshape(1)
    scalar = pl.BlockSpec(memory_space=pltpu.SMEM)
    whole = pl.BlockSpec(memory_space=pltpu.VMEM)
    left = pl.BlockSpec(memory_space=pl.ANY)

    input_rows = relative(layer_input.reshape(span_rows, model_width)).astype(jnp.float32)
    grad_out = relative(out_grad.reshape(span_rows, model_width))
    gain_one = relative(gain_attn.astype(jnp.float32))[None]
    gain_two = relative(gain_mlp.astype(jnp.float32))[None]

    rms_attn = lax.rsqrt(jnp.mean(input_rows * input_rows, -1, keepdims=True) + EPSILON)
    normed_attn = (input_rows * rms_attn * gain_one).astype(jnp.bfloat16)
    qkv_cols = query_cols + 2 * key_cols
    bias = jnp.concatenate([b_q, b_k, b_v]).astype(jnp.float32)[None]
    input_half = own_half(input_rows)
    attn_parts = gather_ctx(side_by_side([w_q, w_k, w_v, w_o]))
    gate_up_pieces = unit_pieces([w_gate, w_up])
    down_pieces = unit_pieces([w_down])
    grad_half = own_half(grad_out)
    (attn_shard,) = place_ctx(attn_parts, [(0, attn_parts[0].shape[1])])
    attn_shard, gate_up_pieces, down_pieces, tables = together(
        attn_shard,
        gate_up_pieces,
        down_pieces,
        (
            normed_attn,
            bias,
            cosines,
            signed_sines,
            query_positions,
            key_positions,
            input_half,
            grad_half,
            gain_two,
        ),
    )
    normed_attn, bias, cosines, signed_sines, query_positions, key_positions = tables[:6]
    input_half, grad_half, gain_two = tables[6:]

    attn_near = near_seq(attn_shard)
    gate_up_parts = exchange_ctx(gate_up_pieces)
    attn_near, gate_up_parts, down_pieces = together(attn_near, gate_up_parts, down_pieces)
    attn_far = far_seq(*attn_near)
    down_parts = exchange_ctx(down_pieces)
    width = units_per(units_here)
    up_shard, gate_shard = place_ctx(gate_up_parts, [(width, width), (0, width)])
    attn_far, up_shard = together(attn_far, up_shard)
    up_near = near_seq(up_shard)

    query, key_value, w_qkv, w_out = call(
        functools.partial(project_body, query_cols, key_cols),
        [
            ((span_rows, query_cols), jnp.bfloat16),
            ((span_rows, 2 * key_cols), jnp.bfloat16),
            ((model_width, qkv_cols), jnp.bfloat16),
            ((model_width, query_cols), jnp.bfloat16),
        ],
        [normed_attn, bias, cosines, signed_sines, attn_shard, *attn_near, *attn_far],
        [pltpu.SemaphoreType.DMA((10,))],
        "project",
        [whole] * 4 + [left] * 5,
    )
    key_value, down_parts = together(key_value, down_parts)

    (gate_down_shard,) = place_ctx(down_parts, [(0, width)], gate_shard)
    keys_values, gate_down_shard = together(gather_ctx(key_value), gate_down_shard)
    half_f32 = ((half_rows, model_width), jnp.float32)
    half_bf16 = ((half_rows, model_width), jnp.bfloat16)
    row_f32 = ((1, model_width), jnp.float32)
    attn_heads, log_sums, attn_mine, attn_send = call(
        functools.partial(attend_body, ctx_size),
        [
            ((span_rows, query_cols), jnp.bfloat16),
            ((span_rows, query_cols), jnp.float32),
            half_f32,
            half_f32,
        ],
        [core_index, query, query_positions, key_positions, w_out, *keys_values],
        [pltpu.VMEM((span_rows, model_width), jnp.float32)],
        "attend",
        [scalar] + [whole] * (4 + ctx_size),
        span_rows * key_positions.size,
    )
    hidden, rms_mlp, normed_half = call(
        norm_body,
        [half_f32, ((half_rows, 1), jnp.float32), half_bf16],
        [attn_mine, swap(attn_send, "wt", 1), input_half, gain_two],
        name="norm",
    )
    normed_half, gate_down_shard, up_near = together(normed_half, gate_down_shard, up_near)

    gate_down_near = near_seq(gate_down_shard)
    normed_parts, gate_down_near, grad_half = together(
        gather_ctx(normed_half), gate_down_near, grad_half
    )

    mlp_far = far_seq(*(jnp.concatenate(pair, 1) for pair in zip(up_near, gate_down_near)))
    normed_mine = jnp.concatenate(normed_parts, 0)
    normed_other, grad_half = together(swap(normed_mine, "wt", 1), grad_half)
    count = normed_mine.shape[0]
    mlp_parts = [up_shard, *up_near, gate_down_shard, *gate_down_near, *mlp_far]
    (gate_up,) = by_tiles(
        forward_tile,
        count,
        [],
        [(normed_mine, normed_other)],
        mlp_parts,
        [(2 * width, jnp.bfloat16)],
        [],
        [(model_width, 2 * width)],
        "gate_up",
        22,
    )
    grad_parts, gate_up = together(gather_ctx(grad_half), gate_up)
    grad_mine = jnp.concatenate(grad_parts, 0)
    grad_other = swap(grad_mine, "wt", 1)
    g_both, act, back_mine, back_send, out_mine, out_send = by_tiles(
        backward_tile,
        count,
        [gate_up],
        [(grad_mine, grad_other)],
        mlp_parts,
        [(2 * width, jnp.bfloat16), (width, jnp.bfloat16)],
        [model_width, model_width],
        [(model_width, 2 * width), (model_width, width)],
        "mlp_back",
        39,
    )
    back_got = swap(back_send, "wt", 1)
    out_got = swap(out_send, "wt", 1)
    g_down = weight_grad(grad_mine, grad_other, act)
    g_normed_pieces = chip_sum(back_mine, back_got)
    g_normed_pieces, g_down, out_got, g_both = together(
        g_normed_pieces, g_down, out_got, g_both
    )

    g_normed_parts = exchange_ctx(g_normed_pieces)
    down_got = scatter_near(g_down)
    g_gate_up = weight_grad(normed_mine, normed_other, g_both)
    down_got, g_gate_up = together(down_got, g_gate_up)
    gate_up_payload = near_payload(g_gate_up)
    mlp_pieces = chip_sum(out_mine, out_got)
    down_sum = scatter_far(g_down, *down_got).astype(jnp.bfloat16)
    g_normed_parts, down_sum, gate_up_payload, mlp_pieces = together(
        g_normed_parts, down_sum, gate_up_payload, mlp_pieces
    )

    down_back = lax.all_to_all(
        down_sum.reshape(ctx_size, -1, down_sum.shape[1]), "ctx", 0, 0, tiled=True
    )
    gate_up_got = near_swap(gate_up_payload)
    grad_gain_mlp, branch_mine, g_hidden = call(
        functools.partial(norm_back_body, ctx_size),
        [row_f32, half_bf16, half_f32],
        [grad_half, hidden, rms_mlp, gain_two, *g_normed_parts],
        name="mlp_norm_back",
    )
    block = (span_rows, 2 * key_cols)
    query_lin, g_out, *g_blocks = call(
        functools.partial(attend_back_body, ctx_size),
        [
            ((span_rows, query_cols), jnp.bfloat16),
            ((model_width, query_cols), jnp.bfloat16),
            (block, jnp.float32),
        ]
        + [(block, jnp.bfloat16)] * (ctx_size - 1),
        [
            core_index,
            branch_mine,
            swap(branch_mine, "wt", 1),
            query,
            query_positions,
            key_positions,
            w_out,
            attn_heads,
            log_sums,
            cosines,
            signed_sines,
            *keys_values,
        ],
        [pltpu.VMEM((span_rows, model_width), jnp.bfloat16)],
        "attend_back",
        [scalar] + [whole] * (10 + ctx_size),
        span_rows * key_positions.size,
    )
    g_blocks, down_back = together(g_blocks, down_back)
    g_key_value_parts, gate_up_got, mlp_pieces = together(
        exchange_ctx(g_blocks), gate_up_got, mlp_pieces
    )

    mlp_parts = exchange_ctx(mlp_pieces)
    on_x, on_y = relay(g_gate_up, *gate_up_got)
    last_x, last_y, g_out = together(swap(on_x, "seq", 1), swap(on_y, "seq", 2), g_out)
    out_got = scatter_near(g_out)
    gate_up_sum = scatter_end(g_gate_up, *gate_up_got, last_x, last_y).astype(jnp.bfloat16)
    gate_up_blocks = gate_up_sum.reshape(ctx_size, -1, 2 * width)
    g_lin, g_bias, grad_gain_attn, normed_mine_grad, normed_send_grad = call(
        functools.partial(project_back_body, ctx_size),
        [
            ((span_rows, qkv_cols), jnp.bfloat16),
            ((1, qkv_cols), jnp.float32),
            row_f32,
            half_f32,
            half_f32,
        ],
        [
            core_index,
            query_lin,
            w_qkv,
            cosines,
            signed_sines,
            input_rows,
            rms_attn,
            *g_key_value_parts,
        ],
        [pltpu.VMEM((span_rows, model_width), jnp.float32)],
        "project_back",
        [scalar] + [whole] * (6 + ctx_size),
    )
    (g_qkv,) = call(
        product_body,
        [((model_width, qkv_cols), jnp.bfloat16)],
        [normed_attn, g_lin],
        name="qkv_grads",
    )
    small = jnp.concatenate(
        [
            relative(grad_gain_attn)[0],
            relative(grad_gain_mlp)[0],
            g_bias[0],
        ]
    ).astype(jnp.bfloat16)
    small_size = small.shape[0]
    small_rows = -(-small_size // (qkv_cols * 16)) * 16
    small = jnp.pad(small, (0, small_rows * qkv_cols - small_size)).reshape(small_rows, qkv_cols)

    payload_x, payload_y = near_payload(g_qkv)
    rows = payload_x.shape[0]
    half = rows // 2
    mlp_parts, gate_up_blocks, out_got, g_qkv, small, payload_y = together(
        mlp_parts, gate_up_blocks, out_got, g_qkv, small, payload_y
    )
    payload_x = jnp.concatenate([near_payload(g_qkv)[0], small], 0)

    gate_up_back = lax.all_to_all(gate_up_blocks, "ctx", 0, 0, tiled=True)
    got_x, got_y = near_swap((payload_x, payload_y))
    qkv_got = (got_x[:rows], got_y)
    small = add_up([small, got_x[rows:]]).astype(jnp.bfloat16)
    on_x, on_y = together(
        *(jnp.concatenate(pair, 1) for pair in zip(relay(g_qkv, *qkv_got), relay(g_out, *out_got)))
    )
    last_x = swap(on_x, "seq", 1)
    last_y = swap(with_rows(on_y, small), "seq", 2)
    small = add_up([small, last_y[half:, :qkv_cols]]).astype(jnp.bfloat16)
    attn_got = tuple(jnp.concatenate(pair, 1) for pair in zip(qkv_got, out_got))
    g_attn = jnp.concatenate([g_qkv, g_out], 1)
    attn_sum = scatter_end(g_attn, *attn_got, last_x, last_y[:half])
    attn_pieces = row_pieces(attn_sum)
    rows, attn_cols = attn_pieces[0].shape
    small_cols = -(-small_size // (rows * LANES)) * LANES
    small = jnp.pad(small.reshape(-1)[:small_size], (0, rows * small_cols - small_size))
    small = small.reshape(rows, small_cols)
    attn_send = [
        jnp.concatenate([piece.astype(jnp.bfloat16), small], 1) for piece in attn_pieces
    ]
    attn_send, gate_up_back, down_back, normed_send_grad, mlp_parts = together(
        attn_send, gate_up_back, down_back, normed_send_grad, mlp_parts
    )

    attn_back = exchange_ctx(attn_send)
    _, grad_input_half = call(
        functools.partial(norm_back_body, 2),
        [row_f32, half_bf16],
        [
            g_hidden,
            input_half,
            own_half(rms_attn),
            gain_one,
            normed_mine_grad,
            swap(normed_send_grad, "wt", 1),
        ],
        name="attn_norm_back",
    )
    grad_input_half = relative(grad_input_half)

    grad_input = join_halves(grad_input_half)
    layer_output = join_halves(relative((hidden + add_up(mlp_parts)).astype(jnp.bfloat16)))
    attn_back, grad_input, layer_output = together(attn_back, grad_input, layer_output)
    attn_back = attn_pieces[:1] + attn_back[1:]
    grad_w_gate, grad_w_up = (
        jnp.concatenate([block[:, start : start + width] for block in gate_up_back], 1)[
            :, :units_here
        ].astype(jnp.float32)
        for start in (0, width)
    )
    grad_w_down = jnp.concatenate(list(down_back), 1)[:, :units_here].astype(jnp.float32)
    grad_w_attn = add_up([part[:, :attn_cols] for part in attn_back])
    grad_w_qkv = grad_w_attn[:, :qkv_cols]
    grad_w_o = grad_w_attn[:, qkv_cols:]
    small = add_tree(
        [small.astype(jnp.float32)]
        + [part[:, attn_cols:].astype(jnp.float32) for part in attn_back[1:]]
    ).reshape(-1)
    gains = small[: 2 * model_width].reshape(-1, LANES)
    gains = (gains + swap(gains, "wt", 1)).reshape(-1)
    grad_bias = small[2 * model_width : small_size]
    return (
        layer_output[None],
        grad_input[None],
        gains[:model_width],
        grad_w_qkv[:, :query_cols],
        grad_bias[:query_cols],
        grad_w_qkv[:, query_cols : query_cols + key_cols],
        grad_bias[query_cols : query_cols + key_cols],
        grad_w_qkv[:, query_cols + key_cols :],
        grad_bias[query_cols + key_cols :],
        grad_w_o,
        gains[model_width:],
        grad_w_gate,
        grad_w_up,
        grad_w_down,
    )


def solution(mesh):
    tokens = P("seq", "ctx", None)
    weight = P(("seq", "ctx"), "wt")
    return jax.shard_map(
        on_device,
        mesh=mesh,
        in_specs=(
            tokens,
            P("seq", None),
            P(),
            weight,
            P("wt"),
            weight,
            P("wt"),
            weight,
            P("wt"),
            weight,
            P(),
            weight,
            weight,
            weight,
            tokens,
        ),
        out_specs=(
            tokens,
            tokens,
            P(),
            weight,
            P("wt"),
            weight,
            P("wt"),
            weight,
            P("wt"),
            weight,
            P(),
            weight,
            weight,
            weight,
        ),
        check_vma=False,
    )
```

```python
import functools
import math

import jax
import jax.numpy as jnp
from jax import lax
from jax.experimental import pallas as pl
from jax.experimental.pallas import tpu as pltpu
from jax.sharding import PartitionSpec as P

HD = 128
LANES = 128


EPSILON = 1e-06
THETA_BASE = 1000000.0
NEGATIVE = -1e30


def rope_tables(positions):
    freqs = THETA_BASE ** (-(jnp.arange(HD // 2, dtype=jnp.float32) * 2.0) / HD)
    angles = positions.astype(jnp.float32)[:, None] * freqs[None, :]
    cosines = jnp.cos(angles)
    sines = jnp.sin(angles)
    return (jnp.concatenate([cosines, cosines], -1), jnp.concatenate([sines, sines], -1))


def matmul(left, right):
    return jnp.dot(left, right, preferred_element_type=jnp.float32)


def times_transposed(left, right):
    return lax.dot_general(
        left, right, (((1,), (1,)), ((), ())), preferred_element_type=jnp.float32
    )


def inner_rows(left, right):
    return lax.dot_general(
        left, right, (((0,), (0,)), ((), ())), preferred_element_type=jnp.float32
    )


def swap(values, axis, offset):
    size = lax.axis_size(axis)
    return lax.ppermute(values, axis, [(i, i ^ offset) for i in range(size)])


def rows_at(values, index, count):
    return lax.dynamic_slice_in_dim(values, index * count, count, 0)


def place_rows(parts, indices):
    rows = len(parts) * parts[0].shape[0]
    whole = jnp.zeros((rows,) + parts[0].shape[1:], parts[0].dtype)
    for part, index in zip(parts, indices):
        whole = lax.dynamic_update_slice_in_dim(whole, part, index * part.shape[0], 0)
    return whole


def together(*values):
    return lax.optimization_barrier(values)


def relative(values):
    me = lax.axis_index("seq")
    width = values.shape[-1] // 4
    blocks = [
        lax.dynamic_slice_in_dim(values, (me ^ j) * width, width, values.ndim - 1)
        for j in range(4)
    ]
    return jnp.concatenate(blocks, -1)


def gather_ctx(block):
    size = lax.axis_size("ctx")
    return [block] + [swap(block, "ctx", k) for k in range(1, size)]


def exchange_ctx(pieces):
    return [pieces[0]] + [swap(pieces[k], "ctx", k) for k in range(1, len(pieces))]


def near_seq(shard):
    return swap(shard, "seq", 1), swap(shard, "seq", 2)


def far_seq(from_x, from_y):
    half = from_x.shape[0] // 2
    return swap(from_y[:half], "seq", 1), swap(from_x[half:], "seq", 2)


def near_payload(partial_sum):
    _, for_x, for_y, for_far = jnp.split(partial_sum, 4, 0)
    half = for_x.shape[0] // 2
    return (
        jnp.concatenate([for_far[half:], for_x[half:]], 0),
        jnp.concatenate([for_far[:half], for_y[:half]], 0),
    )


def near_swap(payload):
    return swap(payload[0], "seq", 1), swap(payload[1], "seq", 2)


def scatter_near(partial_sum):
    return near_swap(near_payload(partial_sum))


def relay(partial_sum, got_x, got_y):
    _, for_x, for_y, _ = jnp.split(partial_sum, 4, 0)
    half = for_x.shape[0] // 2
    on_x = add_up([for_x[:half], got_y[:half]]).astype(jnp.bfloat16)
    on_y = add_up([for_y[half:], got_x[:half]]).astype(jnp.bfloat16)
    return together(on_x, on_y)


def scatter_end(partial_sum, got_x, got_y, last_x, last_y):
    own = partial_sum[: partial_sum.shape[0] // 4]
    half = own.shape[0] // 2
    top = add_up([own[:half], got_y[half:], last_x])
    bottom = add_up([own[half:], got_x[half:], last_y])
    return jnp.concatenate([top, bottom], 0)


def scatter_far(partial_sum, got_x, got_y):
    on_x, on_y = relay(partial_sum, got_x, got_y)
    return scatter_end(
        partial_sum, got_x, got_y, swap(on_x, "seq", 1), swap(on_y, "seq", 2)
    )


def add_up(parts):
    total = parts[0].astype(jnp.float32)
    for part in parts[1:]:
        total = total + part.astype(jnp.float32)
    return total


def units_per(units):
    size = lax.axis_size("ctx")
    return -(-units // (size * LANES)) * LANES


def unit_pieces(shards):
    size = lax.axis_size("ctx")
    ctx = lax.axis_index("ctx")
    width = units_per(shards[0].shape[1])
    padded = [jnp.pad(w, ((0, 0), (0, size * width - w.shape[1]))) for w in shards]
    return [
        jnp.concatenate(
            [lax.dynamic_slice_in_dim(w, (ctx ^ k) * width, width, 1) for w in padded], 1
        )
        for k in range(size)
    ]


def row_pieces(summed):
    size = lax.axis_size("ctx")
    ctx = lax.axis_index("ctx")
    rows = summed.shape[0] // size
    return [rows_at(summed, ctx ^ k, rows) for k in range(size)]


def place_units(parts, units):
    size = lax.axis_size("ctx")
    ctx = lax.axis_index("ctx")
    width = units_per(units)
    wholes = []
    for start in range(0, parts[0].shape[1], width):
        whole = jnp.zeros((parts[0].shape[0], size * width), jnp.float32)
        for k in range(size):
            part = parts[k][:, start : start + width].astype(jnp.float32)
            whole = lax.dynamic_update_slice_in_dim(whole, part, (ctx ^ k) * width, 1)
        wholes.append(whole[:, :units])
    return wholes


def narrow_others(pieces):
    return [pieces[0]] + [piece.astype(jnp.bfloat16) for piece in pieces[1:]]


VMEM_BYTES = 56 * 1024 * 1024
ALONE = ("side_by_side", "mlp_norm_back", "attend_back", "project_back")
LITTLE = pl.CostEstimate(flops=1, bytes_accessed=1, transcendentals=0)


def stack_copies(targets, sems, used=0):
    copies = []
    for target, parts in targets:
        row, cols = 0, target.shape[1]
        group = []
        for part, column in parts:
            group.append(
                pltpu.make_async_copy(
                    part.at[:, pl.ds(column, cols)],
                    target.at[pl.ds(row, part.shape[0])],
                    sems.at[used + sum(map(len, copies)) + len(group)],
                )
            )
            row += part.shape[0]
        copies.append(group)
    return copies


def start_all(groups):
    for group in groups:
        for copy in group:
            copy.start()


def wait_all(groups):
    for group in groups:
        for copy in group:
            copy.wait()


def gate_up_copies(refs, gu, sems):
    up, gate_down, far = refs[:3], refs[3:6], refs[6:8]
    width = gu.shape[1] // 2
    return [
        (gu.at[:, pl.ds(0, width)], [(p, 0) for p in gate_down] + [(p, width) for p in far]),
        (gu.at[:, pl.ds(width, width)], [(p, 0) for p in up] + [(p, 0) for p in far]),
    ]


def forward_tile(tiles_each, x_mine, x_other, *refs):
    parts, (gate_up, gu, sems) = refs[:8], refs[8:]
    step = pl.program_id(0)

    @pl.when(step == 0)
    def _():
        copies = stack_copies(gate_up_copies(parts, gu, sems), sems)
        start_all(copies)
        wait_all(copies)

    rows = jnp.where(step < tiles_each, x_mine[...], x_other[...])
    gate_up[...] = matmul(rows, gu[...]).astype(gate_up.dtype)


def backward_tile(tiles_each, gate_up, o_mine, o_other, *refs):
    parts, refs = refs[:8], refs[8:]
    both_ref, act_ref, back_mine, back_send, out_mine, out_send, gu, down, sems = refs
    step = pl.program_id(0)
    own = step < tiles_each
    width = down.shape[1]

    down_target = [(down, [(p, width) for p in parts[3:6]] + [(p, 2 * width) for p in parts[6:]])]

    @pl.when(step == 0)
    def _():
        first = stack_copies(down_target, sems)
        start_all(first)
        wait_all(first)
        start_all(stack_copies(gate_up_copies(parts, gu, sems), sems, 5))

    grads = jnp.where(own, o_mine[...], o_other[...])
    g_act = matmul(grads, down[...])
    gate = gate_up[:, :width].astype(jnp.float32)
    up = gate_up[:, width:].astype(jnp.float32)
    sigmoid_gate = 1.0 / (1.0 + jnp.exp(-gate))
    silu_gate = gate * sigmoid_gate
    act_ref[...] = (silu_gate * up).astype(jnp.bfloat16)
    both_ref[:, :width] = (
        g_act * up * sigmoid_gate * (1.0 + gate * (1.0 - sigmoid_gate))
    ).astype(jnp.bfloat16)
    both_ref[:, width:] = (g_act * silu_gate).astype(jnp.bfloat16)

    @pl.when(step == 0)
    def _():
        wait_all(stack_copies(gate_up_copies(parts, gu, sems), sems, 5))

    back = times_transposed(both_ref[...], gu[...])
    out = times_transposed(act_ref[...], down[...])

    @pl.when(own)
    def _():
        back_mine[...] = back
        out_mine[...] = out

    @pl.when(jnp.logical_not(own))
    def _():
        back_send[...] = back.astype(jnp.bfloat16)
        out_send[...] = out.astype(jnp.bfloat16)


def by_tiles(body, count, ins, halves, parts, outs, half_outs, scratch, name, grant):
    tile = min(256, count)
    tiles_each = count // tile

    def rows(cols):
        return pl.BlockSpec((tile, cols), lambda i: (i, 0))

    def mine(cols):
        return pl.BlockSpec((tile, cols), lambda i: (jnp.minimum(i, tiles_each - 1), 0))

    def other(cols):
        return pl.BlockSpec((tile, cols), lambda i: (jnp.maximum(i - tiles_each, 0), 0))

    return pl.pallas_call(
        functools.partial(body, tiles_each),
        grid=(2 * tiles_each,),
        in_specs=[rows(x.shape[1]) for x in ins]
        + [spec(x.shape[1]) for pair in halves for spec, x in zip((mine, other), pair)]
        + [pl.BlockSpec(memory_space=pl.ANY)] * len(parts),
        out_specs=[rows(cols) for cols, _ in outs]
        + [spec(cols) for cols in half_outs for spec in (mine, other)],
        out_shape=[jax.ShapeDtypeStruct((2 * count, cols), dtype) for cols, dtype in outs]
        + [
            jax.ShapeDtypeStruct((count, cols), dtype)
            for cols in half_outs
            for dtype in (jnp.float32, jnp.bfloat16)
        ],
        scratch_shapes=[pltpu.VMEM(shape, jnp.bfloat16) for shape in scratch]
        + [pltpu.SemaphoreType.DMA((15,))],
        compiler_params=pltpu.CompilerParams(vmem_limit_bytes=grant * 1024 * 1024),
        cost_estimate=LITTLE,
        name=name,
    )(*ins, *(x for pair in halves for x in pair), *parts)


def weight_tile(x_mine, x_other, grads, out):
    count = x_mine.shape[0]
    out[...] = (
        inner_rows(x_mine[...], grads[:count]) + inner_rows(x_other[...], grads[count:])
    ).astype(jnp.bfloat16)


def weight_grad(x_mine, x_other, grads):
    count, model_width = x_mine.shape
    tile = model_width // 3
    columns = pl.BlockSpec((count, tile), lambda i: (0, i))
    return pl.pallas_call(
        weight_tile,
        grid=(3,),
        in_specs=[columns, columns, pl.BlockSpec(grads.shape, lambda i: (0, 0))],
        out_specs=pl.BlockSpec((tile, grads.shape[1]), lambda i: (i, 0)),
        out_shape=jax.ShapeDtypeStruct((model_width, grads.shape[1]), jnp.bfloat16),
        compiler_params=pltpu.CompilerParams(vmem_limit_bytes=28 * 1024 * 1024),
        cost_estimate=LITTLE,
        name="weight_grad",
    )(x_mine, x_other, grads)


def call(body, outs, args, scratch=(), name=None, in_specs=None, rows_keys=0):
    whole = pl.BlockSpec(memory_space=pltpu.VMEM)
    held = sum(x.size * x.dtype.itemsize for x in args)
    held += sum(math.prod(shape) * jnp.dtype(dtype).itemsize for shape, dtype in outs)
    grant = min(VMEM_BYTES, 2 * held + 48 * rows_keys + 8 * 1024 * 1024)
    if name in ALONE:
        grant = VMEM_BYTES
    return pl.pallas_call(
        body,
        in_specs=in_specs or [whole] * len(args),
        out_specs=[whole] * len(outs),
        out_shape=[jax.ShapeDtypeStruct(shape, dtype) for shape, dtype in outs],
        scratch_shapes=list(scratch),
        compiler_params=pltpu.CompilerParams(vmem_limit_bytes=grant),
        cost_estimate=LITTLE,
        name=name,
    )(*args)


def beside_body(*refs):
    *parts, out = refs
    start = 0
    for part in parts:
        out[:, start : start + part.shape[1]] = part[...]
        start += part.shape[1]


def side_by_side(parts):
    cols = sum(part.shape[1] for part in parts)
    return call(
        beside_body, [((parts[0].shape[0], cols), parts[0].dtype)], parts, name="side_by_side"
    )[0]


def place_body(plan, ctx_ref, *refs):
    count = max(part for part, *_ in plan) + 1
    parts, outs, sems = refs[:count], refs[count:-1], refs[-1]
    copies = []
    for part, k, column, cols, out, start in plan:
        rows = parts[part].shape[0]
        first = 0 if k is None else pl.multiple_of((ctx_ref[0] ^ k) * rows, rows)
        copies.append(
            pltpu.make_async_copy(
                parts[part].at[:, pl.ds(column, cols)],
                outs[out].at[pl.ds(first, rows), pl.ds(start, cols)],
                sems.at[len(copies)],
            )
        )
    for copy in copies:
        copy.start()
    for copy in copies:
        copy.wait()


def place_ctx(parts, spans, beside=None):
    ctx = lax.axis_index("ctx")
    count, rows = len(parts), parts[0].shape[0]
    if rows % 16:
        order = [ctx ^ k for k in range(count)]
        placed = [
            place_rows([part[:, column : column + cols] for part in parts], order)
            for column, cols in spans
        ]
        return placed if beside is None else [jnp.concatenate([beside, placed[0]], 1)]
    start = 0 if beside is None else beside.shape[1]
    plan = [
        (k, k, column, cols, out, start)
        for out, (column, cols) in enumerate(spans)
        for k in range(count)
    ]
    if beside is not None:
        plan.append((count, None, 0, start, 0, 0))
        parts = [*parts, beside]
    return call(
        functools.partial(place_body, plan),
        [((count * rows, start + cols), parts[0].dtype) for _, cols in spans],
        [ctx.astype(jnp.int32).reshape(1), *parts],
        [pltpu.SemaphoreType.DMA((len(plan),))],
        "place",
        [pl.BlockSpec(memory_space=pltpu.SMEM)]
        + [pl.BlockSpec(memory_space=pl.ANY)] * len(parts),
    )


def turn(values, cosines, signed_sines):
    return values * cosines + pltpu.roll(values, HD // 2, 1) * signed_sines


def turn_back(grads, cosines, signed_sines):
    return grads * cosines + pltpu.roll(grads, HD // 2, 1) * (-signed_sines)


def project_body(query_cols, key_cols, x, bias, cosines, signed_sines, *refs):
    shard, from_x, from_y, far_top, far_bottom = refs[:5]
    query, key_value, w_qkv, w_out, sems = refs[5:]
    near = shard.shape[0]
    half = near // 2
    split = w_qkv.shape[1]
    copies = []
    for part, start in (
        (shard, 0),
        (from_x, near),
        (from_y, 2 * near),
        (far_top, 3 * near),
        (far_bottom, 3 * near + half),
    ):
        rows = pl.ds(start, part.shape[0])
        left, right = part.at[:, pl.ds(0, split)], part.at[:, pl.ds(split, w_out.shape[1])]
        for source, target in ((left, w_qkv.at[rows]), (right, w_out.at[rows])):
            copies.append(pltpu.make_async_copy(source, target, sems.at[len(copies)]))
    for copy in copies:
        copy.start()
    for copy in copies[::2]:
        copy.wait()
    lin = matmul(x[...], w_qkv[...]) + bias[...]
    for start in range(0, query_cols, HD):
        query[:, start : start + HD] = turn(
            lin[:, start : start + HD], cosines[...], signed_sines[...]
        ).astype(jnp.bfloat16)
    for start in range(0, key_cols, HD):
        key_value[:, start : start + HD] = turn(
            lin[:, query_cols + start : query_cols + start + HD], cosines[...], signed_sines[...]
        ).astype(jnp.bfloat16)
    key_value[:, key_cols:] = lin[:, query_cols + key_cols :].astype(jnp.bfloat16)
    for copy in copies[1::2]:
        copy.wait()


def attend_body(count, core_ref, query, query_pos, key_pos, w_out, *refs):
    parts, (heads, log_sums, mine, send, total) = refs[:count], refs[count:]
    keys = jnp.concatenate([part[:, :HD] for part in parts], 0)
    values = jnp.concatenate([part[:, HD:] for part in parts], 0)
    visible = key_pos[...] <= query_pos[...]
    for start in range(0, query.shape[1], HD):
        scores = jnp.where(
            visible, times_transposed(query[:, start : start + HD], keys) * HD**-0.5, NEGATIVE
        )
        highest = jnp.max(scores, -1, keepdims=True)
        weights = jnp.exp(scores - highest)
        totals = jnp.sum(weights, -1, keepdims=True)
        heads[:, start : start + HD] = matmul(
            (weights * (1.0 / totals)).astype(jnp.bfloat16), values
        ).astype(jnp.bfloat16)
        log_sums[:, start : start + HD] = jnp.broadcast_to(
            highest + jnp.log(totals), (query.shape[0], HD)
        )
    split_rows(core_ref, times_transposed(heads[...], w_out[...]), total, mine, send)


def split_rows(core_ref, values, total, mine, send):
    half = mine.shape[0]
    core = core_ref[0]
    total[...] = values
    mine[...] = total[pl.ds(pl.multiple_of(core * half, half), half)]
    send[...] = total[pl.ds(pl.multiple_of((1 - core) * half, half), half)]


def norm_body(mine, got, inputs, gain, hidden, inverse_rms, normed):
    values = inputs[...] + mine[...] + got[...]
    hidden[...] = values
    inverse = lax.rsqrt(jnp.mean(values * values, -1, keepdims=True) + EPSILON)
    inverse_rms[...] = inverse
    normed[...] = (values * inverse * gain[...]).astype(jnp.bfloat16)


def norm_back_body(count, base, inputs, inverse_rms, gain, *refs):
    parts, outs = refs[:count], refs[count:]
    grads = parts[0][...].astype(jnp.float32)
    for part in parts[1:]:
        grads = grads + part[...].astype(jnp.float32)
    inverse = inverse_rms[...]
    values = inputs[...]
    weighted = grads * gain[...]
    back = inverse * weighted - values * (inverse * inverse * inverse) * jnp.mean(
        weighted * values, -1, keepdims=True
    )
    result = base[...].astype(jnp.float32) + back
    outs[0][...] = jnp.sum(grads * values * inverse, 0, keepdims=True)
    outs[1][...] = result.astype(jnp.bfloat16)
    if len(outs) > 2:
        outs[2][...] = result


def attend_back_body(
    count,
    core_ref,
    branch_mine,
    branch_other,
    query,
    query_pos,
    key_pos,
    w_out,
    heads,
    log_sums,
    cosines,
    signed_sines,
    *refs,
):
    parts, (query_lin, g_out), g_parts = refs[:count], refs[count : count + 2], refs[count + 2 : -1]
    branch = refs[-1]
    half = branch_mine.shape[0]
    core = core_ref[0]
    branch[pl.ds(pl.multiple_of(core * half, half), half)] = branch_mine[...]
    branch[pl.ds(pl.multiple_of((1 - core) * half, half), half)] = branch_other[...]
    keys = jnp.concatenate([part[:, :HD] for part in parts], 0)
    values = jnp.concatenate([part[:, HD:] for part in parts], 0)
    visible = key_pos[...] <= query_pos[...]
    g_heads = matmul(branch[...], w_out[...]).astype(jnp.bfloat16)
    scale = HD**-0.5
    g_keys = jnp.zeros(keys.shape, jnp.float32)
    g_values = jnp.zeros(values.shape, jnp.float32)
    for start in range(0, query.shape[1], HD):
        head = query[:, start : start + HD]
        g_head = g_heads[:, start : start + HD]
        scores = jnp.where(visible, times_transposed(head, keys) * scale, NEGATIVE)
        probs = jnp.exp(scores - log_sums[:, start : start + 1])
        g_probs = times_transposed(g_head, values)
        delta = jnp.sum(probs * g_probs, -1, keepdims=True)
        g_scores = (probs * (g_probs - delta)).astype(jnp.bfloat16)
        query_lin[:, start : start + HD] = turn_back(
            matmul(g_scores, keys) * scale, cosines[...], signed_sines[...]
        ).astype(jnp.bfloat16)
        g_keys = g_keys + inner_rows(g_scores, head)
        g_values = g_values + inner_rows(probs.astype(jnp.bfloat16), g_head)
    g_keys = g_keys * scale
    g_out[...] = inner_rows(branch[...], heads[...]).astype(jnp.bfloat16)
    rows = parts[0].shape[0]
    for k, out in enumerate(g_parts):
        out[:, :HD] = g_keys[k * rows : (k + 1) * rows].astype(out.dtype)
        out[:, HD:] = g_values[k * rows : (k + 1) * rows].astype(out.dtype)


def product_body(left, right, out):
    out[...] = inner_rows(left[...], right[...]).astype(jnp.bfloat16)


def project_back_body(
    count, core_ref, query_lin, w_qkv, cosines, signed_sines, inputs, inverse_rms, *refs
):
    parts, (lin, g_bias, g_gain, mine, send, total) = refs[:count], refs[count:]
    g_parts = parts[0][...].astype(jnp.float32)
    for part in parts[1:]:
        g_parts = g_parts + part[...].astype(jnp.float32)
    cols = query_lin.shape[1]
    lin[:, :cols] = query_lin[...]
    lin[:, cols : cols + HD] = turn_back(
        g_parts[:, :HD], cosines[...], signed_sines[...]
    ).astype(jnp.bfloat16)
    lin[:, cols + HD :] = g_parts[:, HD:].astype(jnp.bfloat16)
    split_rows(core_ref, times_transposed(lin[...], w_qkv[...]), total, mine, send)
    g_gain[...] = jnp.sum(total[...] * inputs[...] * inverse_rms[...], 0, keepdims=True)
    g_bias[...] = jnp.sum(lin[...].astype(jnp.float32), 0, keepdims=True)


def chip_sum(own, got):
    total = (own + got.astype(jnp.float32)).astype(jnp.bfloat16)
    return jnp.split(total, lax.axis_size("ctx"), 0)


def add_tree(parts):
    while len(parts) > 1:
        parts = [parts[i] + parts[i + 1] for i in range(0, len(parts), 2)]
    return parts[0]


def with_rows(block, rows):
    return jnp.concatenate([block, jnp.pad(rows, ((0, 0), (0, block.shape[1] - rows.shape[1])))], 0)


def on_device(
    layer_input,
    pairs,
    gain_attn,
    w_q,
    b_q,
    w_k,
    b_k,
    w_v,
    b_v,
    w_o,
    gain_mlp,
    w_gate,
    w_up,
    w_down,
    out_grad,
):
    _, span_rows, model_width = layer_input.shape
    half_rows = span_rows // 2
    query_cols = w_q.shape[1]
    key_cols = w_k.shape[1]
    units_here = w_gate.shape[1]
    ctx_size = lax.axis_size("ctx")
    ctx = lax.axis_index("ctx")
    core = lax.axis_index("wt")

    def own_half(values):
        return rows_at(values, core, half_rows)

    def join_halves(mine):
        other = swap(mine, "wt", 1)
        return jnp.where(
            core == 0, jnp.concatenate([mine, other], 0), jnp.concatenate([other, mine], 0)
        )

    within = jnp.arange(half_rows, dtype=jnp.int32)

    def positions_at(index):
        early = lax.dynamic_index_in_dim(pairs[0], index, 0, False)
        return jnp.concatenate(
            [early * half_rows + within, (2 * ctx_size - 1 - early) * half_rows + within]
        )

    query_positions = positions_at(ctx)
    key_positions = jnp.concatenate([positions_at(ctx ^ k) for k in range(ctx_size)])[None]
    cosines, sines = rope_tables(query_positions)
    signed_sines = jnp.concatenate([-sines[:, : HD // 2], sines[:, HD // 2 :]], 1)
    query_positions = query_positions[:, None]
    core_index = core.astype(jnp.int32).reshape(1)
    scalar = pl.BlockSpec(memory_space=pltpu.SMEM)
    whole = pl.BlockSpec(memory_space=pltpu.VMEM)
    left = pl.BlockSpec(memory_space=pl.ANY)

    input_rows = relative(layer_input.reshape(span_rows, model_width)).astype(jnp.float32)
    grad_out = relative(out_grad.reshape(span_rows, model_width))
    gain_one = relative(gain_attn.astype(jnp.float32))[None]
    gain_two = relative(gain_mlp.astype(jnp.float32))[None]

    rms_attn = lax.rsqrt(jnp.mean(input_rows * input_rows, -1, keepdims=True) + EPSILON)
    normed_attn = (input_rows * rms_attn * gain_one).astype(jnp.bfloat16)
    qkv_cols = query_cols + 2 * key_cols
    bias = jnp.concatenate([b_q, b_k, b_v]).astype(jnp.float32)[None]
    input_half = own_half(input_rows)
    attn_parts = gather_ctx(side_by_side([w_q, w_k, w_v, w_o]))
    gate_up_pieces = unit_pieces([w_gate, w_up])
    down_pieces = unit_pieces([w_down])
    grad_half = own_half(grad_out)
    (attn_shard,) = place_ctx(attn_parts, [(0, attn_parts[0].shape[1])])
    attn_shard, gate_up_pieces, down_pieces, tables = together(
        attn_shard,
        gate_up_pieces,
        down_pieces,
        (
            normed_attn,
            bias,
            cosines,
            signed_sines,
            query_positions,
            key_positions,
            input_half,
            grad_half,
            gain_two,
        ),
    )
    normed_attn, bias, cosines, signed_sines, query_positions, key_positions = tables[:6]
    input_half, grad_half, gain_two = tables[6:]

    attn_near = near_seq(attn_shard)
    gate_up_parts = exchange_ctx(gate_up_pieces)
    attn_near, gate_up_parts, down_pieces = together(attn_near, gate_up_parts, down_pieces)
    attn_far = far_seq(*attn_near)
    down_parts = exchange_ctx(down_pieces)
    width = units_per(units_here)
    up_shard, gate_shard = place_ctx(gate_up_parts, [(width, width), (0, width)])
    attn_far, up_shard = together(attn_far, up_shard)
    up_near = near_seq(up_shard)

    query, key_value, w_qkv, w_out = call(
        functools.partial(project_body, query_cols, key_cols),
        [
            ((span_rows, query_cols), jnp.bfloat16),
            ((span_rows, 2 * key_cols), jnp.bfloat16),
            ((model_width, qkv_cols), jnp.bfloat16),
            ((model_width, query_cols), jnp.bfloat16),
        ],
        [normed_attn, bias, cosines, signed_sines, attn_shard, *attn_near, *attn_far],
        [pltpu.SemaphoreType.DMA((10,))],
        "project",
        [whole] * 4 + [left] * 5,
    )
    key_value, down_parts = together(key_value, down_parts)

    (gate_down_shard,) = place_ctx(down_parts, [(0, width)], gate_shard)
    keys_values, gate_down_shard = together(gather_ctx(key_value), gate_down_shard)
    half_f32 = ((half_rows, model_width), jnp.float32)
    half_bf16 = ((half_rows, model_width), jnp.bfloat16)
    row_f32 = ((1, model_width), jnp.float32)
    attn_heads, log_sums, attn_mine, attn_send = call(
        functools.partial(attend_body, ctx_size),
        [
            ((span_rows, query_cols), jnp.bfloat16),
            ((span_rows, query_cols), jnp.float32),
            half_f32,
            half_f32,
        ],
        [core_index, query, query_positions, key_positions, w_out, *keys_values],
        [pltpu.VMEM((span_rows, model_width), jnp.float32)],
        "attend",
        [scalar] + [whole] * (4 + ctx_size),
        span_rows * key_positions.size,
    )
    hidden, rms_mlp, normed_half = call(
        norm_body,
        [half_f32, ((half_rows, 1), jnp.float32), half_bf16],
        [attn_mine, swap(attn_send, "wt", 1), input_half, gain_two],
        name="norm",
    )
    normed_half, gate_down_shard, up_near = together(normed_half, gate_down_shard, up_near)

    gate_down_near = near_seq(gate_down_shard)
    normed_parts, gate_down_near, grad_half = together(
        gather_ctx(normed_half), gate_down_near, grad_half
    )

    mlp_far = far_seq(*(jnp.concatenate(pair, 1) for pair in zip(up_near, gate_down_near)))
    normed_mine = jnp.concatenate(normed_parts, 0)
    normed_other, grad_half = together(swap(normed_mine, "wt", 1), grad_half)
    count = normed_mine.shape[0]
    mlp_parts = [up_shard, *up_near, gate_down_shard, *gate_down_near, *mlp_far]
    (gate_up,) = by_tiles(
        forward_tile,
        count,
        [],
        [(normed_mine, normed_other)],
        mlp_parts,
        [(2 * width, jnp.bfloat16)],
        [],
        [(model_width, 2 * width)],
        "gate_up",
        22,
    )
    grad_parts, gate_up = together(gather_ctx(grad_half), gate_up)
    grad_mine = jnp.concatenate(grad_parts, 0)
    grad_other = swap(grad_mine, "wt", 1)
    g_both, act, back_mine, back_send, out_mine, out_send = by_tiles(
        backward_tile,
        count,
        [gate_up],
        [(grad_mine, grad_other)],
        mlp_parts,
        [(2 * width, jnp.bfloat16), (width, jnp.bfloat16)],
        [model_width, model_width],
        [(model_width, 2 * width), (model_width, width)],
        "mlp_back",
        39,
    )
    back_got = swap(back_send, "wt", 1)
    out_got = swap(out_send, "wt", 1)
    g_down = weight_grad(grad_mine, grad_other, act)
    g_normed_pieces = chip_sum(back_mine, back_got)
    g_normed_pieces, g_down, out_got, g_both = together(
        g_normed_pieces, g_down, out_got, g_both
    )

    g_normed_parts = exchange_ctx(g_normed_pieces)
    down_got = scatter_near(g_down)
    g_gate_up = weight_grad(normed_mine, normed_other, g_both)
    down_got, g_gate_up = together(down_got, g_gate_up)
    gate_up_payload = near_payload(g_gate_up)
    mlp_pieces = chip_sum(out_mine, out_got)
    down_sum = scatter_far(g_down, *down_got).astype(jnp.bfloat16)
    g_normed_parts, down_sum, gate_up_payload, mlp_pieces = together(
        g_normed_parts, down_sum, gate_up_payload, mlp_pieces
    )

    down_back = lax.all_to_all(
        down_sum.reshape(ctx_size, -1, down_sum.shape[1]), "ctx", 0, 0, tiled=True
    )
    gate_up_got = near_swap(gate_up_payload)
    grad_gain_mlp, branch_mine, g_hidden = call(
        functools.partial(norm_back_body, ctx_size),
        [row_f32, half_bf16, half_f32],
        [grad_half, hidden, rms_mlp, gain_two, *g_normed_parts],
        name="mlp_norm_back",
    )
    block = (span_rows, 2 * key_cols)
    query_lin, g_out, *g_blocks = call(
        functools.partial(attend_back_body, ctx_size),
        [
            ((span_rows, query_cols), jnp.bfloat16),
            ((model_width, query_cols), jnp.bfloat16),
            (block, jnp.float32),
        ]
        + [(block, jnp.bfloat16)] * (ctx_size - 1),
        [
            core_index,
            branch_mine,
            swap(branch_mine, "wt", 1),
            query,
            query_positions,
            key_positions,
            w_out,
            attn_heads,
            log_sums,
            cosines,
            signed_sines,
            *keys_values,
        ],
        [pltpu.VMEM((span_rows, model_width), jnp.bfloat16)],
        "attend_back",
        [scalar] + [whole] * (10 + ctx_size),
        span_rows * key_positions.size,
    )
    g_blocks, down_back = together(g_blocks, down_back)
    g_key_value_parts, gate_up_got, mlp_pieces = together(
        exchange_ctx(g_blocks), gate_up_got, mlp_pieces
    )

    mlp_parts = exchange_ctx(mlp_pieces)
    on_x, on_y = relay(g_gate_up, *gate_up_got)
    last_x, last_y, g_out = together(swap(on_x, "seq", 1), swap(on_y, "seq", 2), g_out)
    out_got = scatter_near(g_out)
    gate_up_sum = scatter_end(g_gate_up, *gate_up_got, last_x, last_y).astype(jnp.bfloat16)
    gate_up_blocks = gate_up_sum.reshape(ctx_size, -1, 2 * width)
    g_lin, g_bias, grad_gain_attn, normed_mine_grad, normed_send_grad = call(
        functools.partial(project_back_body, ctx_size),
        [
            ((span_rows, qkv_cols), jnp.bfloat16),
            ((1, qkv_cols), jnp.float32),
            row_f32,
            half_f32,
            half_f32,
        ],
        [
            core_index,
            query_lin,
            w_qkv,
            cosines,
            signed_sines,
            input_rows,
            rms_attn,
            *g_key_value_parts,
        ],
        [pltpu.VMEM((span_rows, model_width), jnp.float32)],
        "project_back",
        [scalar] + [whole] * (6 + ctx_size),
    )
    (g_qkv,) = call(
        product_body,
        [((model_width, qkv_cols), jnp.bfloat16)],
        [normed_attn, g_lin],
        name="qkv_grads",
    )
    small = jnp.concatenate(
        [
            relative(grad_gain_attn)[0],
            relative(grad_gain_mlp)[0],
            g_bias[0],
        ]
    ).astype(jnp.bfloat16)
    small_size = small.shape[0]
    small_rows = -(-small_size // (qkv_cols * 16)) * 16
    small = jnp.pad(small, (0, small_rows * qkv_cols - small_size)).reshape(small_rows, qkv_cols)

    payload_x, payload_y = near_payload(g_qkv)
    rows = payload_x.shape[0]
    half = rows // 2
    mlp_parts, gate_up_blocks, out_got, g_qkv, small, payload_y = together(
        mlp_parts, gate_up_blocks, out_got, g_qkv, small, payload_y
    )
    payload_x = jnp.concatenate([near_payload(g_qkv)[0], small], 0)

    gate_up_back = lax.all_to_all(gate_up_blocks, "ctx", 0, 0, tiled=True)
    got_x, got_y = near_swap((payload_x, payload_y))
    qkv_got = (got_x[:rows], got_y)
    small = add_up([small, got_x[rows:]]).astype(jnp.bfloat16)
    on_x, on_y = together(
        *(jnp.concatenate(pair, 1) for pair in zip(relay(g_qkv, *qkv_got), relay(g_out, *out_got)))
    )
    last_x = swap(on_x, "seq", 1)
    last_y = swap(with_rows(on_y, small), "seq", 2)
    small = add_up([small, last_y[half:, :qkv_cols]]).astype(jnp.bfloat16)
    attn_got = tuple(jnp.concatenate(pair, 1) for pair in zip(qkv_got, out_got))
    g_attn = jnp.concatenate([g_qkv, g_out], 1)
    attn_sum = scatter_end(g_attn, *attn_got, last_x, last_y[:half])
    attn_pieces = row_pieces(attn_sum)
    rows, attn_cols = attn_pieces[0].shape
    small_cols = -(-small_size // (rows * LANES)) * LANES
    small = jnp.pad(small.reshape(-1)[:small_size], (0, rows * small_cols - small_size))
    small = small.reshape(rows, small_cols)
    attn_send = [
        jnp.concatenate([piece.astype(jnp.bfloat16), small], 1) for piece in attn_pieces
    ]
    attn_send, gate_up_back, down_back, normed_send_grad, mlp_parts = together(
        attn_send, gate_up_back, down_back, normed_send_grad, mlp_parts
    )

    attn_back = exchange_ctx(attn_send)
    _, grad_input_half = call(
        functools.partial(norm_back_body, 2),
        [row_f32, half_bf16],
        [
            g_hidden,
            input_half,
            own_half(rms_attn),
            gain_one,
            normed_mine_grad,
            swap(normed_send_grad, "wt", 1),
        ],
        name="attn_norm_back",
    )
    grad_input_half = relative(grad_input_half)

    grad_input = join_halves(grad_input_half)
    layer_output = join_halves(relative((hidden + add_up(mlp_parts)).astype(jnp.bfloat16)))
    attn_back, grad_input, layer_output = together(attn_back, grad_input, layer_output)
    attn_back = attn_pieces[:1] + attn_back[1:]
    grad_w_gate, grad_w_up = (
        jnp.concatenate([block[:, start : start + width] for block in gate_up_back], 1)[
            :, :units_here
        ].astype(jnp.float32)
        for start in (0, width)
    )
    grad_w_down = jnp.concatenate(list(down_back), 1)[:, :units_here].astype(jnp.float32)
    grad_w_attn = add_up([part[:, :attn_cols] for part in attn_back])
    grad_w_qkv = grad_w_attn[:, :qkv_cols]
    grad_w_o = grad_w_attn[:, qkv_cols:]
    small = add_tree(
        [small.astype(jnp.float32)]
        + [part[:, attn_cols:].astype(jnp.float32) for part in attn_back[1:]]
    ).reshape(-1)
    gains = small[: 2 * model_width].reshape(-1, LANES)
    gains = (gains + swap(gains, "wt", 1)).reshape(-1)
    grad_bias = small[2 * model_width : small_size]
    return (
        layer_output[None],
        grad_input[None],
        gains[:model_width],
        grad_w_qkv[:, :query_cols],
        grad_bias[:query_cols],
        grad_w_qkv[:, query_cols : query_cols + key_cols],
        grad_bias[query_cols : query_cols + key_cols],
        grad_w_qkv[:, query_cols + key_cols :],
        grad_bias[query_cols + key_cols :],
        grad_w_o,
        gains[model_width:],
        grad_w_gate,
        grad_w_up,
        grad_w_down,
    )


def solution(mesh):
    tokens = P("seq", "ctx", None)
    weight = P(("seq", "ctx"), "wt")
    return jax.shard_map(
        on_device,
        mesh=mesh,
        in_specs=(
            tokens,
            P("seq", None),
            P(),
            weight,
            P("wt"),
            weight,
            P("wt"),
            weight,
            P("wt"),
            weight,
            P(),
            weight,
            weight,
            weight,
            tokens,
        ),
        out_specs=(
            tokens,
            tokens,
            P(),
            weight,
            P("wt"),
            weight,
            P("wt"),
            weight,
            P("wt"),
            weight,
            P(),
            weight,
            weight,
            weight,
        ),
        check_vma=False,
    )
```
